32 devices in a mesh: seq: 16 (over z, x, core), head: 2 (over y).
Axes of the slice: x: 2, y: 2, z: 4, core: 2. Of those that a mesh axis runs over, the one named last changes fastest.
Arguments:
- rows: bfloat16 [16384, 768], P('seq'), may hold values from -6 to 6
- lengths: int32 [1], replicated, may hold values from 8192 to 16384, as said below
- norm_gains: float32 [2, 768], replicated, may hold values from 0.5 to 1.5
- norm_shifts: float32 [2, 768], replicated, may hold values from -2 to 2
- qkv_weight: bfloat16 [3, 768, 768], P(None, None, 'head'), may hold values from -0.21875 to 0.21875
- qv_bias: float32 [2, 768], P(None, 'head'), may hold values from -3 to 3
- out_weight: bfloat16 [768, 768], P('head'), may hold values from -2.5 to 2.5
- out_bias: float32 [768], replicated, may hold values from -2 to 2
- up_weight: bfloat16 [768, 3072], P(None, 'head'), may hold values from -0.21875 to 0.21875
- up_bias: float32 [3072], P('head'), may hold values from -3 to 3
- down_weight: bfloat16 [3072, 768], P('head'), may hold values from -0.109375 to 0.109375
- down_bias: float32 [768], replicated, may hold values from -2 to 2
- out_cot: bfloat16 [16384, 768], P('seq'), may hold values from -6 to 6
Outputs:
- out_rows: bfloat16 [16384, 768], P('seq')
- rows_grad: float32 [16384, 768], P('seq')
- norm_gains_grad: float32 [2, 768], replicated
- norm_shifts_grad: float32 [2, 768], replicated
- qkv_grad: float32 [3, 768, 768], P(None, None, 'head')
- qv_bias_grad: float32 [2, 768], P(None, 'head')
- out_weight_grad: float32 [768, 768], P('head')
- out_bias_grad: float32 [768], replicated
- up_weight_grad: float32 [768, 3072], P(None, 'head')
- up_bias_grad: float32 [3072], P('head')
- down_weight_grad: float32 [3072, 768], P('head')
- down_bias_grad: float32 [768], replicated
The draws below stay inside these ranges and needn't reach their ends.
Inputs may be any that keep to these rules, and one draw needn't show every extreme that they name: Slide k uses the first lengths[k] rows of its block of 16384 rows; at least one slide uses all of its block.
All inputs are finite; a program needn't handle non-finite values.
Results may differ from the reference program's by a relative error of at most 0.015.
Values may be sent and summed in bfloat16 or wider, within the bound.
No kernel may reach another device: no remote copies, remote signals or barrier semaphores. Data moves between devices by JAX's collectives and lax.ppermute only.
A program may use at most 256 MiB of HBM per device.

```python
import math
import jax
import jax.numpy as jnp
from jax import lax

D = 768
HEADS = 16
HD = 48
FF = 3072
SEG = 1024
TOKENS = 16384
SLIDE = 16384
SLIDES = 1


def draw_lengths(key, part):
    key = jax.random.fold_in(key, 11)
    first_key, second_key = jax.random.split(key)
    drawn = jax.random.randint(first_key, (SLIDES,), SLIDE // 2, SLIDE + 1)
    full_slide = jax.random.randint(second_key, (), 0, SLIDES)
    return jnp.where(jnp.arange(SLIDES) == full_slide, SLIDE, drawn).astype(jnp.int32)


def block_scale(stream_key, extent, shards, low, high):
    def one(dim, blocks):
        draws = jax.random.uniform(jax.random.fold_in(jax.random.fold_in(stream_key, 6), dim), (blocks,), jnp.float32, low / len(shards), high / len(shards))
        return jnp.repeat(jnp.exp(draws), extent[dim] // blocks).reshape((-1,) + (1,) * (len(extent) - dim - 1))

    factor_of = one(*shards[0])
    for cut in shards[1:]:
        factor_of = factor_of * one(*cut)
    return factor_of


def bell_draw(rng, dims, scale, bound, cuts=(), held_as=jnp.bfloat16):
    values = scale * jax.random.normal(rng, dims, jnp.float32)
    if cuts:
        values = values * block_scale(rng, dims, cuts, -0.22, 0.18)
    return jnp.clip(values, -bound, bound).astype(held_as)


def setup_inputs(seed: int = 0) -> dict:
    key_of = jax.random.split(jax.random.key(seed), 14)
    rows = bell_draw(key_of[0], (TOKENS, D), 1.0, 6.0, ((0, 16),))
    lengths = draw_lengths(jax.random.fold_in(key_of[13], 71), 0)
    norm_gains = jnp.clip(1.0 + 0.1 * jax.random.normal(key_of[2], (2, D), jnp.float32), 0.5, 1.5)
    norm_shifts = bell_draw(key_of[3], (2, D), 0.3, 2.0, (), jnp.float32)
    qkv_weight = bell_draw(key_of[4], (3, D, D), D ** -0.5, 0.21875, ((2, 2),))
    qv_bias = bell_draw(key_of[5], (2, D), 0.5, 3.0, ((1, 2),), jnp.float32)
    out_weight = bell_draw(key_of[6], (D, D), (max(D // 128, 1)) ** -0.5, 2.5, ((0, 2),))
    out_bias = bell_draw(key_of[7], (D,), 0.3, 2.0, (), jnp.float32)
    up_weight = bell_draw(key_of[8], (D, FF), D ** -0.5, 0.21875, ((1, 2),))
    up_bias = bell_draw(key_of[9], (FF,), 0.5, 3.0, ((0, 2),), jnp.float32)
    down_weight = bell_draw(key_of[10], (FF, D), FF ** -0.5, 0.109375, ((0, 2),))
    down_bias = bell_draw(key_of[11], (D,), 0.3, 2.0, (), jnp.float32)
    out_cot = bell_draw(key_of[12], (TOKENS, D), 1.0, 6.0, ((0, 16),))
    return {"rows": rows, "lengths": lengths, "norm_gains": norm_gains, "norm_shifts": norm_shifts, "qkv_weight": qkv_weight, "qv_bias": qv_bias, "out_weight": out_weight, "out_bias": out_bias, "up_weight": up_weight, "up_bias": up_bias, "down_weight": down_weight, "down_bias": down_bias, "out_cot": out_cot}


@jax.custom_vjp
def low(v):
    return lax.optimization_barrier(v.astype(jnp.bfloat16)).astype(jnp.float32)

@jax.custom_vjp
def low_back(v):
    return v

def low_keep(v):
    return (low(v), None)

def low_pass(kept, grad):
    return (grad,)

def back_keep(v):
    return (v, None)

def back_low(kept, grad):
    return (low(grad),)
low.defvjp(low_keep, low_pass)
low_back.defvjp(back_keep, back_low)
eps = 1e-05
neg_big = -1e+30
levels = 5

def norm_rows(value_rows, gain, shift):
    row_mean = lax.optimization_barrier(jnp.mean(value_rows, -1, keepdims=True))
    centred = value_rows - row_mean
    return centred * lax.rsqrt(lax.optimization_barrier(jnp.mean(centred * centred, -1, keepdims=True)) + eps) * gain + shift

def product(left, right):
    return jnp.dot(left, right, precision=lax.Precision.HIGHEST)

def attend_head(pieces):
    query_rows, key_matrix, value_rows, present = pieces
    score_scale = 1.0 / math.sqrt(query_rows.shape[-1])
    raw_scores = jnp.einsum('aqd,akd->aqk', query_rows, key_matrix, precision=lax.Precision.HIGHEST)
    scores = low_back(raw_scores * score_scale)
    allowed = jnp.maximum(present[:, None, :], 1.0 - present[:, :, None]) > 0.5
    masked = jnp.where(allowed, scores, neg_big)
    row_top = lax.optimization_barrier(jnp.max(masked, -1, keepdims=True))
    weight_matrix = jnp.exp(masked - row_top)
    row_total = lax.optimization_barrier(jnp.sum(weight_matrix, -1, keepdims=True))
    summed = jnp.einsum('aqk,akd->aqd', low(weight_matrix), value_rows, precision=lax.Precision.HIGHEST)
    return (summed / row_total, (row_top + jnp.log(row_total))[..., 0])

def select_heads(value_rows, picker, spacing, seg_span):
    shaped = value_rows.reshape((value_rows.shape[0] // seg_span, seg_span // spacing, spacing) + value_rows.shape[1:])
    select_mask = picker.reshape((1, 1) + picker.shape + (1,) * (value_rows.ndim - 2))
    chosen = lax.optimization_barrier(jnp.sum(shaped * select_mask, axis=2))
    return jnp.moveaxis(chosen, 2, 0)

def place_heads(chosen, picker, filler):
    moved_rows = jnp.moveaxis(chosen, 0, 2)[:, :, None]
    select_mask = picker.reshape((1, 1) + picker.shape + (1,) * (moved_rows.ndim - 4))
    spread = jnp.where(select_mask > 0.5, moved_rows, filler)
    return spread.reshape((-1,) + spread.shape[3:])

def slide_forward(params, block_rows, length):
    norm_gains, norm_shifts, qkv_weight, qv_bias, out_weight, out_bias, up_weight, up_bias, down_weight, down_bias = params
    row_count = block_rows.shape[0]
    present = (jnp.arange(row_count) < length).astype(jnp.float32)
    normed1 = low(norm_rows(block_rows, norm_gains[0], norm_shifts[0]))
    query_rows = low(low_back(product(normed1, qkv_weight[0])) + qv_bias[0]).reshape(row_count, HEADS, HD)
    key_matrix = low(low_back(product(normed1, qkv_weight[1]))).reshape(row_count, HEADS, HD)
    value_rows = low(low_back(product(normed1, qkv_weight[2])) + qv_bias[1]).reshape(row_count, HEADS, HD)
    present_heads = jnp.broadcast_to(present[:, None], (row_count, HEADS))
    out_parts = []
    lse_parts = []
    for level_index in range(levels):
        spacing = 2 ** level_index
        seg_span = min(SEG * spacing, row_count)
        picker = (jnp.arange(spacing)[:, None] == jnp.arange(HEADS)[None, :] % spacing).astype(jnp.float32)
        pieces = tuple((select_heads(item_piece, picker, spacing, seg_span) for item_piece in (query_rows, key_matrix, value_rows, present_heads)))
        chosen_out, chosen_lse = lax.map(jax.checkpoint(attend_head), pieces)
        out_parts.append(place_heads(chosen_out, picker, 0.0))
        lse_parts.append(place_heads(chosen_lse, picker, neg_big))
    stacked = jnp.stack(lse_parts)
    row_top = lax.optimization_barrier(jnp.max(stacked, 0))
    shares = jnp.exp(stacked - row_top)
    merged = lax.optimization_barrier(jnp.sum(shares[..., None] * jnp.stack(out_parts), 0)) / lax.optimization_barrier(jnp.sum(shares, 0))[..., None]
    mixed = low(low_back(merged.reshape(row_count, HEADS * HD)))
    hidden = block_rows + low_back(product(mixed, out_weight)) + out_bias
    normed2 = low(norm_rows(hidden, norm_gains[1], norm_shifts[1]))
    pre_act = low_back(product(normed2, up_weight)) + up_bias
    activated = low(jax.nn.gelu(pre_act, approximate=False))
    return hidden + product(activated, down_weight) + down_bias

def reference(rows, lengths, norm_gains, norm_shifts, qkv_weight, qv_bias, out_weight, out_bias, up_weight, up_bias, down_weight, down_bias, out_cot):
    params = (norm_gains, norm_shifts, qkv_weight.astype(jnp.float32), qv_bias, out_weight.astype(jnp.float32), out_bias, up_weight.astype(jnp.float32), up_bias, down_weight.astype(jnp.float32), down_bias)
    slide_count = lengths.shape[0]

    def forward(inputs, weight_matrix):
        blocks = inputs.reshape(slide_count, SLIDE, D)

        def scan_step(carry_value, item_pair):
            return (carry_value, jax.checkpoint(slide_forward)(weight_matrix, item_pair[0], item_pair[1]))
        final_carry, results = lax.scan(scan_step, jnp.zeros((), jnp.float32), (blocks, lengths))
        return results.reshape(slide_count * SLIDE, D)
    result, pullback = jax.vjp(forward, rows.astype(jnp.float32), params)
    rows_grad, weight_grads = pullback(out_cot.astype(jnp.float32))
    return (result.astype(jnp.bfloat16), rows_grad, weight_grads[0], weight_grads[1], weight_grads[2], weight_grads[3], weight_grads[4], weight_grads[5], weight_grads[6], weight_grads[7], weight_grads[8], weight_grads[9])
```

```python
import functools
import math

import jax
import jax.numpy as jnp
import numpy as np
from jax import lax
from jax.experimental import pallas as pl
from jax.experimental.pallas import tpu as pltpu
from jax.sharding import PartitionSpec as P

HD = 48
SEG = 1024
LANES = 128
LEVELS = 5
FOLD = 16

EPS = 1e-05
ROOT = math.sqrt(HD)
EXP_SCALE = math.log2(math.e) / ROOT
ROOT_HALF = 1.0 / math.sqrt(2.0)
DENSITY_NORM = 1.0 / math.sqrt(2.0 * math.pi)
ABSENT = -1e20

ONE = 96
MASK = 99
MULT = 100
TOP = 127

ORDER = (0, 8, 4, 12, 2, 6, 10, 14, 1, 3, 5, 7, 9, 11, 13, 15)
CLASS = (4, 3, 2, 2, 1, 1, 1, 1, 0, 0, 0, 0, 0, 0, 0, 0)

F32 = jnp.float32
BF16 = jnp.bfloat16


def params(mib=48):
    return pltpu.CompilerParams(vmem_limit_bytes=mib * 2**20)


def dot(left, right):
    return jnp.dot(left, right, preferred_element_type=F32)


def dot_rt(left, right):
    return lax.dot_general(left, right, (((1,), (1,)), ((), ())), preferred_element_type=F32)


def dot_lt(left, right):
    return lax.dot_general(left, right, (((0,), (0,)), ((), ())), preferred_element_type=F32)


def full(shape):
    return pl.BlockSpec(shape, lambda *_: (0,) * len(shape))


def per_head(rows, lanes=LANES):
    return pl.BlockSpec((1, rows, lanes), lambda h: (h, 0, 0))


def shape(dims, kind):
    return jax.ShapeDtypeStruct(dims, kind)


def split3(x):
    high = x.astype(BF16).astype(F32)
    rest = x - high
    middle = rest.astype(BF16).astype(F32)
    return high, middle, rest - middle


def with_terms(block, lane, terms):
    high, middle, low = split3(terms)
    block = jnp.where(lane == ONE, high, block)
    block = jnp.where(lane == ONE + 1, middle, block)
    return jnp.where(lane == ONE + 2, low, block)


def unit_rows(x):
    mean = jnp.mean(x, -1, keepdims=True)
    centred = x - mean
    inverse = lax.rsqrt(jnp.mean(centred * centred, -1, keepdims=True) + EPS)
    return centred * inverse, inverse


def norm_back(gradient, unit, inverse, gain):
    z = gradient * gain
    return inverse * (
        z - jnp.mean(z, -1, keepdims=True) - unit * jnp.mean(z * unit, -1, keepdims=True)
    )


def mult_table(level, blocks):
    table = np.zeros((len(blocks), LANES), np.float32)
    for row, key_class in enumerate(blocks):
        for j in range(level + 1, key_class + 1):
            value = np.float32(ROOT * math.log((j - level + 1) / (j - level)))
            high = np.float32(value.astype(jnp.bfloat16))
            table[row, MULT + j - 1] = high
            table[row, MULT + 4 + j - 1] = np.float32((value - high).astype(jnp.bfloat16))
    return table


def own_table():
    return mult_table(0, CLASS)


def peer_table():
    return np.concatenate(
        [
            mult_table(1, CLASS[:8]),
            mult_table(2, CLASS[:4] * 2),
            mult_table(3, CLASS[:2] * 4),
            mult_table(4, CLASS[:1] * 8),
        ]
    )


def project_kernel(
    place, rows, gain, shift, w, bias, table, q, kv, s1, sx, sz1, sz, normed, wide, w_tmp, b_tmp, q_tmp, kv_tmp
):
    h = pl.program_id(0)
    n, d = rows.shape
    heads = w.shape[2] // HD
    block = n // FOLD

    @pl.when(h == 0)
    def _():
        unit, _ = unit_rows(rows[...].astype(F32))
        normed[...] = (unit * gain[...] + shift[...]).astype(BF16)

    for k in range(heads):

        @pl.when(h == k)
        def _():
            cut = slice(k * HD, (k + 1) * HD)
            w_tmp[:, :LANES] = jnp.concatenate(
                [w[0, :, cut], jnp.zeros((d, LANES - HD), BF16)], axis=1
            )
            w_tmp[:, LANES:] = jnp.concatenate(
                [w[1, :, cut], w[2, :, cut], jnp.zeros((d, LANES - 2 * HD), BF16)], axis=1
            )
            b_tmp[:, :LANES] = jnp.concatenate(
                [bias[0:1, cut], jnp.zeros((1, LANES - HD), F32)], axis=1
            )
            b_tmp[:, LANES:] = jnp.concatenate(
                [
                    jnp.zeros((1, HD), F32),
                    bias[1:2, cut],
                    jnp.ones((1, 3), F32),
                    jnp.zeros((1, LANES - 2 * HD - 3), F32),
                ],
                axis=1,
            )

    wide[0] = w_tmp[...]
    product = dot(normed[...], w_tmp[...]) + b_tmp[...]
    q_tmp[...] = product[:, :LANES]
    kv_tmp[...] = product[:, LANES:]
    lane = lax.broadcasted_iota(jnp.int32, (block, LANES), 1)
    step = lax.broadcasted_iota(jnp.int32, (block, LANES), 0) * FOLD
    head = place[0] + h
    for p in range(FOLD):
        c = (head + ORDER[p]) % FOLD
        here = step + c < place[1]
        at = pl.ds(p * block, block)
        q_rows = q_tmp[pl.ds(c, block, stride=FOLD), :]
        kv_rows = kv_tmp[pl.ds(c, block, stride=FOLD), :]
        level = CLASS[p]
        flags = ((lane >= MULT) & (lane < MULT + level)) | (
            (lane >= MULT + 4) & (lane < MULT + 4 + level)
        )
        q_rows = jnp.where(flags, 1.0, q_rows)
        q_rows = jnp.where(lane == MASK, jnp.where(here, 1.0, 0.0), q_rows)
        q[0, at, :] = q_rows.astype(BF16)
        kv_rows = jnp.where(lane == MASK, jnp.where(here, 0.0, ABSENT), kv_rows)
        kv[0, at, :] = (kv_rows + table[p : p + 1, :]).astype(BF16)
        if level >= 1:
            low = kv_rows.astype(BF16)
            s1[0, at, :] = low
            if level >= 2:
                sx[0, at, :] = low
            if level >= 3:
                sz1[0, at, :] = low
            if level >= 4:
                sz[0, at, :] = low


def project(place, rows, gain, shift, w, bias):
    n, d = rows.shape
    heads = w.shape[2] // HD
    table = jnp.asarray(own_table())
    sizes = (n, n, n // 2, n // 4, n // 8, n // 16)
    return pl.pallas_call(
        project_kernel,
        grid=(heads,),
        in_specs=[
            pl.BlockSpec(memory_space=pltpu.SMEM),
            full(rows.shape),
            full(gain.shape),
            full(shift.shape),
            full(w.shape),
            full(bias.shape),
            full(table.shape),
        ],
        out_specs=[per_head(m) for m in sizes]
        + [full((n, d)), pl.BlockSpec((1, d, 2 * LANES), lambda h: (h, 0, 0))],
        out_shape=[shape((heads, m, LANES), BF16) for m in sizes]
        + [shape((n, d), BF16), shape((heads, d, 2 * LANES), BF16)],
        scratch_shapes=[
            pltpu.VMEM((d, 2 * LANES), BF16),
            pltpu.VMEM((1, 2 * LANES), F32),
            pltpu.VMEM((n, LANES), F32),
            pltpu.VMEM((n, LANES), F32),
        ],
        compiler_params=params(),
        cost_estimate=pl.CostEstimate(
            flops=2 * n * d * heads * 256, bytes_accessed=14 * 2**20, transcendentals=0
        ),
        name="project",
    )(place, rows, gain, shift, w, bias, table)


def own_kernel(q, kv, out, *, block):
    n = q.shape[1]
    keys = kv[0]
    lane = lax.broadcasted_iota(jnp.int32, (block, LANES), 1)

    def scores(i):
        return dot_rt(q[0, pl.ds(i * block, block), :], keys)

    now = scores(0)
    for i in range(n // block):
        later = scores(i + 1) if (i + 1) * block < n else None
        top = jnp.max(now, -1, keepdims=True)
        weights = jnp.exp2((now - top) * EXP_SCALE).astype(BF16)
        out[0, pl.ds(i * block, block), :] = jnp.where(lane == TOP, top, dot(weights, keys))
        now = later


def own_attention(q, kv):
    heads, n, _ = q.shape
    return pl.pallas_call(
        functools.partial(own_kernel, block=256),
        grid=(heads,),
        in_specs=[per_head(n)] * 2,
        out_specs=per_head(n),
        out_shape=shape((heads, n, LANES), F32),
        compiler_params=params(),
        cost_estimate=pl.CostEstimate(
            flops=heads * n * n * 1024, bytes_accessed=8 * 2**20, transcendentals=heads * n * n
        ),
        name="own_attention",
    )(q, kv)


def peers_kernel(
    place, q, own, cs1, rx, crx, zc, rx2, czc, crx2, table, pick, merged, kv_all, qb, low, nat, wide
):
    h = pl.program_id(0)
    n = q.shape[1]
    block = n // FOLD
    at = 0
    near = (zc, rx2, czc, crx2)
    pieces = [(cs1, 0, n // 2), (rx, 0, n // 4), (crx, 0, n // 4)]
    pieces += [(r, 0, n // 8) for r in near] + [(r, n // 8, n // 8) for r in near]
    for ref, start, count in pieces:
        for k in range(count // block):
            rows = ref[0, pl.ds(start + k * block, block), :].astype(F32)
            index = at // block
            kv_all[0, pl.ds(at, block), :] = (rows + table[index : index + 1, :]).astype(BF16)
            at += block

    head = place[0] + h
    chunks = [
        (0, n // 16, 2 * n),
        (n // 16, n // 16, 3 * n // 2),
        (n // 8, n // 8, n),
        (n // 4, n // 4, n // 2),
        (n // 2, n // 2, 0),
    ]
    scores = []
    for start, count, keys in chunks:
        if keys:
            scores.append(dot_rt(q[0, pl.ds(start, count), :], kv_all[0, pl.ds(0, keys), :]))
        else:
            scores.append(None)
    for (start, count, keys), s in zip(chunks, scores):
        rows = pl.ds(start, count)
        lane = lax.broadcasted_iota(jnp.int32, (count, LANES), 1)
        o = own[0, rows, :]
        top = o[:, TOP : TOP + 1]
        if keys:
            new = jnp.maximum(top, jnp.max(s, -1, keepdims=True))
            weights = jnp.exp2((s - new) * EXP_SCALE).astype(BF16)
            o = o * jnp.exp2((top - new) * EXP_SCALE) + dot(weights, kv_all[0, pl.ds(0, keys), :])
            top = new
        total = o[:, ONE : ONE + 1]
        o = jnp.where((lane >= HD) & (lane < 2 * HD), o / total, 0.0)
        merged[0, rows, :] = o
        lse = top + jnp.log2(total) * (1.0 / EXP_SCALE)
        qb[0, rows, :] = with_terms(q[0, rows, :].astype(F32), lane, -lse).astype(BF16)
        for p in range(start // block, (start + count) // block):
            c = (head + ORDER[p]) % FOLD
            off = p * block - start
            nat[pl.ds(c, block, stride=FOLD), :] = o[off : off + block]
    wide[:, pl.ds(pl.multiple_of(h * LANES, LANES), LANES)] = nat[...].astype(BF16)

    @pl.when(h == pl.num_programs(0) - 1)
    def _():
        low[...] = dot(wide[...], pick[...]).astype(BF16)


def pick_values(heads):
    m = np.zeros((heads * LANES, heads * HD), np.float32)
    for h in range(heads):
        for j in range(HD):
            m[h * LANES + HD + j, h * HD + j] = 1.0
    return m


def peers_attention(place, q, own, received):
    heads, n, _ = q.shape
    table = jnp.asarray(peer_table())
    pick = jnp.asarray(pick_values(heads), BF16)
    return pl.pallas_call(
        peers_kernel,
        grid=(heads,),
        in_specs=[pl.BlockSpec(memory_space=pltpu.SMEM), per_head(n), per_head(n)]
        + [per_head(r.shape[1]) for r in received]
        + [full(table.shape), full(pick.shape)],
        out_specs=[per_head(n), per_head(2 * n), per_head(n), full((n, heads * HD))],
        out_shape=[
            shape((heads, n, LANES), F32),
            shape((heads, 2 * n, LANES), BF16),
            shape((heads, n, LANES), BF16),
            shape((n, heads * HD), BF16),
        ],
        scratch_shapes=[pltpu.VMEM((n, LANES), F32), pltpu.VMEM((n, heads * LANES), BF16)],
        compiler_params=params(),
        cost_estimate=pl.CostEstimate(
            flops=heads * n * n * 512, bytes_accessed=24 * 2**20, transcendentals=heads * n * n // 2
        ),
        name="peers_attention",
    )(place, q, own, *received, table, pick)


def feed_kernel(
    place, rows, cot, own_c, peer_c, own_w, peer_w, out_b, gain, shift, up_w, up_b, down_w,
    hidden, normed, act, grad_pre, grad_normed, up_b_grad, w_tmp,
):
    i = pl.program_id(0)
    half = own_w.shape[0]
    first = place[2] == 0

    @pl.when(i == 0)
    def _():
        w_tmp[:half] = jnp.where(first, own_w[...], peer_w[...])
        w_tmp[half:] = jnp.where(first, peer_w[...], own_w[...])

    one = jnp.where(first, own_c[...], peer_c[...])
    two = jnp.where(first, peer_c[...], own_c[...])
    attended = dot(one, w_tmp[:half]) + dot(two, w_tmp[half:])
    hid = rows[...].astype(F32) + (attended + out_b[...])
    hidden[...] = hid
    unit, _ = unit_rows(hid)
    low = (unit * gain[...] + shift[...]).astype(BF16)
    normed[...] = low
    pre = dot(low, up_w[...]) + up_b[...]
    phi = 0.5 * (1.0 + lax.erf(pre * ROOT_HALF))
    act[...] = (pre * phi).astype(BF16)
    slope = phi + pre * jnp.exp(-0.5 * pre * pre) * DENSITY_NORM
    gradient = dot_rt(cot[...], down_w[...]) * slope
    total = jnp.sum(gradient, 0, keepdims=True)

    @pl.when(i == 0)
    def _():
        up_b_grad[...] = total

    @pl.when(i > 0)
    def _():
        up_b_grad[...] += total

    gradient = gradient.astype(BF16)
    grad_pre[...] = gradient
    grad_normed[...] = dot_rt(gradient, up_w[...]).astype(BF16)


def feed(place, rows, cot, own_c, peer_c, own_w, peer_w, out_b, gain, shift, up_w, up_b, down_w):
    n, d = rows.shape
    block = 256
    ff = up_w.shape[1]
    half = own_w.shape[0]

    def part(lanes):
        return pl.BlockSpec((block, lanes), lambda i: (i, 0))

    return pl.pallas_call(
        feed_kernel,
        grid=(n // block,),
        in_specs=[
            pl.BlockSpec(memory_space=pltpu.SMEM),
            part(d),
            part(d),
            part(half),
            part(half),
            full(own_w.shape),
            full(peer_w.shape),
            full((1, d)),
            full((1, d)),
            full((1, d)),
            full(up_w.shape),
            full((1, ff)),
            full(down_w.shape),
        ],
        out_specs=[part(d), part(d), part(ff), part(ff), part(d), full((1, ff))],
        out_shape=[
            shape((n, d), F32),
            shape((n, d), BF16),
            shape((n, ff), BF16),
            shape((n, ff), BF16),
            shape((n, d), BF16),
            shape((1, ff), F32),
        ],
        scratch_shapes=[pltpu.VMEM((2 * half, d), BF16)],
        compiler_params=params(),
        cost_estimate=pl.CostEstimate(
            flops=2 * n * d * (ff * 3 + d), bytes_accessed=24 * 2**20, transcendentals=2 * n * ff
        ),
        name="feed_forward",
    )(place, rows, cot, own_c, peer_c, own_w, peer_w, out_b, gain, shift, up_w, up_b, down_w)


def turn_kernel(
    place, cot, own_g, peer_g, hidden, gain, out_w, merged, grad_hidden, low_out, do, sums, gm_tmp
):
    h = pl.program_id(0)
    n, d = cot.shape
    block = n // FOLD

    @pl.when(h == 0)
    def _():
        unit, inverse = unit_rows(hidden[...])
        gradient = own_g[...].astype(F32) + peer_g[...].astype(F32)
        outer = cot[...].astype(F32)
        total = outer + norm_back(gradient, unit, inverse, gain[...])
        grad_hidden[...] = total
        low_out[...] = total.astype(BF16)
        sums[0:1, :] = jnp.sum(gradient * unit, 0, keepdims=True)
        sums[1:2, :] = jnp.sum(gradient, 0, keepdims=True)
        sums[2:3, :] = jnp.sum(total, 0, keepdims=True)
        sums[3:4, :] = jnp.sum(outer, 0, keepdims=True)
        sums[4:8, :] = jnp.zeros((4, d), F32)

    gm_tmp[...] = dot_rt(low_out[...], out_w[0]).astype(BF16).astype(F32)
    lane = lax.broadcasted_iota(jnp.int32, (block, LANES), 1)
    head = place[0] + h
    for p in range(FOLD):
        c = (head + ORDER[p]) % FOLD
        at = pl.ds(p * block, block)
        gradient = gm_tmp[pl.ds(c, block, stride=FOLD), :]
        delta = jnp.sum(gradient * merged[0, at, :], -1, keepdims=True)
        do[0, at, :] = with_terms(gradient, lane, -delta).astype(BF16)


def turn(place, cot, own_g, peer_g, hidden, gain, out_w, merged):
    n, d = cot.shape
    heads = merged.shape[0]
    return pl.pallas_call(
        turn_kernel,
        grid=(heads,),
        in_specs=[
            pl.BlockSpec(memory_space=pltpu.SMEM),
            full((n, d)),
            full((n, d)),
            full((n, d)),
            full((n, d)),
            full((1, d)),
            per_head(LANES, d),
            per_head(n),
        ],
        out_specs=[full((n, d)), full((n, d)), per_head(n), full((8, d))],
        out_shape=[
            shape((n, d), F32),
            shape((n, d), BF16),
            shape((heads, n, LANES), BF16),
            shape((8, d), F32),
        ],
        scratch_shapes=[pltpu.VMEM((n, LANES), F32)],
        compiler_params=params(),
        cost_estimate=pl.CostEstimate(
            flops=2 * n * d * heads * LANES, bytes_accessed=20 * 2**20, transcendentals=0
        ),
        name="turn",
    )(place, cot, own_g, peer_g, hidden, gain, out_w, merged)


def pair_back(keys, q, do):
    weights = jnp.exp2(dot_rt(keys, q) * EXP_SCALE)
    inner = (weights * dot_rt(keys, do)).astype(BF16)
    grad_keys = dot(weights.astype(BF16), do) + dot(inner, q)
    return grad_keys, dot(keys.T, inner)


def peers_back_kernel(q, do, kv_all, dq, to_core, kept, acc):
    half = q.shape[1]
    n = 2 * half
    for level in (1, 2, 3, 4):
        count = n >> level
        start = (level - 1) * half
        for k in range(0, half, 256):
            grad, grad_q = pair_back(
                kv_all[0, pl.ds(start + k, 256), :], q[0, pl.ds(0, count), :], do[0, pl.ds(0, count), :]
            )
            if level == 1:
                to_core[0, pl.ds(k, 256), :] = grad.astype(BF16)
            elif level == 2:
                if k == 0:
                    kept[0, pl.ds(0, 256), :] = grad
                else:
                    to_core[0, pl.ds(half, 256), :] = grad.astype(BF16)
            else:
                unit = 256 >> 1
                off = 0 if level == 3 else unit
                one, two = grad[:unit], grad[unit:]
                if k == 0:
                    kept[0, pl.ds(256 + off, unit), :] = one
                    kept[0, pl.ds(512 + off, unit), :] = two
                else:
                    to_core[0, pl.ds(half + 256 + off, unit), :] = one.astype(BF16)
                    to_core[0, pl.ds(half + 512 + off, unit), :] = two.astype(BF16)
            if count >= LANES:
                if level == 1 and k == 0:
                    acc[...] = grad_q
                else:
                    acc[:, :count] += grad_q
            else:
                acc[:, :LANES] += jnp.concatenate(
                    [grad_q, jnp.zeros((LANES, LANES - count), F32)], axis=1
                )
    dq[0] = acc[...].T


def peers_back(q, do, kv_all):
    heads, n, _ = q.shape
    assert n == SEG
    return pl.pallas_call(
        peers_back_kernel,
        grid=(heads,),
        in_specs=[per_head(n // 2), per_head(n // 2), per_head(2 * n)],
        out_specs=[per_head(n // 2), per_head(n + n // 4), per_head(3 * n // 4)],
        out_shape=[
            shape((heads, n // 2, LANES), F32),
            shape((heads, n + n // 4, LANES), BF16),
            shape((heads, 3 * n // 4, LANES), F32),
        ],
        scratch_shapes=[pltpu.VMEM((LANES, n // 2), F32)],
        compiler_params=params(),
        cost_estimate=pl.CostEstimate(
            flops=heads * n * n * 1280, bytes_accessed=24 * 2**20, transcendentals=heads * n * n // 2
        ),
        name="peers_back",
    )(q, do, kv_all)


def own_back_kernel(q, do, kv, dq, dkv, acc, *, block):
    n = q.shape[1]
    for i in range(n // block):
        at = pl.ds(i * block, block)
        grad, grad_q = pair_back(kv[0, at, :], q[0], do[0])
        dkv[0, at, :] = grad
        if i == 0:
            acc[...] = grad_q
        else:
            acc[...] += grad_q
    dq[0] = acc[...].T


def own_back(q, do, kv):
    heads, n, _ = q.shape
    return pl.pallas_call(
        functools.partial(own_back_kernel, block=256),
        grid=(heads,),
        in_specs=[per_head(n)] * 3,
        out_specs=[per_head(n)] * 2,
        out_shape=[shape((heads, n, LANES), F32)] * 2,
        scratch_shapes=[pltpu.VMEM((LANES, n), F32)],
        compiler_params=params(),
        cost_estimate=pl.CostEstimate(
            flops=heads * n * n * 2560, bytes_accessed=16 * 2**20, transcendentals=heads * n * n
        ),
        name="own_back",
    )(q, do, kv)


def finish_kernel(
    place, dq_own, dq_peer, dkv_own, r_core, r_x, r_z1, r_z2, r_z3, normed, rows, wide,
    grad_normed, grad_w, grad_b, sums, acc, q_nat, kv_nat, both,
):
    h = pl.program_id(0)
    n, d = rows.shape
    block = n // FOLD
    head = place[0] + h
    for p in range(FOLD):
        c = (head + ORDER[p]) % FOLD
        at = pl.ds(p * block, block)
        q_rows = dq_own[0, at, :]
        kv_rows = dkv_own[0, at, :]
        if CLASS[p] >= 1:
            q_rows = q_rows + dq_peer[0, at, :]
            kv_rows = kv_rows + r_core[0, at, :].astype(F32)
        if CLASS[p] >= 2:
            kv_rows = kv_rows + r_x[0, at, :].astype(F32)
        if CLASS[p] >= 3:
            kv_rows = kv_rows + r_z1[0, at, :].astype(F32)
        if CLASS[p] >= 4:
            kv_rows = kv_rows + (r_z2[0, at, :].astype(F32) + r_z3[0, at, :].astype(F32))
        q_nat[pl.ds(c, block, stride=FOLD), :] = q_rows
        kv_nat[pl.ds(c, block, stride=FOLD), :] = kv_rows
    lane = lax.broadcasted_iota(jnp.int32, (n, LANES), 1)
    q_rows = jnp.where(lane < HD, q_nat[...] * (1.0 / ROOT), 0.0)
    kv_rows = kv_nat[...]
    kv_rows = jnp.where(lane < HD, kv_rows * (1.0 / ROOT), jnp.where(lane < 2 * HD, kv_rows, 0.0))
    grad_b[0, 0:1, :] = jnp.sum(q_rows, 0, keepdims=True)
    grad_b[0, 1:2, :] = jnp.sum(kv_rows, 0, keepdims=True)
    both[:, :LANES] = q_rows.astype(BF16)
    both[:, LANES:] = kv_rows.astype(BF16)
    gradient = dot_lt(both[...], normed[...])
    grad_w[0, 0] = gradient[:HD]
    grad_w[1, 0] = gradient[LANES : LANES + HD]
    grad_w[2, 0] = gradient[LANES + HD : LANES + 2 * HD]
    part = dot_rt(both[...], wide[0])

    @pl.when(h == 0)
    def _():
        acc[...] = part

    @pl.when(h > 0)
    def _():
        acc[...] += part

    @pl.when(h == pl.num_programs(0) - 1)
    def _():
        total = acc[...]
        grad_normed[...] = total.astype(BF16)
        unit, _ = unit_rows(rows[...].astype(F32))
        sums[0:1, :] = jnp.sum(total * unit, 0, keepdims=True)
        sums[1:2, :] = jnp.sum(total, 0, keepdims=True)
        sums[2:8, :] = jnp.zeros((6, d), F32)


def finish(place, dq_own, dq_peer, dkv_own, received, normed, rows, wide):
    heads, n, _ = dq_own.shape
    d = rows.shape[1]
    return pl.pallas_call(
        finish_kernel,
        grid=(heads,),
        in_specs=[
            pl.BlockSpec(memory_space=pltpu.SMEM),
            per_head(n),
            per_head(n // 2),
            per_head(n),
            per_head(n // 2),
            per_head(n // 4),
            per_head(n // 8),
            per_head(n // 16),
            per_head(n // 16),
            full((n, d)),
            full((n, d)),
            per_head(d, 2 * LANES),
        ],
        out_specs=[
            full((n, d)),
            pl.BlockSpec((3, 1, HD, d), lambda h: (0, h, 0, 0)),
            pl.BlockSpec((1, 2, LANES), lambda h: (h, 0, 0)),
            full((8, d)),
        ],
        out_shape=[
            shape((n, d), BF16),
            shape((3, heads, HD, d), F32),
            shape((heads, 2, LANES), F32),
            shape((8, d), F32),
        ],
        scratch_shapes=[
            pltpu.VMEM((n, d), F32),
            pltpu.VMEM((n, LANES), F32),
            pltpu.VMEM((n, LANES), F32),
            pltpu.VMEM((n, 2 * LANES), BF16),
        ],
        compiler_params=params(),
        cost_estimate=pl.CostEstimate(
            flops=4 * n * d * heads * 256, bytes_accessed=30 * 2**20, transcendentals=0
        ),
        name="finish",
    )(place, dq_own, dq_peer, dkv_own, *received, normed, rows, wide)


def last_kernel(rows, own_g, peer_g, grad_hidden, gain, out):
    unit, inverse = unit_rows(rows[...].astype(F32))
    gradient = own_g[...].astype(F32) + peer_g[...].astype(F32)
    out[...] = grad_hidden[...] + norm_back(gradient, unit, inverse, gain[...])


def last(rows, own_g, peer_g, grad_hidden, gain):
    n, d = rows.shape
    part = pl.BlockSpec((256, d), lambda i: (i, 0))
    return pl.pallas_call(
        last_kernel,
        grid=(n // 256,),
        in_specs=[part] * 4 + [full((1, d))],
        out_specs=part,
        out_shape=shape((n, d), F32),
        compiler_params=params(),
        name="last",
    )(rows, own_g, peer_g, grad_hidden, gain)


def swap(x, axis, apart):
    count = lax.axis_size(axis)
    return lax.ppermute(x, axis, [(i, i ^ apart) for i in range(count)])


def local(
    rows,
    lengths,
    norm_gains,
    norm_shifts,
    qkv_weight,
    qv_bias,
    out_weight,
    out_bias,
    up_weight,
    up_bias,
    down_weight,
    down_bias,
    out_cot,
):
    n, d = rows.shape
    width = qkv_weight.shape[2]
    heads = width // HD
    seq_place = lax.axis_index("seq")
    head_place = lax.axis_index("head")
    slide_rows = min(FOLD * SEG, n * lax.axis_size("seq"))
    start = seq_place * n
    slide = start // slide_rows
    length = jnp.sum(jnp.where(jnp.arange(lengths.shape[0]) == slide, lengths, 0))
    limit = jnp.clip(length - start % slide_rows, 0, n)
    place = jnp.stack([head_place * heads, limit, head_place]).astype(jnp.int32)

    peer_out_weight = swap(out_weight, "head", 1)
    wide_out = jnp.pad(
        out_weight.reshape(heads, HD, d), ((0, 0), (HD, LANES - 2 * HD), (0, 0))
    )

    q, kv, s1, sx, sz1, sz, normed1, wide = project(
        place, rows, norm_gains[:1], norm_shifts[:1], qkv_weight, qv_bias
    )
    rz1 = swap(sz1, "seq", 4)
    rx = swap(sx, "seq", 2)
    rz2 = swap(sz, "seq", 8)
    rz3 = swap(sz, "seq", 12)
    cs1 = swap(s1, "seq", 1)
    zc = jnp.concatenate([rz1, rz2, rz3], 1)
    rx2 = swap(zc, "seq", 2)
    crx = swap(rx, "seq", 1)
    czc = swap(zc, "seq", 1)
    crx2 = swap(rx2, "seq", 1)

    own = own_attention(q, kv)
    merged, kv_all, qb, merged_low = peers_attention(
        place, q, own, (cs1, rx, crx, zc, rx2, czc, crx2)
    )
    peer_low = swap(merged_low, "head", 1)

    hidden, normed2, act, grad_pre, grad_normed2, up_bias_grad = feed(
        place,
        rows,
        out_cot,
        merged_low,
        peer_low,
        out_weight,
        peer_out_weight,
        out_bias[None],
        norm_gains[1:],
        norm_shifts[1:],
        up_weight,
        up_bias[None],
        down_weight,
    )
    peer_normed2 = swap(grad_normed2, "head", 1)
    mlp = dot(act, down_weight).astype(BF16)
    down_weight_grad = dot_lt(act, out_cot)
    up_weight_grad = dot_lt(normed2, grad_pre)
    peer_mlp = swap(mlp, "head", 1)
    out_rows = (
        hidden + ((mlp.astype(F32) + peer_mlp.astype(F32)) + down_bias)
    ).astype(BF16)

    grad_hidden, grad_low, do, sums2 = turn(
        place, out_cot, grad_normed2, peer_normed2, hidden, norm_gains[1:], wide_out, merged
    )
    out_weight_grad = dot_lt(merged_low, grad_low)

    dq_peer, to_core, kept = peers_back(qb, do, kv_all)
    r_core = swap(to_core, "seq", 1)
    half = n // 2
    quarter = n // 4

    def both(at):
        return (
            kept[:, at : at + quarter] + r_core[:, half + at : half + at + quarter].astype(F32)
        )

    r_x2 = swap(both(2 * quarter).astype(BF16), "seq", 2)
    r_x = swap(both(0).astype(BF16), "seq", 2)
    z_sum = (both(quarter) + r_x2.astype(F32)).astype(BF16)
    eighth = n // 8
    r_z1 = swap(z_sum[:, :eighth], "seq", 4)
    r_z2 = swap(z_sum[:, eighth : eighth + n // 16], "seq", 8)
    r_z3 = swap(z_sum[:, eighth + n // 16 :], "seq", 12)

    dq_own, dkv_own = own_back(qb, do, kv)
    grad_normed1, grad_w, grad_b, sums1 = finish(
        place, dq_own, dq_peer, dkv_own, (r_core, r_x, r_z1, r_z2, r_z3), normed1, rows, wide
    )
    peer_normed1 = swap(grad_normed1, "head", 1)
    rows_grad = last(rows, grad_normed1, peer_normed1, grad_hidden, norm_gains[:1])

    up_weight_grad, down_weight_grad, out_weight_grad = (
        g.astype(F32)
        for g in lax.psum(
            tuple(g.astype(BF16) for g in (up_weight_grad, down_weight_grad, out_weight_grad)),
            "seq",
        )
    )
    grad_w = lax.psum(grad_w.astype(BF16), "seq").astype(F32)
    qkv_grad = jnp.swapaxes(grad_w.reshape(3, width, d), 1, 2)
    qv_bias_grad = jnp.stack(
        [grad_b[:, 0, :HD].reshape(width), grad_b[:, 1, HD : 2 * HD].reshape(width)]
    )
    up_bias_grad, qv_bias_grad, sums2 = lax.psum((up_bias_grad, qv_bias_grad, sums2), "seq")
    sums1 = lax.psum(sums1, ("seq", "head"))
    return (
        out_rows,
        rows_grad,
        jnp.stack([sums1[0], sums2[0]]),
        jnp.stack([sums1[1], sums2[1]]),
        qkv_grad,
        qv_bias_grad,
        out_weight_grad,
        sums2[2],
        up_weight_grad,
        up_bias_grad[0],
        down_weight_grad,
        sums2[3],
    )


def solution(mesh):
    placed = (
        P("seq", None),
        P(),
        P(),
        P(),
        P(None, None, "head"),
        P(None, "head"),
        P("head", None),
        P(),
        P(None, "head"),
        P("head"),
        P("head", None),
        P(),
        P("seq", None),
    )
    return jax.shard_map(
        local,
        mesh=mesh,
        in_specs=placed,
        out_specs=(
            P("seq", None),
            P("seq", None),
            P(),
            P(),
            P(None, None, "head"),
            P(None, "head"),
            P("head", None),
            P(),
            P(None, "head"),
            P("head"),
            P("head", None),
            P(),
        ),
        check_vma=False,
    )
```

```python
import functools
import math

import jax
import jax.numpy as jnp
import numpy as np
from jax import lax
from jax.experimental import pallas as pl
from jax.experimental.pallas import tpu as pltpu
from jax.sharding import PartitionSpec as P

HD = 48
SEG = 1024
LANES = 128
LEVELS = 5
FOLD = 16

EPS = 1e-05
ROOT = math.sqrt(HD)
EXP_SCALE = math.log2(math.e) / ROOT
ROOT_HALF = 1.0 / math.sqrt(2.0)
DENSITY_NORM = 1.0 / math.sqrt(2.0 * math.pi)
ABSENT = -1e20

ONE = 96
MASK = 99
MULT = 100
TOP = 127

ORDER = (0, 8, 4, 12, 2, 6, 10, 14, 1, 3, 5, 7, 9, 11, 13, 15)
CLASS = (4, 3, 2, 2, 1, 1, 1, 1, 0, 0, 0, 0, 0, 0, 0, 0)

F32 = jnp.float32
BF16 = jnp.bfloat16


LIGHT = pl.CostEstimate(flops=0, bytes_accessed=0, transcendentals=0)


def params(mib=48):
    return pltpu.CompilerParams(vmem_limit_bytes=mib * 2**20)


def dot(left, right):
    return jnp.dot(left, right, preferred_element_type=F32)


def dot_rt(left, right):
    return lax.dot_general(left, right, (((1,), (1,)), ((), ())), preferred_element_type=F32)


def dot_lt(left, right):
    return lax.dot_general(left, right, (((0,), (0,)), ((), ())), preferred_element_type=F32)


def full(shape):
    return pl.BlockSpec(shape, lambda *_: (0,) * len(shape))


def per_head(rows, lanes=LANES):
    return pl.BlockSpec((1, rows, lanes), lambda h: (h, 0, 0))


def shape(dims, kind):
    return jax.ShapeDtypeStruct(dims, kind)


def split3(x):
    high = x.astype(BF16).astype(F32)
    rest = x - high
    middle = rest.astype(BF16).astype(F32)
    return high, middle, rest - middle


def with_terms(block, lane, terms):
    high, middle, low = split3(terms)
    block = jnp.where(lane == ONE, high, block)
    block = jnp.where(lane == ONE + 1, middle, block)
    return jnp.where(lane == ONE + 2, low, block)


def unit_rows(x):
    mean = jnp.mean(x, -1, keepdims=True)
    centred = x - mean
    inverse = lax.rsqrt(jnp.mean(centred * centred, -1, keepdims=True) + EPS)
    return centred * inverse, inverse


def norm_back(gradient, unit, inverse, gain):
    z = gradient * gain
    return inverse * (
        z - jnp.mean(z, -1, keepdims=True) - unit * jnp.mean(z * unit, -1, keepdims=True)
    )


def mult_table(level, blocks):
    table = np.zeros((len(blocks), LANES), np.float32)
    for row, key_class in enumerate(blocks):
        for j in range(level + 1, key_class + 1):
            value = np.float32(ROOT * math.log((j - level + 1) / (j - level)))
            high = np.float32(value.astype(jnp.bfloat16))
            table[row, MULT + j - 1] = high
            table[row, MULT + 4 + j - 1] = np.float32((value - high).astype(jnp.bfloat16))
    return table


def own_table():
    return mult_table(0, CLASS)


def peer_table():
    return np.concatenate(
        [
            mult_table(1, CLASS[:8]),
            mult_table(2, CLASS[:4] * 2),
            mult_table(3, CLASS[:2] * 4),
            mult_table(4, CLASS[:1] * 8),
        ]
    )


def project_kernel(
    place, rows, gain, shift, w, bias, table, q, kv, s1, sx, sz1, sz, normed, wide, w_tmp, b_tmp, q_tmp, kv_tmp
):
    h = pl.program_id(0)
    n, d = rows.shape
    heads = w.shape[2] // HD
    block = n // FOLD

    @pl.when(h == 0)
    def _():
        unit, _ = unit_rows(rows[...].astype(F32))
        normed[...] = (unit * gain[...] + shift[...]).astype(BF16)

    for k in range(heads):

        @pl.when(h == k)
        def _():
            cut = slice(k * HD, (k + 1) * HD)
            w_tmp[:, :LANES] = jnp.concatenate(
                [w[0, :, cut], jnp.zeros((d, LANES - HD), BF16)], axis=1
            )
            w_tmp[:, LANES:] = jnp.concatenate(
                [w[1, :, cut], w[2, :, cut], jnp.zeros((d, LANES - 2 * HD), BF16)], axis=1
            )
            b_tmp[:, :LANES] = jnp.concatenate(
                [bias[0:1, cut], jnp.zeros((1, LANES - HD), F32)], axis=1
            )
            b_tmp[:, LANES:] = jnp.concatenate(
                [
                    jnp.zeros((1, HD), F32),
                    bias[1:2, cut],
                    jnp.ones((1, 3), F32),
                    jnp.zeros((1, LANES - 2 * HD - 3), F32),
                ],
                axis=1,
            )

    wide[0] = w_tmp[...]
    product = dot(normed[...], w_tmp[...]) + b_tmp[...]
    q_tmp[...] = product[:, :LANES]
    kv_tmp[...] = product[:, LANES:]
    lane = lax.broadcasted_iota(jnp.int32, (block, LANES), 1)
    step = lax.broadcasted_iota(jnp.int32, (block, LANES), 0) * FOLD
    head = place[0] + h
    for p in range(FOLD):
        c = (head + ORDER[p]) % FOLD
        here = step + c < place[1]
        at = pl.ds(p * block, block)
        q_rows = q_tmp[pl.ds(c, block, stride=FOLD), :]
        kv_rows = kv_tmp[pl.ds(c, block, stride=FOLD), :]
        level = CLASS[p]
        flags = ((lane >= MULT) & (lane < MULT + level)) | (
            (lane >= MULT + 4) & (lane < MULT + 4 + level)
        )
        q_rows = jnp.where(flags, 1.0, q_rows)
        q_rows = jnp.where(lane == MASK, jnp.where(here, 1.0, 0.0), q_rows)
        q[0, at, :] = q_rows.astype(BF16)
        kv_rows = jnp.where(lane == MASK, jnp.where(here, 0.0, ABSENT), kv_rows)
        kv[0, at, :] = (kv_rows + table[p : p + 1, :]).astype(BF16)
        if level >= 1:
            low = kv_rows.astype(BF16)
            s1[0, at, :] = low
            if level >= 2:
                sx[0, at, :] = low
            if level >= 3:
                sz1[0, at, :] = low
            if level >= 4:
                sz[0, at, :] = low


def project(place, rows, gain, shift, w, bias):
    n, d = rows.shape
    heads = w.shape[2] // HD
    table = jnp.asarray(own_table())
    sizes = (n, n, n // 2, n // 4, n // 8, n // 16)
    return pl.pallas_call(
        project_kernel,
        grid=(heads,),
        in_specs=[
            pl.BlockSpec(memory_space=pltpu.SMEM),
            full(rows.shape),
            full(gain.shape),
            full(shift.shape),
            full(w.shape),
            full(bias.shape),
            full(table.shape),
        ],
        out_specs=[per_head(m) for m in sizes]
        + [full((n, d)), pl.BlockSpec((1, d, 2 * LANES), lambda h: (h, 0, 0))],
        out_shape=[shape((heads, m, LANES), BF16) for m in sizes]
        + [shape((n, d), BF16), shape((heads, d, 2 * LANES), BF16)],
        scratch_shapes=[
            pltpu.VMEM((d, 2 * LANES), BF16),
            pltpu.VMEM((1, 2 * LANES), F32),
            pltpu.VMEM((n, LANES), F32),
            pltpu.VMEM((n, LANES), F32),
        ],
        compiler_params=params(),
        cost_estimate=pl.CostEstimate(
            flops=2 * n * d * heads * 256, bytes_accessed=14 * 2**20, transcendentals=0
        ),
        name="project",
    )(place, rows, gain, shift, w, bias, table)


def own_kernel(q, kv, out, *, block):
    n = q.shape[1]
    keys = kv[0]
    lane = lax.broadcasted_iota(jnp.int32, (block, LANES), 1)

    def scores(i):
        return dot_rt(q[0, pl.ds(i * block, block), :], keys)

    now = scores(0)
    for i in range(n // block):
        later = scores(i + 1) if (i + 1) * block < n else None
        top = jnp.max(now, -1, keepdims=True)
        weights = jnp.exp2((now - top) * EXP_SCALE).astype(BF16)
        out[0, pl.ds(i * block, block), :] = jnp.where(lane == TOP, top, dot(weights, keys))
        now = later


def group_spec(rows, start, lanes=LANES):
    return pl.BlockSpec((1, rows, lanes), lambda h: (h + start, 0, 0))


ANYWHERE = pl.BlockSpec(memory_space=pl.ANY)


def own_attention(q, kv, start, count, into=None):
    heads, n, _ = q.shape
    spec = group_spec(n, start)
    kernel = functools.partial(own_kernel, block=256)
    extra = () if into is None else (into,)
    return pl.pallas_call(
        kernel if into is None else lambda q, kv, _, out: kernel(q, kv, out),
        grid=(count,),
        in_specs=[spec] * 2 + [ANYWHERE] * len(extra),
        out_specs=spec,
        out_shape=shape((heads, n, LANES), F32),
        input_output_aliases={2: 0} if extra else {},
        compiler_params=params(),
        cost_estimate=pl.CostEstimate(
            flops=count * n * n * 1024, bytes_accessed=4 * 2**20, transcendentals=count * n * n
        ),
        name="own_attention",
    )(q, kv, *extra)


def peers_kernel(
    place, q, own, cs1, rx, crx, zc, rx2, czc, crx2, table, pick, merged, kv_all, qb, low, nat, wide
):
    h = pl.program_id(0)
    n = q.shape[1]
    block = n // FOLD
    at = 0
    near = (zc, rx2, czc, crx2)
    pieces = [(cs1, 0, n // 2), (rx, 0, n // 4), (crx, 0, n // 4)]
    pieces += [(r, 0, n // 8) for r in near] + [(r, n // 8, n // 8) for r in near]
    for ref, start, count in pieces:
        for k in range(count // block):
            rows = ref[0, pl.ds(start + k * block, block), :].astype(F32)
            index = at // block
            kv_all[0, pl.ds(at, block), :] = (rows + table[index : index + 1, :]).astype(BF16)
            at += block

    head = place[0] + h
    chunks = [
        (0, n // 16, 2 * n),
        (n // 16, n // 16, 3 * n // 2),
        (n // 8, n // 8, n),
        (n // 4, n // 4, n // 2),
        (n // 2, n // 2, 0),
    ]
    scores = []
    for start, count, keys in chunks:
        if keys:
            scores.append(dot_rt(q[0, pl.ds(start, count), :], kv_all[0, pl.ds(0, keys), :]))
        else:
            scores.append(None)
    for (start, count, keys), s in zip(chunks, scores):
        rows = pl.ds(start, count)
        lane = lax.broadcasted_iota(jnp.int32, (count, LANES), 1)
        o = own[0, rows, :]
        top = o[:, TOP : TOP + 1]
        if keys:
            new = jnp.maximum(top, jnp.max(s, -1, keepdims=True))
            weights = jnp.exp2((s - new) * EXP_SCALE).astype(BF16)
            o = o * jnp.exp2((top - new) * EXP_SCALE) + dot(weights, kv_all[0, pl.ds(0, keys), :])
            top = new
        total = o[:, ONE : ONE + 1]
        o = jnp.where((lane >= HD) & (lane < 2 * HD), o / total, 0.0)
        merged[0, rows, :] = o
        lse = top + jnp.log2(total) * (1.0 / EXP_SCALE)
        qb[0, rows, :] = with_terms(q[0, rows, :].astype(F32), lane, -lse).astype(BF16)
        for p in range(start // block, (start + count) // block):
            c = (head + ORDER[p]) % FOLD
            off = p * block - start
            nat[pl.ds(c, block, stride=FOLD), :] = o[off : off + block]
    wide[:, pl.ds(pl.multiple_of(h * LANES, LANES), LANES)] = nat[...].astype(BF16)

    @pl.when(h == pl.num_programs(0) - 1)
    def _():
        low[...] = dot(wide[...], pick[...]).astype(BF16)


def pick_values(heads):
    m = np.zeros((heads * LANES, heads * HD), np.float32)
    for h in range(heads):
        for j in range(HD):
            m[h * LANES + HD + j, h * HD + j] = 1.0
    return m


def peers_attention(place, q, own, received):
    heads, n, _ = q.shape
    table = jnp.asarray(peer_table())
    pick = jnp.asarray(pick_values(heads), BF16)
    return pl.pallas_call(
        peers_kernel,
        grid=(heads,),
        in_specs=[pl.BlockSpec(memory_space=pltpu.SMEM), per_head(n), per_head(n)]
        + [per_head(r.shape[1]) for r in received]
        + [full(table.shape), full(pick.shape)],
        out_specs=[per_head(n), per_head(2 * n), per_head(n), full((n, heads * HD))],
        out_shape=[
            shape((heads, n, LANES), F32),
            shape((heads, 2 * n, LANES), BF16),
            shape((heads, n, LANES), BF16),
            shape((n, heads * HD), BF16),
        ],
        scratch_shapes=[pltpu.VMEM((n, LANES), F32), pltpu.VMEM((n, heads * LANES), BF16)],
        compiler_params=params(),
        cost_estimate=pl.CostEstimate(
            flops=heads * n * n * 512, bytes_accessed=24 * 2**20, transcendentals=heads * n * n // 2
        ),
        name="peers_attention",
    )(place, q, own, *received, table, pick)


def feed_kernel(
    place, rows, cot, own_c, peer_c, own_w, peer_w, out_b, gain, shift, up_w, up_b, down_w,
    hidden, normed, act, grad_pre, grad_normed, up_b_grad, w_tmp,
):
    i = pl.program_id(0)
    half = own_w.shape[0]
    first = place[2] == 0

    @pl.when(i == 0)
    def _():
        w_tmp[:half] = jnp.where(first, own_w[...], peer_w[...])
        w_tmp[half:] = jnp.where(first, peer_w[...], own_w[...])

    one = jnp.where(first, own_c[...], peer_c[...])
    two = jnp.where(first, peer_c[...], own_c[...])
    attended = dot(one, w_tmp[:half]) + dot(two, w_tmp[half:])
    hid = rows[...].astype(F32) + (attended + out_b[...])
    hidden[...] = hid
    unit, _ = unit_rows(hid)
    low = (unit * gain[...] + shift[...]).astype(BF16)
    normed[...] = low
    pre = dot(low, up_w[...]) + up_b[...]
    phi = 0.5 * (1.0 + lax.erf(pre * ROOT_HALF))
    act[...] = (pre * phi).astype(BF16)
    slope = phi + pre * jnp.exp(-0.5 * pre * pre) * DENSITY_NORM
    gradient = dot_rt(cot[...], down_w[...]) * slope
    total = jnp.sum(gradient, 0, keepdims=True)

    @pl.when(i == 0)
    def _():
        up_b_grad[...] = total

    @pl.when(i > 0)
    def _():
        up_b_grad[...] += total

    gradient = gradient.astype(BF16)
    grad_pre[...] = gradient
    grad_normed[...] = dot_rt(gradient, up_w[...]).astype(BF16)


def feed(
    place, rows, cot, own_c, peer_c, own_w, peer_w, out_b, gain, shift, up_w, up_b, down_w, start, count, into=None
):
    n, d = rows.shape
    block = 256
    ff = up_w.shape[1]
    half = own_w.shape[0]
    first = start // block
    extra = () if into is None else tuple(into)

    def part(lanes):
        return pl.BlockSpec((block, lanes), lambda i: (i + first, 0))

    def kernel(*refs):
        feed_kernel(*refs[:13], *refs[13 + len(extra) :])

    return pl.pallas_call(
        kernel,
        grid=(count // block,),
        in_specs=[
            pl.BlockSpec(memory_space=pltpu.SMEM),
            part(d),
            part(d),
            part(half),
            part(half),
            full(own_w.shape),
            full(peer_w.shape),
            full((1, d)),
            full((1, d)),
            full((1, d)),
            full(up_w.shape),
            full((1, ff)),
            full(down_w.shape),
        ]
        + [ANYWHERE] * len(extra),
        out_specs=[
            part(d),
            part(d),
            part(ff),
            part(ff),
            pl.BlockSpec((block, d), lambda i: (i, 0)),
            full((1, ff)),
        ],
        out_shape=[
            shape((n, d), F32),
            shape((n, d), BF16),
            shape((n, ff), BF16),
            shape((n, ff), BF16),
            shape((count, d), BF16),
            shape((1, ff), F32),
        ],
        input_output_aliases={13 + k: k for k in range(len(extra))},
        scratch_shapes=[pltpu.VMEM((2 * half, d), BF16)],
        compiler_params=params(),
        cost_estimate=pl.CostEstimate(
            flops=2 * count * d * (ff * 3 + d),
            bytes_accessed=12 * 2**20,
            transcendentals=2 * count * ff,
        ),
        name="feed_forward",
    )(
        place, rows, cot, own_c, peer_c, own_w, peer_w, out_b, gain, shift, up_w, up_b, down_w, *extra
    )


def weights_kernel(place, act, grad_pre, normed, cot, down_w, mlp, keep, send, acc):
    i = pl.program_id(0)
    part = dot(act[...], down_w[...])

    @pl.when(i == 0)
    def _():
        acc[...] = part

    @pl.when(i > 0)
    def _():
        acc[...] += part

    down = dot_lt(act[...], cot[...])
    up = dot_lt(grad_pre[...], normed[...])
    first = place[3] == 0
    keep[...] = jnp.where(first, down, up)
    send[...] = jnp.where(first, up, down).astype(BF16)

    @pl.when(i == pl.num_programs(0) - 1)
    def _():
        mlp[...] = acc[...].astype(BF16)


def weights(place, act, grad_pre, normed, cot, down_w):
    n, ff = act.shape
    d = cot.shape[1]
    block = 256
    lanes = pl.BlockSpec((n, block), lambda i: (0, i))
    rows = pl.BlockSpec((block, d), lambda i: (i, 0))
    return pl.pallas_call(
        weights_kernel,
        grid=(ff // block,),
        in_specs=[
            pl.BlockSpec(memory_space=pltpu.SMEM),
            lanes,
            lanes,
            full((n, d)),
            full((n, d)),
            rows,
        ],
        out_specs=[full((n, d)), rows, rows],
        out_shape=[shape((n, d), BF16), shape((ff, d), F32), shape((ff, d), BF16)],
        scratch_shapes=[pltpu.VMEM((n, d), F32)],
        compiler_params=params(),
        cost_estimate=pl.CostEstimate(
            flops=6 * n * d * ff, bytes_accessed=20 * 2**20, transcendentals=0
        ),
        name="weights",
    )(place, act, grad_pre, normed, cot, down_w)


def turn_kernel(cot, own_g, peer_g, hidden, gain, out_w, grad_hidden, low_out, gm, sums):
    i = pl.program_id(0)
    unit, inverse = unit_rows(hidden[...])
    gradient = own_g[...].astype(F32) + peer_g[...].astype(F32)
    outer = cot[...].astype(F32)
    total = outer + norm_back(gradient, unit, inverse, gain[...])
    grad_hidden[...] = total
    low = total.astype(BF16)
    low_out[...] = low
    gm[...] = dot_rt(low, out_w[...]).astype(BF16).astype(F32)

    @pl.when(i == 0)
    def _():
        sums[...] = jnp.zeros_like(sums)

    sums[0:1, :] += jnp.sum(gradient * unit, 0, keepdims=True)
    sums[1:2, :] += jnp.sum(gradient, 0, keepdims=True)
    sums[2:3, :] += jnp.sum(total, 0, keepdims=True)
    sums[3:4, :] += jnp.sum(outer, 0, keepdims=True)


def turn(cot, own_g, peer_g, hidden, gain, out_w, start, count, into=None):
    n, d = cot.shape
    block = 256
    first = start // block
    wide = out_w.shape[0]
    extra = () if into is None else tuple(into)

    def part(lanes):
        return pl.BlockSpec((block, lanes), lambda i: (i + first, 0))

    own_part = pl.BlockSpec((block, d), lambda i: (i, 0))

    def kernel(*refs):
        turn_kernel(*refs[:6], *refs[6 + len(extra) :])

    return pl.pallas_call(
        kernel,
        grid=(count // block,),
        in_specs=[part(d), own_part, own_part, part(d), full((1, d)), full((wide, d))]
        + [ANYWHERE] * len(extra),
        out_specs=[part(d), part(d), part(wide), full((8, d))],
        out_shape=[
            shape((n, d), F32),
            shape((n, d), BF16),
            shape((n, wide), F32),
            shape((8, d), F32),
        ],
        input_output_aliases={6 + k: k for k in range(len(extra))},
        compiler_params=params(),
        cost_estimate=LIGHT,
        name="turn",
    )(cot, own_g, peer_g, hidden, gain, out_w, *extra)


def pair_back(keys, q, do):
    weights = jnp.exp2(dot_rt(keys, q) * EXP_SCALE)
    inner = (weights * dot_rt(keys, do)).astype(BF16)
    grad_keys = dot(weights.astype(BF16), do) + dot(inner, q)
    return grad_keys, dot(keys.T, inner)


def peers_back_kernel(place, gm, merged, q, kv_all, do, dq, to_core, kept, acc):
    half = q.shape[1]
    n = 2 * half
    block = n // FOLD
    lane = lax.broadcasted_iota(jnp.int32, (block, LANES), 1)
    head = place[0] + pl.program_id(0)
    for p in range(FOLD):
        c = (head + ORDER[p]) % FOLD
        at = pl.ds(p * block, block)
        gradient = gm[pl.ds(c, block, stride=FOLD), :]
        delta = jnp.sum(gradient * merged[0, at, :], -1, keepdims=True)
        do[0, at, :] = with_terms(gradient, lane, -delta).astype(BF16)
    for level in (1, 2, 3, 4):
        count = n >> level
        start = (level - 1) * half
        for k in range(0, half, 256):
            grad, grad_q = pair_back(
                kv_all[0, pl.ds(start + k, 256), :], q[0, pl.ds(0, count), :], do[0, pl.ds(0, count), :]
            )
            if level == 1:
                to_core[0, pl.ds(k, 256), :] = grad.astype(BF16)
            elif level == 2:
                if k == 0:
                    kept[0, pl.ds(0, 256), :] = grad
                else:
                    to_core[0, pl.ds(half, 256), :] = grad.astype(BF16)
            else:
                unit = 256 >> 1
                off = 0 if level == 3 else unit
                one, two = grad[:unit], grad[unit:]
                if k == 0:
                    kept[0, pl.ds(256 + off, unit), :] = one
                    kept[0, pl.ds(512 + off, unit), :] = two
                else:
                    to_core[0, pl.ds(half + 256 + off, unit), :] = one.astype(BF16)
                    to_core[0, pl.ds(half + 512 + off, unit), :] = two.astype(BF16)
            if count >= LANES:
                if level == 1 and k == 0:
                    acc[...] = grad_q
                else:
                    acc[:, :count] += grad_q
            else:
                acc[:, :LANES] += jnp.concatenate(
                    [grad_q, jnp.zeros((LANES, LANES - count), F32)], axis=1
                )
    dq[0] = acc[...].T


def peers_back(place, gm, merged, q, kv_all):
    heads, n, _ = q.shape
    assert n == SEG
    return pl.pallas_call(
        peers_back_kernel,
        grid=(heads,),
        in_specs=[
            pl.BlockSpec(memory_space=pltpu.SMEM),
            pl.BlockSpec((n, LANES), lambda h: (0, h)),
            per_head(n),
            per_head(n // 2),
            per_head(2 * n),
        ],
        out_specs=[per_head(n), per_head(n // 2), per_head(n + n // 4), per_head(3 * n // 4)],
        out_shape=[
            shape((heads, n, LANES), BF16),
            shape((heads, n // 2, LANES), F32),
            shape((heads, n + n // 4, LANES), BF16),
            shape((heads, 3 * n // 4, LANES), F32),
        ],
        scratch_shapes=[pltpu.VMEM((LANES, n // 2), F32)],
        compiler_params=params(),
        cost_estimate=pl.CostEstimate(
            flops=heads * n * n * 1280, bytes_accessed=24 * 2**20, transcendentals=heads * n * n // 2
        ),
        name="peers_back",
    )(place, gm, merged, q, kv_all)


def own_back_kernel(q, do, kv, dq, dkv, acc, *, block):
    n = q.shape[1]
    for i in range(n // block):
        at = pl.ds(i * block, block)
        grad, grad_q = pair_back(kv[0, at, :], q[0], do[0])
        dkv[0, at, :] = grad
        if i == 0:
            acc[...] = grad_q
        else:
            acc[...] += grad_q
    dq[0] = acc[...].T


def own_back(q, do, kv, start, count, into=None):
    heads, n, _ = q.shape
    spec = group_spec(n, start)
    kernel = functools.partial(own_back_kernel, block=256)
    extra = () if into is None else tuple(into)
    return pl.pallas_call(
        kernel if into is None else lambda q, do, kv, _, __, *out: kernel(q, do, kv, *out),
        grid=(count,),
        in_specs=[spec] * 3 + [ANYWHERE] * len(extra),
        out_specs=[spec] * 2,
        out_shape=[shape((heads, n, LANES), F32)] * 2,
        input_output_aliases={3: 0, 4: 1} if extra else {},
        scratch_shapes=[pltpu.VMEM((LANES, n), F32)],
        compiler_params=params(),
        cost_estimate=pl.CostEstimate(
            flops=count * n * n * 2560, bytes_accessed=8 * 2**20, transcendentals=count * n * n
        ),
        name="own_back",
    )(q, do, kv, *extra)


def finish_q_kernel(
    place, dq_own, dq_peer, normed, wide, merged, grad_low, acc, grad_w, grad_b, nat0, nat1
):
    i = pl.program_id(0)
    n = nat0.shape[0]
    lane = lax.broadcasted_iota(jnp.int32, (n, LANES), 1)
    low = []
    for j, nat in enumerate((nat0, nat1)):
        unpermute(place[0] + 2 * i + j, j, (dq_own, dq_peer), nat)
        rows = jnp.where(lane < HD, nat[...] * (1.0 / ROOT), 0.0)
        grad_b[j, 0:1, :] = jnp.sum(rows, 0, keepdims=True)
        low.append(rows.astype(BF16))
    low = jnp.concatenate(low, axis=1)
    gradient = dot_lt(low, normed[...])
    grad_w[0, 0] = gradient[:HD]
    grad_w[0, 1] = gradient[LANES : LANES + HD]
    for k in range(merged.shape[1] // (2 * HD)):

        @pl.when(i == k)
        def _():
            pair = dot_lt(merged[:, 2 * k * HD : 2 * (k + 1) * HD], grad_low[...])
            grad_w[1, 0] = pair[:HD]
            grad_w[1, 1] = pair[HD:]

    part = dot_rt(low, jnp.concatenate([wide[0], wide[1]], axis=1))

    @pl.when(i == 0)
    def _():
        acc[...] = part

    @pl.when(i > 0)
    def _():
        acc[...] += part


def unpermute(head, j, sources, nat):
    n = nat.shape[0]
    block = n // FOLD
    for p in range(FOLD):
        c = (head + ORDER[p]) % FOLD
        at = pl.ds(p * block, block)
        total = None
        for ref in sources:
            if p * block < ref.shape[1]:
                piece = ref[j, at, :].astype(F32)
                total = piece if total is None else total + piece
        nat[pl.ds(c, block, stride=FOLD), :] = total


def finish_kv_kernel(
    place, dkv_own, r_core, r_x, r_z1, r_z2, r_z3, normed, rows, wide, start,
    grad_normed, grad_w, grad_b, sums, acc, nat0, nat1,
):
    i = pl.program_id(0)
    n, d = rows.shape
    lane = lax.broadcasted_iota(jnp.int32, (n, LANES), 1)
    low = []
    for j, nat in enumerate((nat0, nat1)):
        unpermute(place[0] + 2 * i + j, j, (dkv_own, r_core, r_x, r_z1, r_z2, r_z3), nat)
        both = nat[...]
        both = jnp.where(lane < HD, both * (1.0 / ROOT), jnp.where(lane < 2 * HD, both, 0.0))
        grad_b[j, 0:1, :] = jnp.sum(both, 0, keepdims=True)
        low.append(both.astype(BF16))
    low = jnp.concatenate(low, axis=1)
    gradient = dot_lt(low, normed[...])
    for j in range(2):
        grad_w[0, j] = gradient[j * LANES : j * LANES + HD]
        grad_w[1, j] = gradient[j * LANES + HD : j * LANES + 2 * HD]
    part = dot_rt(low, jnp.concatenate([wide[0], wide[1]], axis=1))

    @pl.when(i == 0)
    def _():
        acc[...] = start[...] + part

    @pl.when(i > 0)
    def _():
        acc[...] += part

    @pl.when(i == pl.num_programs(0) - 1)
    def _():
        total = acc[...]
        grad_normed[...] = total.astype(BF16)
        unit, _ = unit_rows(rows[...].astype(F32))
        sums[0:1, :] = jnp.sum(total * unit, 0, keepdims=True)
        sums[1:2, :] = jnp.sum(total, 0, keepdims=True)
        sums[2:8, :] = jnp.zeros((6, d), F32)


def pairs(rows):
    return pl.BlockSpec((2, rows, LANES), lambda i: (i, 0, 0))


def finish_q(place, dq_own, dq_peer, normed, wide, merged, grad_low):
    heads, n, _ = dq_own.shape
    d = normed.shape[1]
    return pl.pallas_call(
        finish_q_kernel,
        grid=(heads // 2,),
        in_specs=[
            pl.BlockSpec(memory_space=pltpu.SMEM),
            pairs(n),
            pairs(n // 2),
            full((n, d)),
            pl.BlockSpec((2, d, LANES), lambda i: (i, 0, 0)),
            full(merged.shape),
            full((n, d)),
        ],
        out_specs=[
            full((n, d)),
            pl.BlockSpec((2, 2, HD, d), lambda i: (0, i, 0, 0)),
            pl.BlockSpec((2, 1, LANES), lambda i: (i, 0, 0)),
        ],
        out_shape=[
            shape((n, d), F32),
            shape((2, heads, HD, d), F32),
            shape((heads, 1, LANES), F32),
        ],
        scratch_shapes=[pltpu.VMEM((n, LANES), F32)] * 2,
        compiler_params=params(),
        cost_estimate=pl.CostEstimate(
            flops=4 * n * d * heads * 128, bytes_accessed=14 * 2**20, transcendentals=0
        ),
        name="finish_q",
    )(place, dq_own, dq_peer, normed, wide, merged, grad_low)


def finish_kv(place, dkv_own, received, normed, rows, wide, start):
    heads, n, _ = dkv_own.shape
    d = normed.shape[1]
    return pl.pallas_call(
        finish_kv_kernel,
        grid=(heads // 2,),
        in_specs=[
            pl.BlockSpec(memory_space=pltpu.SMEM),
            pairs(n),
            pairs(n // 2),
            pairs(n // 4),
            pairs(n // 8),
            pairs(n // 16),
            pairs(n // 16),
            full((n, d)),
            full((n, d)),
            pl.BlockSpec((2, d, LANES), lambda i: (i, 0, 1)),
            full((n, d)),
        ],
        out_specs=[
            full((n, d)),
            pl.BlockSpec((2, 2, HD, d), lambda i: (0, i, 0, 0)),
            pl.BlockSpec((2, 1, LANES), lambda i: (i, 0, 0)),
            full((8, d)),
        ],
        out_shape=[
            shape((n, d), BF16),
            shape((2, heads, HD, d), F32),
            shape((heads, 1, LANES), F32),
            shape((8, d), F32),
        ],
        scratch_shapes=[pltpu.VMEM((n, d), F32)] + [pltpu.VMEM((n, LANES), F32)] * 2,
        compiler_params=params(),
        cost_estimate=pl.CostEstimate(
            flops=4 * n * d * heads * 128, bytes_accessed=20 * 2**20, transcendentals=0
        ),
        name="finish_kv",
    )(place, dkv_own, *received, normed, rows, wide, start)


def spread_kernel(place, own, peer, down, up):
    first = place[3] == 0
    down[...] = jnp.where(first, own[...], peer[...]).astype(F32)
    up[...] = jnp.where(first, peer[...], own[...]).astype(F32).T


def spread(place, own, peer):
    ff, d = own.shape
    block = 256
    rows = pl.BlockSpec((block, d), lambda i: (i, 0))
    return pl.pallas_call(
        spread_kernel,
        grid=(ff // block,),
        in_specs=[pl.BlockSpec(memory_space=pltpu.SMEM), rows, rows],
        out_specs=[rows, pl.BlockSpec((d, block), lambda i: (0, i))],
        out_shape=[shape((ff, d), F32), shape((d, ff), F32)],
        compiler_params=params(),
        name="spread",
    )(place, own, peer)


def spread_qkv_kernel(place, own, peer, qkv, out):
    first = place[3] == 0
    half, d = own.shape
    width = qkv.shape[2]
    one = jnp.where(first, own[...], peer[...]).astype(F32)
    two = jnp.where(first, peer[...], own[...]).astype(F32)
    qkv[0] = one[:width].T
    qkv[1] = two[:width].T
    qkv[2] = two[width:].T
    out[...] = one[width:]


def spread_qkv(place, own, peer):
    half, d = own.shape
    width = half // 2
    return pl.pallas_call(
        spread_qkv_kernel,
        in_specs=[pl.BlockSpec(memory_space=pltpu.SMEM), full(own.shape), full(own.shape)],
        out_specs=[full((3, d, width)), full((width, d))],
        grid=(1,),
        out_shape=[shape((3, d, width), F32), shape((width, d), F32)],
        compiler_params=params(),
        name="spread_qkv",
    )(place, own, peer)


def last_kernel(rows, own_g, peer_g, grad_hidden, gain, out):
    unit, inverse = unit_rows(rows[...].astype(F32))
    gradient = own_g[...].astype(F32) + peer_g[...].astype(F32)
    out[...] = grad_hidden[...] + norm_back(gradient, unit, inverse, gain[...])


def last(rows, own_g, peer_g, grad_hidden, gain):
    n, d = rows.shape
    part = pl.BlockSpec((256, d), lambda i: (i, 0))
    return pl.pallas_call(
        last_kernel,
        grid=(n // 256,),
        in_specs=[part] * 4 + [full((1, d))],
        out_specs=part,
        out_shape=shape((n, d), F32),
        compiler_params=params(),
        name="last",
    )(rows, own_g, peer_g, grad_hidden, gain)


def swap(x, axis, apart):
    count = lax.axis_size(axis)
    return lax.ppermute(x, axis, [(i, i ^ apart) for i in range(count)])


def whole_call(kernel, place, inputs, outputs, name):
    return pl.pallas_call(
        kernel,
        grid=(1,),
        in_specs=[pl.BlockSpec(memory_space=pltpu.SMEM)] + [full(x.shape) for x in inputs],
        out_specs=[full(dims) for dims, _ in outputs],
        out_shape=[shape(dims, kind) for dims, kind in outputs],
        compiler_params=params(),
        cost_estimate=LIGHT,
        name=name,
    )(place, *inputs)


def added(refs, at=slice(None)):
    total = refs[0][at, :].astype(F32)
    for ref in refs[1:]:
        total = total + ref[at, :].astype(F32)
    return total


def cut(index, count):
    return pl.ds(pl.multiple_of(index * count, count), count)


class Sum:
    def __init__(self, place, rows, width):
        self.place, self.rows, self.width = place, rows, width
        self.third, self.twelfth = rows // 3, rows // 12

    def call(self, kernel, inputs, outputs, name):
        dims = [((count, self.width), kind) for count, kind in outputs]
        return whole_call(kernel, self.place, inputs, dims, name)

    def start(self, keep, got):
        third, twelfth = self.third, self.twelfth

        def kernel(place, keep, got, m1, s1, m2, *s2):
            side, line = place[4], place[5]
            m1[...] = added((keep, got), cut(side, third))
            s1[...] = added((keep, got), cut(1 - side, third)).astype(BF16)

            def quarter(k):
                at = pl.multiple_of(2 * third + (line ^ k) * twelfth, twelfth)
                return added((keep, got), pl.ds(at, twelfth))

            m2[...] = quarter(0)
            for k in (1, 2, 3):
                s2[k - 1][...] = quarter(k).astype(BF16)

        return self.call(
            kernel,
            (keep, got),
            [(third, F32), (third, BF16), (twelfth, F32)] + [(twelfth, BF16)] * 3,
            "start_sum",
        )

    def send1(self, state):
        m1, s1, m2, *s2 = state
        got = swap(s1, "seq", 2)
        return (m1, m2, got) + tuple(swap(x, "seq", 4 * k) for k, x in zip((1, 2, 3), s2))

    def middle(self, state):
        twelfth = self.twelfth

        def kernel(place, m1, m2, g1, ga, gb, gc, n1, n2, s2, *s1):
            side, line = place[4], place[5]
            n1[...] = added((m1, g1), cut(line, twelfth))
            for k in (1, 2, 3):
                s1[k - 1][...] = added((m1, g1), cut(line ^ k, twelfth)).astype(BF16)
            n2[...] = added((m2, ga, gb, gc), cut(side, twelfth // 2))
            s2[...] = added((m2, ga, gb, gc), cut(1 - side, twelfth // 2)).astype(BF16)

        return self.call(
            kernel,
            state,
            [(twelfth, F32), (twelfth // 2, F32), (twelfth // 2, BF16)] + [(twelfth, BF16)] * 3,
            "middle_sum",
        )

    def send2(self, state):
        n1, n2, s2, *s1 = state
        got = tuple(swap(x, "seq", 4 * k) for k, x in zip((1, 2, 3), s1))
        return (n1, n2) + got + (swap(s2, "seq", 2),)

    def end(self, state):
        twelfth = self.twelfth

        def kernel(place, n1, n2, ga, gb, gc, g2, one, two):
            one[...] = added((n1, ga, gb, gc)).astype(BF16)
            two[...] = added((n2, g2)).astype(BF16)

        pair = self.call(kernel, state, [(twelfth, BF16), (twelfth // 2, BF16)], "end_sum")
        return tuple(self.beyond(x) for x in pair)

    def beyond(self, low):
        apart = FOLD
        while apart < lax.axis_size("seq"):
            low = (low.astype(F32) + swap(low, "seq", apart).astype(F32)).astype(BF16)
            apart *= 2
        return low

    def send3(self, pair):
        one, two = pair
        got = tuple(swap(one, "seq", 4 * k) for k in (1, 2, 3))
        return (one, two) + got + (swap(two, "seq", 2),)

    def join(self, state):
        twelfth, third = self.twelfth, self.third

        def kernel(place, one, two, ga, gb, gc, g2, out1, out2):
            side, line = place[4], place[5]
            for k, ref in enumerate((one, ga, gb, gc)):
                out1[cut(line ^ k, twelfth), :] = ref[...]
            out2[cut(side, twelfth // 2), :] = two[...]
            out2[cut(1 - side, twelfth // 2), :] = g2[...]

        return self.call(kernel, state, [(third, BF16), (twelfth, BF16)], "join_sum")

    def send4(self, pair):
        one, two = pair
        got = swap(one, "seq", 2)
        return (one, two, got) + tuple(swap(two, "seq", 4 * k) for k in (1, 2, 3))

    def whole(self, state):
        twelfth, third = self.twelfth, self.third

        def kernel(place, one, two, g1, ga, gb, gc, out):
            side, line = place[4], place[5]
            out[cut(side, third), :] = one[...]
            out[cut(1 - side, third), :] = g1[...]
            for k, ref in enumerate((two, ga, gb, gc)):
                at = pl.multiple_of(2 * third + (line ^ k) * twelfth, twelfth)
                out[pl.ds(at, twelfth), :] = ref[...]

        return self.call(kernel, state, [(self.rows, BF16)], "whole_sum")[0]


def send_home(place, kept, r_core):
    heads, rows, lanes = kept.shape
    quarter = rows // 3
    half = r_core.shape[1] - rows

    def kernel(place, kept, r_core, far, near, stay):
        def both(k):
            return kept[:, cut(k, quarter), :] + r_core[
                :, pl.ds(half + k * quarter, quarter), :
            ].astype(F32)

        near[...] = both(0).astype(BF16)
        stay[...] = both(1)
        far[...] = both(2).astype(BF16)

    dims = (heads, quarter, lanes)
    return whole_call(
        kernel, place, (kept, r_core), [(dims, BF16), (dims, BF16), (dims, F32)], "send_home"
    )


def send_line(place, stay, got):
    heads, rows, lanes = stay.shape

    def kernel(place, stay, got, z1, z2, z3):
        def both(start, count):
            at = pl.ds(start, count)
            return (stay[:, at, :] + got[:, at, :].astype(F32)).astype(BF16)

        z1[...] = both(0, rows // 2)
        z2[...] = both(rows // 2, rows // 4)
        z3[...] = both(3 * rows // 4, rows // 4)

    return whole_call(
        kernel,
        place,
        (stay, got),
        [((heads, count, lanes), BF16) for count in (rows // 2, rows // 4, rows // 4)],
        "send_line",
    )


def tie(*xs):
    return lax.optimization_barrier(xs)


def sum_small(x, apart):
    while apart < lax.axis_size("seq"):
        x = x + swap(x, "seq", apart)
        apart *= 2
    return x


def local(
    rows,
    lengths,
    norm_gains,
    norm_shifts,
    qkv_weight,
    qv_bias,
    out_weight,
    out_bias,
    up_weight,
    up_bias,
    down_weight,
    down_bias,
    out_cot,
):
    n, d = rows.shape
    width = qkv_weight.shape[2]
    heads = width // HD
    seq_place = lax.axis_index("seq")
    head_place = lax.axis_index("head")
    slide_rows = min(FOLD * SEG, n * lax.axis_size("seq"))
    start = seq_place * n
    slide = start // slide_rows
    length = jnp.sum(jnp.where(jnp.arange(lengths.shape[0]) == slide, lengths, 0))
    limit = jnp.clip(length - start % slide_rows, 0, n)
    place = jnp.stack(
        [
            head_place * heads,
            limit,
            head_place,
            seq_place % 2,
            seq_place // 2 % 2,
            seq_place // 4 % 4,
        ]
    ).astype(jnp.int32)
    half, quarter, eighth = n // 2, n // 4, n // 8
    first_heads = heads // 2

    peer_out_weight = swap(out_weight, "head", 1)
    wide_out = jnp.pad(
        out_weight.reshape(heads, HD, d), ((0, 0), (HD, LANES - 2 * HD), (0, 0))
    ).reshape(heads * LANES, d)

    q, kv, s1, sx, sz1, sz, normed1, wide = project(
        place, rows, norm_gains[:1], norm_shifts[:1], qkv_weight, qv_bias
    )
    rz1 = swap(sz1, "seq", 4)
    rx = swap(sx, "seq", 2)
    rz2 = swap(sz, "seq", 8)
    rz3 = swap(sz, "seq", 12)
    cs1 = swap(s1, "seq", 1)
    own = own_attention(q, kv, 0, first_heads)
    own, rz1, rx, rz2, rz3, cs1 = tie(own, rz1, rx, rz2, rz3, cs1)
    zc = jnp.concatenate([rz1, rz2, rz3], 1)
    rx2 = swap(zc, "seq", 2)
    crx = swap(rx, "seq", 1)
    czc = swap(zc, "seq", 1)
    own = own_attention(q, kv, first_heads, heads - first_heads, own)
    own, rx2, crx, czc, peer_out_weight = tie(own, rx2, crx, czc, peer_out_weight)
    crx2 = swap(rx2, "seq", 1)
    merged, kv_all, qb, merged_low = peers_attention(
        place, q, own, (cs1, rx, crx, zc, rx2, czc, crx2)
    )
    peer_low = swap(merged_low, "head", 1)

    def feed_rows(start, into):
        return feed(
            place,
            rows,
            out_cot,
            merged_low,
            peer_low,
            out_weight,
            peer_out_weight,
            out_bias[None],
            norm_gains[1:],
            norm_shifts[1:],
            up_weight,
            up_bias[None],
            down_weight,
            start,
            half,
            into,
        )

    *fed, g2_one, ub_one = feed_rows(0, None)
    peer_one = swap(g2_one, "head", 1)
    *fed, g2_two, ub_two = feed_rows(half, fed)
    *fed, peer_one = tie(*fed, peer_one)
    hidden, normed2, act, grad_pre = fed
    up_bias_grad = ub_one + ub_two
    peer_two = swap(g2_two, "head", 1)
    mlp, keep, send = weights(place, act, grad_pre, normed2, out_cot, down_weight)
    peer_two, mlp, keep, send = tie(peer_two, mlp, keep, send)

    ff = up_bias.shape[0]
    sums = Sum(place, ff, d)
    got = swap(send, "seq", 1)
    *turned, sums2_one = turn(
        out_cot, g2_one, peer_one, hidden, norm_gains[1:], wide_out, 0, half
    )
    grad_hidden, grad_low, gm, sums2_two = turn(
        out_cot, g2_two, peer_two, hidden, norm_gains[1:], wide_out, half, half, turned
    )
    sums2 = sums2_one + sums2_two
    gm, keep, got = tie(gm, keep, got)
    ff_state = sums.send1(sums.start(keep, got))
    peer_mlp = swap(mlp, "head", 1)
    do, dq_peer, to_core, kept = peers_back(place, gm, merged, qb, kv_all)
    do, dq_peer, to_core, kept, *ff_state = tie(do, dq_peer, to_core, kept, *ff_state)
    r_core = swap(to_core, "seq", 1)
    ff_state = sums.send2(sums.middle(ff_state))
    back = own_back(qb, do, kv, 0, first_heads)
    dq_own, dkv_own, r_core, *ff_state = tie(*back, r_core, *ff_state)
    far, near, stay = send_home(place, kept, r_core)
    r_x2 = swap(far, "seq", 2)
    r_x = swap(near, "seq", 2)
    ff_state = sums.send3(sums.end(ff_state))
    back = own_back(qb, do, kv, first_heads, heads - first_heads, (dq_own, dkv_own))
    dq_own, dkv_own, r_x2, *ff_state = tie(*back, r_x2, *ff_state)
    z1, z2, z3 = send_line(place, stay, r_x2)
    r_z1 = swap(z1, "seq", 4)
    r_z2 = swap(z2, "seq", 8)
    r_z3 = swap(z3, "seq", 12)
    start_g, grad_one, grad_bq = finish_q(
        place, dq_own, dq_peer, normed1, wide, merged_low, grad_low
    )
    start_g, grad_one, peer_mlp, r_x, r_z1, r_z2, r_z3, *ff_state = tie(
        start_g, grad_one, peer_mlp, r_x, r_z1, r_z2, r_z3, *ff_state
    )
    out_rows = (
        hidden + ((mlp.astype(F32) + peer_mlp.astype(F32)) + down_bias)
    ).astype(BF16)
    ff_state = sums.send4(sums.join(ff_state))
    grad_normed1, grad_two, grad_bkv, sums1 = finish_kv(
        place, dkv_own, (r_core, r_x, r_z1, r_z2, r_z3), normed1, rows, wide, start_g
    )
    grad_normed1, grad_two, sums1, out_rows, *ff_state = tie(
        grad_normed1, grad_two, sums1, out_rows, *ff_state
    )

    peer_normed1 = swap(grad_normed1, "head", 1)
    ff_own = sums.whole(ff_state)
    ff_peer = swap(ff_own, "seq", 1)
    first = seq_place % 2 == 0
    count = 2 * width
    grad_one, grad_two = grad_one.reshape(count, d), grad_two.reshape(count, d)
    got = swap(jnp.where(first, grad_two, grad_one).astype(BF16), "seq", 1)
    keep = jnp.where(first, grad_one, grad_two)
    up_rows = ff // d
    qv_bias_grad = jnp.concatenate(
        [grad_bq[:, 0, :HD].reshape(1, width), grad_bkv[:, 0, HD : 2 * HD].reshape(1, width)], 1
    )
    small = jnp.concatenate([sums1[:2], sums2[:4], up_bias_grad.reshape(-1, d), qv_bias_grad], 0)
    keep, got, ff_own, ff_peer, small = tie(keep, got, ff_own, ff_peer, small)
    w_sums = Sum(place, count, d)
    state = w_sums.send1(w_sums.start(keep, got))
    small = small + swap(small, "seq", 1)
    down_weight_grad, up_weight_grad = spread(place, ff_own, ff_peer)
    *state, small, down_weight_grad = tie(*state, small, down_weight_grad)
    state = w_sums.send2(w_sums.middle(state))
    small = small + swap(small, "seq", 2)
    *state, small, peer_normed1 = tie(*state, small, peer_normed1)
    state = w_sums.send3(w_sums.end(state))
    small = small + swap(small, "seq", 4)
    rows_grad = last(rows, grad_normed1, peer_normed1, grad_hidden, norm_gains[:1])
    *state, small, rows_grad = tie(*state, small, rows_grad)
    state = w_sums.send4(w_sums.join(state))
    small = sum_small(small, 8)
    *state, small = tie(*state, small)
    w_own = w_sums.whole(state)
    w_peer = swap(w_own, "seq", 1)
    small = jnp.concatenate([small[:2] + swap(small[:2], "head", 1), small[2:]], 0)
    qkv_grad, out_weight_grad = spread_qkv(place, w_own, w_peer)
    return (
        out_rows,
        rows_grad,
        jnp.stack([small[0], small[2]]),
        jnp.stack([small[1], small[3]]),
        qkv_grad,
        small[6 + up_rows].reshape(2, width),
        out_weight_grad,
        small[4],
        up_weight_grad,
        small[6 : 6 + up_rows].reshape(-1),
        down_weight_grad,
        small[5],
    )


def solution(mesh):
    placed = (
        P("seq", None),
        P(),
        P(),
        P(),
        P(None, None, "head"),
        P(None, "head"),
        P("head", None),
        P(),
        P(None, "head"),
        P("head"),
        P("head", None),
        P(),
        P("seq", None),
    )
    return jax.shard_map(
        local,
        mesh=mesh,
        in_specs=placed,
        out_specs=(
            P("seq", None),
            P("seq", None),
            P(),
            P(),
            P(None, None, "head"),
            P(None, "head"),
            P("head", None),
            P(),
            P(None, "head"),
            P("head"),
            P("head", None),
            P(),
        ),
        check_vma=False,
    )
```

```python
import functools
import math

import jax
import jax.numpy as jnp
import numpy as np
from jax import lax
from jax.experimental import pallas as pl
from jax.experimental.pallas import tpu as pltpu
from jax.sharding import PartitionSpec as P

HD = 48
SEG = 1024
LANES = 128
LEVELS = 5
FOLD = 16

EPS = 1e-05
ROOT = math.sqrt(HD)
EXP_SCALE = math.log2(math.e) / ROOT
ROOT_HALF = 1.0 / math.sqrt(2.0)
DENSITY_NORM = 1.0 / math.sqrt(2.0 * math.pi)
ABSENT = -1e20

ONE = 96
MASK = 99
MULT = 100
TOP = 127

ORDER = (0, 8, 4, 12, 2, 6, 10, 14, 1, 3, 5, 7, 9, 11, 13, 15)
CLASS = (4, 3, 2, 2, 1, 1, 1, 1, 0, 0, 0, 0, 0, 0, 0, 0)

F32 = jnp.float32
BF16 = jnp.bfloat16


LIGHT = pl.CostEstimate(flops=0, bytes_accessed=0, transcendentals=0)


def params(mib=48):
    return pltpu.CompilerParams(vmem_limit_bytes=mib * 2**20)


def dot(left, right):
    return jnp.dot(left, right, preferred_element_type=F32)


def dot_rt(left, right):
    return lax.dot_general(left, right, (((1,), (1,)), ((), ())), preferred_element_type=F32)


def dot_lt(left, right):
    return lax.dot_general(left, right, (((0,), (0,)), ((), ())), preferred_element_type=F32)


def full(shape):
    return pl.BlockSpec(shape, lambda *_: (0,) * len(shape))


def once(shape):
    return pl.BlockSpec(shape, lambda *_: (0,) * len(shape), pipeline_mode=pl.Buffered(1))


def per_head(rows, lanes=LANES):
    return pl.BlockSpec((1, rows, lanes), lambda h: (h, 0, 0))


def shape(dims, kind):
    return jax.ShapeDtypeStruct(dims, kind)


def stored(dims, kind):
    return pltpu.HBM(dims, kind)


def far(x):
    return pltpu.with_memory_space_constraint(x, pltpu.HBM)


def split3(x):
    high = x.astype(BF16).astype(F32)
    rest = x - high
    middle = rest.astype(BF16).astype(F32)
    return high, middle, rest - middle


def with_terms(block, lane, terms):
    high, middle, low = split3(terms)
    block = jnp.where(lane == ONE, high, block)
    block = jnp.where(lane == ONE + 1, middle, block)
    return jnp.where(lane == ONE + 2, low, block)


def unit_rows(x):
    mean = jnp.mean(x, -1, keepdims=True)
    centred = x - mean
    inverse = lax.rsqrt(jnp.mean(centred * centred, -1, keepdims=True) + EPS)
    return centred * inverse, inverse


def norm_back(gradient, unit, inverse, gain):
    z = gradient * gain
    return inverse * (
        z - jnp.mean(z, -1, keepdims=True) - unit * jnp.mean(z * unit, -1, keepdims=True)
    )


def mult_table(level, blocks):
    table = np.zeros((len(blocks), LANES), np.float32)
    for row, key_class in enumerate(blocks):
        for j in range(level + 1, key_class + 1):
            value = np.float32(ROOT * math.log((j - level + 1) / (j - level)))
            high = np.float32(value.astype(jnp.bfloat16))
            table[row, MULT + j - 1] = high
            table[row, MULT + 4 + j - 1] = np.float32((value - high).astype(jnp.bfloat16))
    return table


def flag_table():
    table = np.zeros((FOLD, LANES), np.float32)
    for row, level in enumerate(CLASS):
        table[row, MULT : MULT + level] = 1.0
        table[row, MULT + 4 : MULT + 4 + level] = 1.0
    return table


def project_kernel(
    place, rows, gain, shift, w, bias, flags, table, one, two, three, four,
    q, kv, s1, sx, sz1, sz, normed, wide, w_tmp, b_tmp, q_tmp, kv_tmp, extra,
):
    h = pl.program_id(0)
    n, d = rows.shape
    heads = w.shape[2] // HD
    block = n // FOLD

    @pl.when(h == 0)
    def _():
        unit, _ = unit_rows(rows[...].astype(F32))
        normed[...] = (unit * gain[...] + shift[...]).astype(BF16)
        lane = lax.broadcasted_iota(jnp.int32, (n, LANES), 1)
        here = lax.broadcasted_iota(jnp.int32, (n, LANES), 0) < place[1]
        extra[:, :LANES] = jnp.where(here & (lane == MASK), 1.0, 0.0)
        extra[:, LANES:] = jnp.where(here | (lane != MASK), 0.0, ABSENT)

    for k in range(heads):

        @pl.when(h == k)
        def _():
            cut = slice(k * HD, (k + 1) * HD)
            w_tmp[:, :LANES] = jnp.concatenate(
                [w[0, :, cut], jnp.zeros((d, LANES - HD), BF16)], axis=1
            )
            w_tmp[:, LANES:] = jnp.concatenate(
                [w[1, :, cut], w[2, :, cut], jnp.zeros((d, LANES - 2 * HD), BF16)], axis=1
            )
            b_tmp[:, :LANES] = jnp.concatenate(
                [bias[0:1, cut], jnp.zeros((1, LANES - HD), F32)], axis=1
            )
            b_tmp[:, LANES:] = jnp.concatenate(
                [
                    jnp.zeros((1, HD), F32),
                    bias[1:2, cut],
                    jnp.ones((1, 3), F32),
                    jnp.zeros((1, LANES - 2 * HD - 3), F32),
                ],
                axis=1,
            )

    wide[0] = w_tmp[...]
    product = dot(normed[...], w_tmp[...]) + b_tmp[...] + extra[...]
    q_tmp[...] = product[:, :LANES]
    kv_tmp[...] = product[:, LANES:]
    head = place[0] + h
    for p in range(FOLD):
        c = (head + ORDER[p]) % FOLD
        at = pl.ds(p * block, block)
        row = slice(p, p + 1)
        q[0, at, :] = (q_tmp[pl.ds(c, block, stride=FOLD), :] + flags[row, :]).astype(BF16)
        kv_rows = kv_tmp[pl.ds(c, block, stride=FOLD), :]
        kv[0, at, :] = (kv_rows + table[row, :]).astype(BF16)
        for out, lanes in ((s1, one), (sx, two), (sz1, three), (sz, four)):
            if (p + 1) * block <= out.shape[1]:
                out[0, at, :] = (kv_rows + lanes[row, :]).astype(BF16)


def project(place, rows, gain, shift, w, bias):
    n, d = rows.shape
    heads = w.shape[2] // HD
    tables = [jnp.asarray(flag_table())]
    tables += [jnp.asarray(mult_table(level, CLASS)) for level in range(LEVELS)]
    sizes = (n, n, n // 2, n // 4, n // 8, n // 16)
    return pl.pallas_call(
        project_kernel,
        grid=(heads,),
        in_specs=[
            pl.BlockSpec(memory_space=pltpu.SMEM),
            once(rows.shape),
            once(gain.shape),
            once(shift.shape),
            once(w.shape),
            once(bias.shape),
        ]
        + [once(t.shape) for t in tables],
        out_specs=[per_head(m) for m in sizes]
        + [full((n, d)), pl.BlockSpec((1, d, 2 * LANES), lambda h: (h, 0, 0))],
        out_shape=[stored((heads, m, LANES), BF16) for m in sizes[:2]]
        + [shape((heads, m, LANES), BF16) for m in sizes[2:]]
        + [stored((n, d), BF16), stored((heads, d, 2 * LANES), BF16)],
        scratch_shapes=[
            pltpu.VMEM((d, 2 * LANES), BF16),
            pltpu.VMEM((1, 2 * LANES), F32),
            pltpu.VMEM((n, LANES), F32),
            pltpu.VMEM((n, LANES), F32),
            pltpu.VMEM((n, 2 * LANES), F32),
        ],
        compiler_params=params(24),
        cost_estimate=pl.CostEstimate(
            flops=2 * n * d * heads * 256, bytes_accessed=14 * 2**20, transcendentals=0
        ),
        name="project",
    )(place, *(far(x) for x in (rows, gain, shift, w, bias, *tables)))


def own_kernel(q, kv, out, *, block):
    n = q.shape[1]
    keys = kv[0]
    lane = lax.broadcasted_iota(jnp.int32, (block, LANES), 1)

    def scores(i):
        return dot_rt(q[0, pl.ds(i * block, block), :], keys)

    now = scores(0)
    for i in range(n // block):
        later = scores(i + 1) if (i + 1) * block < n else None
        top = jnp.max(now, -1, keepdims=True)
        weights = jnp.exp2((now - top) * EXP_SCALE).astype(BF16)
        out[0, pl.ds(i * block, block), :] = jnp.where(lane == TOP, top, dot(weights, keys))
        now = later


def group_spec(rows, start, lanes=LANES):
    return pl.BlockSpec((1, rows, lanes), lambda h: (h + start, 0, 0))


ANYWHERE = pl.BlockSpec(memory_space=pl.ANY)


def own_attention(q, kv, start, count, into=None):
    heads, n, _ = q.shape
    spec = group_spec(n, start)
    kernel = functools.partial(own_kernel, block=256)
    extra = () if into is None else (into,)
    return pl.pallas_call(
        kernel if into is None else lambda q, kv, _, out: kernel(q, kv, out),
        grid=(count,),
        in_specs=[spec] * 2 + [ANYWHERE] * len(extra),
        out_specs=spec,
        out_shape=shape((heads, n, LANES), F32),
        input_output_aliases={2: 0} if extra else {},
        compiler_params=params(12),
        cost_estimate=pl.CostEstimate(
            flops=count * n * n * 1024, bytes_accessed=4 * 2**20, transcendentals=count * n * n
        ),
        name="own_attention",
    )(far(q), far(kv), *extra)


def peers_kernel(
    place, q, own, cs1, rx, crx, zc, rx2, czc, crx2, pick, merged, kv_all, qb, low, nat, wide, *, start
):
    h = pl.program_id(0)
    n = q.shape[1]
    block = n // FOLD
    at = 0
    near = (zc, rx2, czc, crx2)
    pieces = [(cs1, 0, n // 2), (rx, 0, n // 4), (crx, 0, n // 4)]
    pieces += [(r, 0, n // 8) for r in near] + [(r, n // 8, n // 8) for r in near]
    for ref, begin, count in pieces:
        kv_all[0, pl.ds(at, count), :] = ref[0, pl.ds(begin, count), :]
        at += count

    head = place[0] + h + start
    chunks = [
        (0, n // 16, 2 * n),
        (n // 16, n // 16, 3 * n // 2),
        (n // 8, n // 8, n),
        (n // 4, n // 4, n // 2),
        (n // 2, n // 2, 0),
    ]
    scores = []
    for begin, count, keys in chunks:
        if keys:
            scores.append(dot_rt(q[0, pl.ds(begin, count), :], kv_all[0, pl.ds(0, keys), :]))
        else:
            scores.append(None)
    for (begin, count, keys), s in zip(chunks, scores):
        rows = pl.ds(begin, count)
        lane = lax.broadcasted_iota(jnp.int32, (count, LANES), 1)
        o = own[0, rows, :]
        top = o[:, TOP : TOP + 1]
        if keys:
            new = jnp.maximum(top, jnp.max(s, -1, keepdims=True))
            weights = jnp.exp2((s - new) * EXP_SCALE).astype(BF16)
            o = o * jnp.exp2((top - new) * EXP_SCALE) + dot(weights, kv_all[0, pl.ds(0, keys), :])
            top = new
        total = o[:, ONE : ONE + 1]
        o = jnp.where((lane >= HD) & (lane < 2 * HD), o / total, 0.0)
        merged[0, rows, :] = o
        lse = top + jnp.log2(total) * (1.0 / EXP_SCALE)
        qb[0, rows, :] = with_terms(q[0, rows, :].astype(F32), lane, -lse).astype(BF16)
        for p in range(begin // block, (begin + count) // block):
            c = (head + ORDER[p]) % FOLD
            off = p * block - begin
            nat[pl.ds(c, block, stride=FOLD), :] = o[off : off + block]
    wide[:, pl.ds(pl.multiple_of(h * LANES, LANES), LANES)] = nat[...].astype(BF16)

    @pl.when(h == pl.num_programs(0) - 1)
    def _():
        low[...] = dot_rt(pick[...], wide[...]).astype(BF16)


def pick_values(heads):
    m = np.zeros((heads * HD, heads * LANES), np.float32)
    for h in range(heads):
        for j in range(HD):
            m[h * HD + j, h * LANES + HD + j] = 1.0
    return m


def peers_attention(place, q, own, received, start, count, into=None):
    heads, n, _ = q.shape
    pick = jnp.asarray(pick_values(count), BF16)
    extra = () if into is None else tuple(into)
    inputs = 4 + len(received)

    def kernel(*refs):
        peers_kernel(*refs[:inputs], *refs[inputs + len(extra) :], start=start)

    return pl.pallas_call(
        kernel,
        grid=(count,),
        in_specs=[
            pl.BlockSpec(memory_space=pltpu.SMEM),
            group_spec(n, start),
            group_spec(n, start),
        ]
        + [group_spec(r.shape[1], start) for r in received]
        + [once(pick.shape)]
        + [ANYWHERE] * len(extra),
        out_specs=[group_spec(n, start), group_spec(2 * n, start), group_spec(n, start)]
        + [full((count * HD, n))],
        out_shape=[
            stored((heads, n, LANES), F32),
            stored((heads, 2 * n, LANES), BF16),
            stored((heads, n, LANES), BF16),
            shape((count * HD, n), BF16),
        ],
        input_output_aliases={inputs + k: k for k in range(len(extra))},
        scratch_shapes=[pltpu.VMEM((n, LANES), F32), pltpu.VMEM((n, count * LANES), BF16)],
        compiler_params=params(20),
        cost_estimate=pl.CostEstimate(
            flops=count * n * n * 512, bytes_accessed=12 * 2**20, transcendentals=count * n * n // 2
        ),
        name="peers_attention",
    )(place, far(q), own, *received, pick, *extra)


def feed_kernel(
    place, rows, cot, own_c, own_d, peer_c, peer_d, own_w, peer_w, out_b, gain, shift, up_w, up_b, down_w,
    hidden, normed, act, grad_pre, grad_normed, up_b_grad, w_tmp, c_tmp,
):
    i = pl.program_id(0)
    half = own_w.shape[0]
    group = own_c.shape[0]
    first = place[2] == 0

    @pl.when(i == 0)
    def _():
        w_tmp[:half] = jnp.where(first, own_w[...], peer_w[...])
        w_tmp[half:] = jnp.where(first, peer_w[...], own_w[...])

    c_tmp[:group] = jnp.where(first, own_c[...], peer_c[...])
    c_tmp[group:half] = jnp.where(first, own_d[...], peer_d[...])
    c_tmp[half : half + group] = jnp.where(first, peer_c[...], own_c[...])
    c_tmp[half + group :] = jnp.where(first, peer_d[...], own_d[...])
    attended = dot_lt(c_tmp[...], w_tmp[...])
    hid = rows[...].astype(F32) + (attended + out_b[...])
    hidden[...] = hid
    unit, _ = unit_rows(hid)
    low = (unit * gain[...] + shift[...]).astype(BF16)
    normed[...] = low
    pre = dot(low, up_w[...]) + up_b[...]
    phi = 0.5 * (1.0 + lax.erf(pre * ROOT_HALF))
    act[...] = (pre * phi).astype(BF16)
    slope = phi + pre * jnp.exp(-0.5 * pre * pre) * DENSITY_NORM
    gradient = dot_rt(cot[...], down_w[...]) * slope
    total = jnp.sum(gradient, 0, keepdims=True)

    @pl.when(i == 0)
    def _():
        up_b_grad[...] = total

    @pl.when(i > 0)
    def _():
        up_b_grad[...] += total

    gradient = gradient.astype(BF16)
    grad_pre[...] = gradient
    grad_normed[...] = dot_rt(gradient, up_w[...]).astype(BF16)


def feed(
    place, rows, cot, merged, own_w, peer_w, out_b, gain, shift, up_w, up_b, down_w, start, count, into=None
):
    n, d = rows.shape
    block = 256
    ff = up_w.shape[1]
    half = own_w.shape[0]
    first = start // block
    extra = () if into is None else tuple(into)

    def part(lanes):
        return pl.BlockSpec((block, lanes), lambda i: (i + first, 0))

    def kernel(*refs):
        feed_kernel(*refs[:15], *refs[15 + len(extra) :])

    return pl.pallas_call(
        kernel,
        grid=(count // block,),
        in_specs=[
            pl.BlockSpec(memory_space=pltpu.SMEM),
            part(d),
            part(d),
        ]
        + [pl.BlockSpec((m.shape[0], block), lambda i: (0, i + first)) for m in merged]
        + [
            once(own_w.shape),
            once(peer_w.shape),
            once((1, d)),
            once((1, d)),
            once((1, d)),
            once(up_w.shape),
            once((1, ff)),
            once(down_w.shape),
        ]
        + [ANYWHERE] * len(extra),
        out_specs=[
            part(d),
            part(d),
            part(ff),
            part(ff),
            pl.BlockSpec((block, d), lambda i: (i, 0)),
            full((1, ff)),
        ],
        out_shape=[
            shape((n, d), F32),
            shape((n, d), BF16),
            shape((n, ff), BF16),
            shape((n, ff), BF16),
            shape((count, d), BF16),
            shape((1, ff), F32),
        ],
        input_output_aliases={15 + k: k for k in range(len(extra))},
        scratch_shapes=[pltpu.VMEM((2 * half, d), BF16), pltpu.VMEM((2 * half, block), BF16)],
        compiler_params=params(30),
        cost_estimate=pl.CostEstimate(
            flops=2 * count * d * (ff * 3 + d),
            bytes_accessed=12 * 2**20,
            transcendentals=2 * count * ff,
        ),
        name="feed_forward",
    )(
        place, rows, cot, *merged, own_w, peer_w, out_b, gain, shift, up_w, up_b, down_w, *extra
    )


def weights_kernel(place, act, grad_pre, normed, cot, down_w, mlp, keep, send, acc):
    i = pl.program_id(0)
    part = dot(act[...], down_w[...])

    @pl.when(i == 0)
    def _():
        acc[...] = part

    @pl.when(i > 0)
    def _():
        acc[...] += part

    down = dot_lt(act[...], cot[...])
    up = dot_lt(grad_pre[...], normed[...])
    first = place[3] == 0
    keep[...] = jnp.where(first, down, up).astype(BF16)
    send[...] = jnp.where(first, up, down).astype(BF16)

    @pl.when(i == pl.num_programs(0) - 1)
    def _():
        mlp[...] = acc[...].astype(BF16)


def weights(place, act, grad_pre, normed, cot, down_w):
    n, ff = act.shape
    d = cot.shape[1]
    block = 256
    lanes = pl.BlockSpec((n, block), lambda i: (0, i))
    rows = pl.BlockSpec((block, d), lambda i: (i, 0))
    return pl.pallas_call(
        weights_kernel,
        grid=(ff // block,),
        in_specs=[
            pl.BlockSpec(memory_space=pltpu.SMEM),
            lanes,
            lanes,
            once((n, d)),
            once((n, d)),
            rows,
        ],
        out_specs=[full((n, d)), rows, rows],
        out_shape=[shape((n, d), BF16), shape((ff, d), BF16), shape((ff, d), BF16)],
        scratch_shapes=[pltpu.VMEM((n, d), F32)],
        compiler_params=params(26),
        cost_estimate=pl.CostEstimate(
            flops=6 * n * d * ff, bytes_accessed=20 * 2**20, transcendentals=0
        ),
        name="weights",
    )(place, act, grad_pre, normed, cot, down_w)


def turn_kernel(cot, own_g, peer_g, hidden, gain, out_w, grad_hidden, low_out, gm, sums):
    i = pl.program_id(0)
    unit, inverse = unit_rows(hidden[...])
    gradient = own_g[...].astype(F32) + peer_g[...].astype(F32)
    outer = cot[...].astype(F32)
    total = outer + norm_back(gradient, unit, inverse, gain[...])
    grad_hidden[...] = total
    low = total.astype(BF16)
    low_out[...] = low
    gm[...] = dot_rt(low, out_w[...]).astype(BF16).astype(F32)

    @pl.when(i == 0)
    def _():
        sums[...] = jnp.zeros_like(sums)

    sums[0:1, :] += jnp.sum(gradient * unit, 0, keepdims=True)
    sums[1:2, :] += jnp.sum(gradient, 0, keepdims=True)
    sums[2:3, :] += jnp.sum(total, 0, keepdims=True)
    sums[3:4, :] += jnp.sum(outer, 0, keepdims=True)


def turn(cot, own_g, peer_g, hidden, gain, out_w, start, count, into=None):
    n, d = cot.shape
    block = 256
    first = start // block
    wide = out_w.shape[0]
    extra = () if into is None else tuple(into)

    def part(lanes):
        return pl.BlockSpec((block, lanes), lambda i: (i + first, 0))

    own_part = pl.BlockSpec((block, d), lambda i: (i, 0))

    def kernel(*refs):
        turn_kernel(*refs[:6], *refs[6 + len(extra) :])

    return pl.pallas_call(
        kernel,
        grid=(count // block,),
        in_specs=[part(d), own_part, own_part, part(d), once((1, d)), once((wide, d))]
        + [ANYWHERE] * len(extra),
        out_specs=[part(d), part(d), part(wide), full((8, d))],
        out_shape=[
            stored((n, d), F32),
            stored((n, d), BF16),
            stored((n, wide), F32),
            shape((8, d), F32),
        ],
        input_output_aliases={6 + k: k for k in range(len(extra))},
        compiler_params=params(16),
        cost_estimate=LIGHT,
        name="turn",
    )(cot, own_g, peer_g, hidden, gain, out_w, *extra)


def pair_back(keys, q, do):
    weights = jnp.exp2(dot_rt(keys, q) * EXP_SCALE)
    inner = (weights * dot_rt(keys, do)).astype(BF16)
    grad_keys = dot(weights.astype(BF16), do) + dot(inner, q)
    return grad_keys, dot(keys.T, inner)


def peers_back_kernel(place, gm, merged, q, kv_all, do, dq, to_core, kept, acc):
    half = q.shape[1]
    n = 2 * half
    block = n // FOLD
    lane = lax.broadcasted_iota(jnp.int32, (block, LANES), 1)
    head = place[0] + pl.program_id(0)
    for p in range(FOLD):
        c = (head + ORDER[p]) % FOLD
        at = pl.ds(p * block, block)
        gradient = gm[pl.ds(c, block, stride=FOLD), :]
        delta = jnp.sum(gradient * merged[0, at, :], -1, keepdims=True)
        do[0, at, :] = with_terms(gradient, lane, -delta).astype(BF16)
    for level in (1, 2, 3, 4):
        count = n >> level
        start = (level - 1) * half
        for k in range(0, half, 256):
            grad, grad_q = pair_back(
                kv_all[0, pl.ds(start + k, 256), :], q[0, pl.ds(0, count), :], do[0, pl.ds(0, count), :]
            )
            if level == 1:
                to_core[0, pl.ds(k, 256), :] = grad.astype(BF16)
            elif level == 2:
                if k == 0:
                    kept[0, pl.ds(0, 256), :] = grad
                else:
                    to_core[0, pl.ds(half, 256), :] = grad.astype(BF16)
            else:
                unit = 256 >> 1
                off = 0 if level == 3 else unit
                one, two = grad[:unit], grad[unit:]
                if k == 0:
                    kept[0, pl.ds(256 + off, unit), :] = one
                    kept[0, pl.ds(512 + off, unit), :] = two
                else:
                    to_core[0, pl.ds(half + 256 + off, unit), :] = one.astype(BF16)
                    to_core[0, pl.ds(half + 512 + off, unit), :] = two.astype(BF16)
            if count >= LANES:
                if level == 1 and k == 0:
                    acc[...] = grad_q
                else:
                    acc[:, :count] += grad_q
            else:
                acc[:, :LANES] += jnp.concatenate(
                    [grad_q, jnp.zeros((LANES, LANES - count), F32)], axis=1
                )
    dq[0] = acc[...].T.astype(BF16)


def peers_back(place, gm, merged, q, kv_all):
    heads, n, _ = q.shape
    assert n == SEG
    return pl.pallas_call(
        peers_back_kernel,
        grid=(heads,),
        in_specs=[
            pl.BlockSpec(memory_space=pltpu.SMEM),
            pl.BlockSpec((n, LANES), lambda h: (0, h)),
            per_head(n),
            per_head(n // 2),
            per_head(2 * n),
        ],
        out_specs=[per_head(n), per_head(n // 2), per_head(n + n // 4), per_head(3 * n // 4)],
        out_shape=[
            stored((heads, n, LANES), BF16),
            stored((heads, n // 2, LANES), BF16),
            shape((heads, n + n // 4, LANES), BF16),
            shape((heads, 3 * n // 4, LANES), F32),
        ],
        scratch_shapes=[pltpu.VMEM((LANES, n // 2), F32)],
        compiler_params=params(16),
        cost_estimate=pl.CostEstimate(
            flops=heads * n * n * 1280, bytes_accessed=24 * 2**20, transcendentals=heads * n * n // 2
        ),
        name="peers_back",
    )(place, far(gm), far(merged), far(q), far(kv_all))


def own_back_kernel(q, do, kv, dq, dkv, acc, *, block):
    n = q.shape[1]
    for i in range(n // block):
        at = pl.ds(i * block, block)
        grad, grad_q = pair_back(kv[0, at, :], q[0], do[0])
        dkv[0, at, :] = grad.astype(BF16)
        if i == 0:
            acc[...] = grad_q
        else:
            acc[...] += grad_q
    dq[0] = acc[...].T.astype(BF16)


def own_back(q, do, kv, start, count, into=None):
    heads, n, _ = q.shape
    spec = group_spec(n, start)
    kernel = functools.partial(own_back_kernel, block=256)
    extra = () if into is None else tuple(into)
    return pl.pallas_call(
        kernel if into is None else lambda q, do, kv, _, __, *out: kernel(q, do, kv, *out),
        grid=(count,),
        in_specs=[spec] * 3 + [ANYWHERE] * len(extra),
        out_specs=[spec] * 2,
        out_shape=[stored((heads, n, LANES), BF16)] * 2,
        input_output_aliases={3: 0, 4: 1} if extra else {},
        scratch_shapes=[pltpu.VMEM((LANES, n), F32)],
        compiler_params=params(16),
        cost_estimate=pl.CostEstimate(
            flops=count * n * n * 2560, bytes_accessed=8 * 2**20, transcendentals=count * n * n
        ),
        name="own_back",
    )(far(q), far(do), far(kv), *extra)


def finish_q_kernel(
    place, dq_own, dq_peer, normed, wide, merged_c, merged_d, grad_low, out, grad_w, grad_b, nat0, nat1, acc
):
    i = pl.program_id(0)
    n = nat0.shape[0]
    lane = lax.broadcasted_iota(jnp.int32, (n, LANES), 1)
    low = []
    for j, nat in enumerate((nat0, nat1)):
        unpermute(place[0] + 2 * i + j, j, (dq_own, dq_peer), nat)
        rows = jnp.where(lane < HD, nat[...] * (1.0 / ROOT), 0.0)
        grad_b[j, 0:1, :] = jnp.sum(rows, 0, keepdims=True)
        low.append(rows.astype(BF16))
    low = jnp.concatenate(low, axis=1)
    gradient = dot_lt(low, normed[...])
    grad_w[0, 0] = gradient[:HD].astype(BF16)
    grad_w[0, 1] = gradient[LANES : LANES + HD].astype(BF16)
    steps = merged_c.shape[0] // (2 * HD)
    for ref, base in ((merged_c, 0), (merged_d, steps)):

        @pl.when((i >= base) & (i < base + steps))
        def _():
            pair = dot(ref[cut(i - base, 2 * HD), :], grad_low[...])
            grad_w[1, 0] = pair[:HD].astype(BF16)
            grad_w[1, 1] = pair[HD:].astype(BF16)

    part = dot_rt(low, jnp.concatenate([wide[0], wide[1]], axis=1))

    @pl.when(i == 0)
    def _():
        acc[...] = part

    @pl.when(i > 0)
    def _():
        acc[...] += part

    @pl.when(i == pl.num_programs(0) - 1)
    def _():
        out[...] = acc[...].astype(BF16)


def unpermute(head, j, sources, nat):
    n = nat.shape[0]
    block = n // FOLD
    for p in range(FOLD):
        c = (head + ORDER[p]) % FOLD
        at = pl.ds(p * block, block)
        total = None
        for ref in sources:
            if p * block < ref.shape[1]:
                piece = ref[j, at, :].astype(F32)
                total = piece if total is None else total + piece
        nat[pl.ds(c, block, stride=FOLD), :] = total


def finish_kv_kernel(
    place, dkv_own, r_core, r_x, r_z1, r_z2, r_z3, normed, rows, wide, start, grad_one,
    grad_normed, keep, send, grad_b, sums, acc, nat0, nat1,
):
    i = pl.program_id(0)
    n, d = rows.shape
    lane = lax.broadcasted_iota(jnp.int32, (n, LANES), 1)
    low = []
    for j, nat in enumerate((nat0, nat1)):
        unpermute(place[0] + 2 * i + j, j, (dkv_own, r_core, r_x, r_z1, r_z2, r_z3), nat)
        both = nat[...]
        both = jnp.where(lane < HD, both * (1.0 / ROOT), jnp.where(lane < 2 * HD, both, 0.0))
        grad_b[j, 0:1, :] = jnp.sum(both, 0, keepdims=True)
        low.append(both.astype(BF16))
    low = jnp.concatenate(low, axis=1)
    gradient = dot_lt(low, normed[...])
    first = place[3] == 0
    for j in range(2):
        for k in range(2):
            one = grad_one[k, j]
            two = gradient[j * LANES + k * HD : j * LANES + (k + 1) * HD].astype(BF16)
            keep[k, j] = jnp.where(first, one, two)
            send[k, j] = jnp.where(first, two, one)
    part = dot_rt(low, jnp.concatenate([wide[0], wide[1]], axis=1))

    @pl.when(i == 0)
    def _():
        acc[...] = start[...].astype(F32) + part

    @pl.when(i > 0)
    def _():
        acc[...] += part

    @pl.when(i == pl.num_programs(0) - 1)
    def _():
        total = acc[...]
        grad_normed[...] = total.astype(BF16)
        unit, _ = unit_rows(rows[...].astype(F32))
        sums[0:1, :] = jnp.sum(total * unit, 0, keepdims=True)
        sums[1:2, :] = jnp.sum(total, 0, keepdims=True)
        sums[2:8, :] = jnp.zeros((6, d), F32)


def pairs(rows):
    return pl.BlockSpec((2, rows, LANES), lambda i: (i, 0, 0))


def finish_q(place, dq_own, dq_peer, normed, wide, merged, grad_low):
    heads, n, _ = dq_own.shape
    d = normed.shape[1]
    return pl.pallas_call(
        finish_q_kernel,
        grid=(heads // 2,),
        in_specs=[
            pl.BlockSpec(memory_space=pltpu.SMEM),
            pairs(n),
            pairs(n // 2),
            once((n, d)),
            pl.BlockSpec((2, d, LANES), lambda i: (i, 0, 0)),
            once(merged[0].shape),
            once(merged[1].shape),
            once((n, d)),
        ],
        out_specs=[
            full((n, d)),
            pl.BlockSpec((2, 2, HD, d), lambda i: (0, i, 0, 0)),
            pl.BlockSpec((2, 1, LANES), lambda i: (i, 0, 0)),
        ],
        out_shape=[
            stored((n, d), BF16),
            stored((2, heads, HD, d), BF16),
            shape((heads, 1, LANES), F32),
        ],
        scratch_shapes=[pltpu.VMEM((n, LANES), F32)] * 2 + [pltpu.VMEM((n, d), F32)],
        compiler_params=params(28),
        cost_estimate=pl.CostEstimate(
            flops=4 * n * d * heads * 128, bytes_accessed=14 * 2**20, transcendentals=0
        ),
        name="finish_q",
    )(place, far(dq_own), far(dq_peer), normed, far(wide), *merged, grad_low)


def finish_kv(place, dkv_own, received, normed, rows, wide, start, grad_one):
    heads, n, _ = dkv_own.shape
    d = normed.shape[1]
    return pl.pallas_call(
        finish_kv_kernel,
        grid=(heads // 2,),
        in_specs=[
            pl.BlockSpec(memory_space=pltpu.SMEM),
            pairs(n),
            pairs(n // 2),
            pairs(n // 4),
            pairs(n // 8),
            pairs(n // 16),
            pairs(n // 16),
            once((n, d)),
            once((n, d)),
            pl.BlockSpec((2, d, LANES), lambda i: (i, 0, 1)),
            once((n, d)),
            pl.BlockSpec((2, 2, HD, d), lambda i: (0, i, 0, 0)),
        ],
        out_specs=[
            full((n, d)),
            pl.BlockSpec((2, 2, HD, d), lambda i: (0, i, 0, 0)),
            pl.BlockSpec((2, 2, HD, d), lambda i: (0, i, 0, 0)),
            pl.BlockSpec((2, 1, LANES), lambda i: (i, 0, 0)),
            full((8, d)),
        ],
        out_shape=[
            shape((n, d), BF16),
            stored((2, heads, HD, d), BF16),
            shape((2, heads, HD, d), BF16),
            shape((heads, 1, LANES), F32),
            shape((8, d), F32),
        ],
        scratch_shapes=[pltpu.VMEM((n, d), F32)] + [pltpu.VMEM((n, LANES), F32)] * 2,
        compiler_params=params(36),
        cost_estimate=pl.CostEstimate(
            flops=4 * n * d * heads * 128, bytes_accessed=20 * 2**20, transcendentals=0
        ),
        name="finish_kv",
    )(place, far(dkv_own), *received, normed, rows, far(wide), far(start), far(grad_one))


def spread_kernel(place, own, peer, down, up):
    first = place[3] == 0
    down[...] = jnp.where(first, own[...], peer[...]).astype(F32)
    up[...] = jnp.where(first, peer[...], own[...]).astype(F32).T


def spread(place, own, peer):
    ff, d = own.shape
    block = 256
    rows = pl.BlockSpec((block, d), lambda i: (i, 0))
    return pl.pallas_call(
        spread_kernel,
        grid=(ff // block,),
        in_specs=[pl.BlockSpec(memory_space=pltpu.SMEM), rows, rows],
        out_specs=[rows, pl.BlockSpec((d, block), lambda i: (0, i))],
        out_shape=[shape((ff, d), F32), shape((d, ff), F32)],
        compiler_params=params(12),
        name="spread",
    )(place, own, peer)


def spread_qkv_kernel(place, own, peer, qkv, out):
    first = place[3] == 0
    half, d = own.shape
    width = qkv.shape[2]
    one = jnp.where(first, own[...], peer[...]).astype(F32)
    two = jnp.where(first, peer[...], own[...]).astype(F32)
    qkv[0] = one[:width].T
    qkv[1] = two[:width].T
    qkv[2] = two[width:].T
    out[...] = one[width:]


def spread_qkv(place, own, peer):
    half, d = own.shape
    width = half // 2
    return pl.pallas_call(
        spread_qkv_kernel,
        in_specs=[pl.BlockSpec(memory_space=pltpu.SMEM), once(own.shape), once(own.shape)],
        out_specs=[full((3, d, width)), full((width, d))],
        grid=(1,),
        out_shape=[shape((3, d, width), F32), shape((width, d), F32)],
        compiler_params=params(20),
        name="spread_qkv",
    )(place, own, peer)


def last_kernel(rows, own_g, peer_g, grad_hidden, gain, out):
    unit, inverse = unit_rows(rows[...].astype(F32))
    gradient = own_g[...].astype(F32) + peer_g[...].astype(F32)
    out[...] = grad_hidden[...] + norm_back(gradient, unit, inverse, gain[...])


def last(rows, own_g, peer_g, grad_hidden, gain):
    n, d = rows.shape
    part = pl.BlockSpec((256, d), lambda i: (i, 0))
    return pl.pallas_call(
        last_kernel,
        grid=(n // 256,),
        in_specs=[part] * 4 + [once((1, d))],
        out_specs=part,
        out_shape=shape((n, d), F32),
        compiler_params=params(12),
        cost_estimate=LIGHT,
        name="last",
    )(rows, own_g, peer_g, grad_hidden, gain)


def gather_small_kernel(sums1, sums_a, sums_c, up_a, up_c, grad_bq, grad_bkv, out):
    heads = grad_bq.shape[0]
    d = out.shape[1]
    out[...] = jnp.zeros_like(out)
    out[0:2, :] = sums1[0:2, :]
    out[2:6, :] = sums_a[0:4, :] + sums_c[0:4, :]
    up = up_a[...] + up_c[...]
    for k in range(up.shape[1] // d):
        out[6 + k : 7 + k, :] = up[:, k * d : (k + 1) * d]
    row = [grad_bq[h, :, :HD] for h in range(heads)]
    row += [grad_bkv[h, :, HD : 2 * HD] for h in range(heads)]
    out[15:16, :] = jnp.concatenate(row, axis=1)


def gather_small(sums1, sums2, up_b, grad_bq, grad_bkv):
    d = sums1.shape[1]
    inputs = (sums1, *sums2, *up_b, grad_bq, grad_bkv)
    return pl.pallas_call(
        gather_small_kernel,
        grid=(1,),
        in_specs=[once(x.shape) for x in inputs],
        out_specs=full((FOLD, d)),
        out_shape=shape((FOLD, d), F32),
        compiler_params=params(4),
        cost_estimate=LIGHT,
        name="gather_small",
    )(*inputs)


def spread_small_kernel(small, peer, gains, shifts, qv, out_b, up_b, down_b):
    d = small.shape[1]
    width = qv.shape[1]
    gains[0:1, :] = small[0:1, :] + peer[0:1, :]
    shifts[0:1, :] = small[1:2, :] + peer[1:2, :]
    gains[1:2, :] = small[2:3, :]
    shifts[1:2, :] = small[3:4, :]
    out_b[...] = small[4:5, :]
    down_b[...] = small[5:6, :]
    for k in range(up_b.shape[1] // d):
        up_b[:, k * d : (k + 1) * d] = small[6 + k : 7 + k, :]
    qv[0:1, :] = small[15:16, :width]
    qv[1:2, :] = small[15:16, width:]


def spread_small(small, peer, ff):
    d = small.shape[1]
    dims = [(2, d), (2, d), (2, d // 2), (1, d), (1, ff), (1, d)]
    return pl.pallas_call(
        spread_small_kernel,
        grid=(1,),
        in_specs=[once(small.shape), once(peer.shape)],
        out_specs=[full(x) for x in dims],
        out_shape=[shape(x, F32) for x in dims],
        compiler_params=params(4),
        cost_estimate=LIGHT,
        name="spread_small",
    )(small, peer)


def swap(x, axis, apart):
    count = lax.axis_size(axis)
    return lax.ppermute(x, axis, [(i, i ^ apart) for i in range(count)])


def whole_call(kernel, place, inputs, outputs, name):
    return pl.pallas_call(
        kernel,
        grid=(1,),
        in_specs=[pl.BlockSpec(memory_space=pltpu.SMEM)] + [once(x.shape) for x in inputs],
        out_specs=[full(dims) for dims, _ in outputs],
        out_shape=[shape(dims, kind) for dims, kind in outputs],
        compiler_params=params(24),
        cost_estimate=LIGHT,
        name=name,
    )(place, *inputs)


def added(refs, at=slice(None)):
    total = refs[0][at, :].astype(F32)
    for ref in refs[1:]:
        total = total + ref[at, :].astype(F32)
    return total


def cut(index, count):
    return pl.ds(pl.multiple_of(index * count, count), count)


class Sum:
    def __init__(self, place, rows, width):
        self.place, self.rows, self.width = place, rows, width
        self.third, self.twelfth = rows // 3, rows // 12

    def call(self, kernel, inputs, outputs, name):
        dims = [((count, self.width), kind) for count, kind in outputs]
        return whole_call(kernel, self.place, inputs, dims, name)

    def start(self, keep, got):
        third, twelfth = self.third, self.twelfth

        def kernel(place, keep, got, m1, s1, m2, *s2):
            side, line = place[4], place[5]
            m1[...] = added((keep, got), cut(side, third))
            s1[...] = added((keep, got), cut(1 - side, third)).astype(BF16)

            def quarter(k):
                at = pl.multiple_of(2 * third + (line ^ k) * twelfth, twelfth)
                return added((keep, got), pl.ds(at, twelfth))

            m2[...] = quarter(0)
            for k in (1, 2, 3):
                s2[k - 1][...] = quarter(k).astype(BF16)

        return self.call(
            kernel,
            (keep, got),
            [(third, F32), (third, BF16), (twelfth, F32)] + [(twelfth, BF16)] * 3,
            "start_sum",
        )

    def send1(self, state):
        m1, s1, m2, *s2 = state
        got = swap(s1, "seq", 2)
        return (m1, m2, got) + tuple(swap(x, "seq", 4 * k) for k, x in zip((1, 2, 3), s2))

    def middle(self, state):
        twelfth = self.twelfth

        def kernel(place, m1, m2, g1, ga, gb, gc, n1, n2, s2, *s1):
            side, line = place[4], place[5]
            n1[...] = added((m1, g1), cut(line, twelfth))
            for k in (1, 2, 3):
                s1[k - 1][...] = added((m1, g1), cut(line ^ k, twelfth)).astype(BF16)
            n2[...] = added((m2, ga, gb, gc), cut(side, twelfth // 2))
            s2[...] = added((m2, ga, gb, gc), cut(1 - side, twelfth // 2)).astype(BF16)

        return self.call(
            kernel,
            state,
            [(twelfth, F32), (twelfth // 2, F32), (twelfth // 2, BF16)] + [(twelfth, BF16)] * 3,
            "middle_sum",
        )

    def send2(self, state):
        n1, n2, s2, *s1 = state
        got = tuple(swap(x, "seq", 4 * k) for k, x in zip((1, 2, 3), s1))
        return (n1, n2) + got + (swap(s2, "seq", 2),)

    def end(self, state):
        twelfth = self.twelfth

        def kernel(place, n1, n2, ga, gb, gc, g2, one, two):
            one[...] = added((n1, ga, gb, gc)).astype(BF16)
            two[...] = added((n2, g2)).astype(BF16)

        pair = self.call(kernel, state, [(twelfth, BF16), (twelfth // 2, BF16)], "end_sum")
        return tuple(self.beyond(x) for x in pair)

    def beyond(self, low):
        apart = FOLD
        while apart < lax.axis_size("seq"):
            low = (low.astype(F32) + swap(low, "seq", apart).astype(F32)).astype(BF16)
            apart *= 2
        return low

    def send3(self, pair):
        one, two = pair
        got = tuple(swap(one, "seq", 4 * k) for k in (1, 2, 3))
        return (one, two) + got + (swap(two, "seq", 2),)

    def join(self, state):
        twelfth, third = self.twelfth, self.third

        def kernel(place, one, two, ga, gb, gc, g2, out1, out2):
            side, line = place[4], place[5]
            for k, ref in enumerate((one, ga, gb, gc)):
                out1[cut(line ^ k, twelfth), :] = ref[...]
            out2[cut(side, twelfth // 2), :] = two[...]
            out2[cut(1 - side, twelfth // 2), :] = g2[...]

        return self.call(kernel, state, [(third, BF16), (twelfth, BF16)], "join_sum")

    def send4(self, pair):
        one, two = pair
        got = swap(one, "seq", 2)
        return (one, two, got) + tuple(swap(two, "seq", 4 * k) for k in (1, 2, 3))

    def whole(self, state):
        twelfth, third = self.twelfth, self.third

        def kernel(place, one, two, g1, ga, gb, gc, out):
            side, line = place[4], place[5]
            out[cut(side, third), :] = one[...]
            out[cut(1 - side, third), :] = g1[...]
            for k, ref in enumerate((two, ga, gb, gc)):
                at = pl.multiple_of(2 * third + (line ^ k) * twelfth, twelfth)
                out[pl.ds(at, twelfth), :] = ref[...]

        return self.call(kernel, state, [(self.rows, BF16)], "whole_sum")[0]


def send_home(place, kept, r_core):
    heads, rows, lanes = kept.shape
    quarter = rows // 3
    half = r_core.shape[1] - rows

    def kernel(place, kept, r_core, far, near, stay):
        def both(k):
            return kept[:, cut(k, quarter), :] + r_core[
                :, pl.ds(half + k * quarter, quarter), :
            ].astype(F32)

        near[...] = both(0).astype(BF16)
        stay[...] = both(1)
        far[...] = both(2).astype(BF16)

    dims = (heads, quarter, lanes)
    return whole_call(
        kernel, place, (kept, r_core), [(dims, BF16), (dims, BF16), (dims, F32)], "send_home"
    )


def send_line(place, stay, got):
    heads, rows, lanes = stay.shape

    def kernel(place, stay, got, z1, z2, z3):
        def both(start, count):
            at = pl.ds(start, count)
            return (stay[:, at, :] + got[:, at, :].astype(F32)).astype(BF16)

        z1[...] = both(0, rows // 2)
        z2[...] = both(rows // 2, rows // 4)
        z3[...] = both(3 * rows // 4, rows // 4)

    return whole_call(
        kernel,
        place,
        (stay, got),
        [((heads, count, lanes), BF16) for count in (rows // 2, rows // 4, rows // 4)],
        "send_line",
    )


def tie(*xs):
    return lax.optimization_barrier(xs)


def sum_small(x, apart):
    while apart < lax.axis_size("seq"):
        x = x + swap(x, "seq", apart)
        apart *= 2
    return x


def local(
    rows,
    lengths,
    norm_gains,
    norm_shifts,
    qkv_weight,
    qv_bias,
    out_weight,
    out_bias,
    up_weight,
    up_bias,
    down_weight,
    down_bias,
    out_cot,
):
    n, d = rows.shape
    width = qkv_weight.shape[2]
    heads = width // HD
    seq_place = lax.axis_index("seq")
    head_place = lax.axis_index("head")
    slide_rows = min(FOLD * SEG, n * lax.axis_size("seq"))
    start = seq_place * n
    slide = start // slide_rows
    length = jnp.sum(jnp.where(jnp.arange(lengths.shape[0]) == slide, lengths, 0))
    limit = jnp.clip(length - start % slide_rows, 0, n)
    place = jnp.stack(
        [
            head_place * heads,
            limit,
            head_place,
            seq_place % 2,
            seq_place // 2 % 2,
            seq_place // 4 % 4,
        ]
    ).astype(jnp.int32)
    half, quarter, eighth = n // 2, n // 4, n // 8
    first_heads = heads // 2

    peer_out_weight = swap(out_weight, "head", 1)
    wide_out = jnp.pad(
        out_weight.reshape(heads, HD, d), ((0, 0), (HD, LANES - 2 * HD), (0, 0))
    ).reshape(heads * LANES, d)

    q, kv, s1, sx, sz1, sz, normed1, wide = project(
        place, rows, norm_gains[:1], norm_shifts[:1], qkv_weight, qv_bias
    )
    rz1 = swap(sz1, "seq", 4)
    rx = swap(sx, "seq", 2)
    rz2 = swap(sz, "seq", 8)
    rz3 = swap(sz, "seq", 12)
    cs1 = swap(s1, "seq", 1)
    own = own_attention(q, kv, 0, first_heads)
    own, rz1, rx, rz2, rz3, cs1 = tie(own, rz1, rx, rz2, rz3, cs1)
    zc = jnp.concatenate([rz1, rz2, rz3], 1)
    rx2 = swap(zc, "seq", 2)
    crx = swap(rx, "seq", 1)
    czc = swap(zc, "seq", 1)
    own = own_attention(q, kv, first_heads, heads - first_heads, own)
    own, rx2, crx, czc, peer_out_weight = tie(own, rx2, crx, czc, peer_out_weight)
    crx2 = swap(rx2, "seq", 1)
    received = (cs1, rx, crx, zc, rx2, czc, crx2)
    *state, low_one = peers_attention(place, q, own, received, 0, first_heads)
    peer_low_one = swap(low_one, "head", 1)
    *state, low_two = peers_attention(
        place, q, own, received, first_heads, heads - first_heads, state
    )
    merged, kv_all, qb = state
    merged, low_two, peer_low_one = tie(merged, low_two, peer_low_one)
    merged_low = (low_one, low_two)
    peer_low = (peer_low_one, swap(low_two, "head", 1))

    def feed_rows(start, into):
        return feed(
            place,
            rows,
            out_cot,
            merged_low + peer_low,
            out_weight,
            peer_out_weight,
            out_bias[None],
            norm_gains[1:],
            norm_shifts[1:],
            up_weight,
            up_bias[None],
            down_weight,
            start,
            half,
            into,
        )

    *fed, g2_one, ub_one = feed_rows(0, None)
    peer_one = swap(g2_one, "head", 1)
    *fed, g2_two, ub_two = feed_rows(half, fed)
    *fed, peer_one = tie(*fed, peer_one)
    hidden, normed2, act, grad_pre = fed
    peer_two = swap(g2_two, "head", 1)
    mlp, keep, send = weights(place, act, grad_pre, normed2, out_cot, down_weight)
    *turned, sums2_one = turn(
        out_cot, g2_one, peer_one, hidden, norm_gains[1:], wide_out, 0, half
    )
    peer_two, mlp, keep, send, *turned = tie(peer_two, mlp, keep, send, *turned)

    ff = up_bias.shape[0]
    sums = Sum(place, ff, d)
    got = swap(send, "seq", 1)
    grad_hidden, grad_low, gm, sums2_two = turn(
        out_cot, g2_two, peer_two, hidden, norm_gains[1:], wide_out, half, half, turned
    )
    gm, keep, got = tie(gm, keep, got)
    ff_state = sums.send1(sums.start(keep, got))
    peer_mlp = swap(mlp, "head", 1)
    do, dq_peer, to_core, kept = peers_back(place, gm, merged, qb, kv_all)
    do, dq_peer, to_core, kept, *ff_state = tie(do, dq_peer, to_core, kept, *ff_state)
    r_core = swap(to_core, "seq", 1)
    ff_state = sums.send2(sums.middle(ff_state))
    back = own_back(qb, do, kv, 0, first_heads)
    dq_own, dkv_own, r_core, *ff_state = tie(*back, r_core, *ff_state)
    far, near, stay = send_home(place, kept, r_core)
    r_x2 = swap(far, "seq", 2)
    r_x = swap(near, "seq", 2)
    ff_state = sums.send3(sums.end(ff_state))
    back = own_back(qb, do, kv, first_heads, heads - first_heads, (dq_own, dkv_own))
    dq_own, dkv_own, r_x2, *ff_state = tie(*back, r_x2, *ff_state)
    z1, z2, z3 = send_line(place, stay, r_x2)
    r_z1 = swap(z1, "seq", 4)
    r_z2 = swap(z2, "seq", 8)
    r_z3 = swap(z3, "seq", 12)
    start_g, grad_one, grad_bq = finish_q(
        place, dq_own, dq_peer, normed1, wide, merged_low, grad_low
    )
    start_g, grad_one, peer_mlp, r_x, r_z1, r_z2, r_z3, *ff_state = tie(
        start_g, grad_one, peer_mlp, r_x, r_z1, r_z2, r_z3, *ff_state
    )
    out_rows = (
        hidden + ((mlp.astype(F32) + peer_mlp.astype(F32)) + down_bias)
    ).astype(BF16)
    ff_state = sums.send4(sums.join(ff_state))
    grad_normed1, keep, send, grad_bkv, sums1 = finish_kv(
        place, dkv_own, (r_core, r_x, r_z1, r_z2, r_z3), normed1, rows, wide, start_g, grad_one
    )
    ff_own = sums.whole(ff_state)
    keep, send, sums1, out_rows, ff_own, grad_normed1 = tie(
        keep, send, sums1, out_rows, ff_own, grad_normed1
    )

    count = 2 * width
    keep, send = keep.reshape(count, d), send.reshape(count, d)
    got = swap(send, "seq", 1)
    peer_normed1 = swap(grad_normed1, "head", 1)
    small = gather_small(sums1, (sums2_one, sums2_two), (ub_one, ub_two), grad_bq, grad_bkv)
    keep, got, small = tie(keep, got, small)
    w_sums = Sum(place, count, d)
    state = w_sums.send1(w_sums.start(keep, got))
    small = small + swap(small, "seq", 1)
    *state, small = tie(*state, small)
    state = w_sums.send2(w_sums.middle(state))
    small = small + swap(small, "seq", 2)
    ff_peer = swap(ff_own, "seq", 1)
    *state, small, ff_peer = tie(*state, small, ff_peer)
    state = w_sums.send3(w_sums.end(state))
    small = small + swap(small, "seq", 4)
    rows_grad = last(rows, grad_normed1, peer_normed1, grad_hidden, norm_gains[:1])
    *state, small, rows_grad = tie(*state, small, rows_grad)
    state = w_sums.send4(w_sums.join(state))
    small = sum_small(small, 8)
    down_weight_grad, up_weight_grad = spread(place, ff_own, ff_peer)
    *state, small, down_weight_grad = tie(*state, small, down_weight_grad)
    w_own = w_sums.whole(state)
    w_peer = swap(w_own, "seq", 1)
    gains_grad, shifts_grad, qv_bias_grad, out_bias_grad, up_bias_grad, down_bias_grad = (
        spread_small(small, swap(small, "head", 1), ff)
    )
    qkv_grad, out_weight_grad = spread_qkv(place, w_own, w_peer)
    return (
        out_rows,
        rows_grad,
        gains_grad,
        shifts_grad,
        qkv_grad,
        qv_bias_grad,
        out_weight_grad,
        out_bias_grad.reshape(-1),
        up_weight_grad,
        up_bias_grad.reshape(-1),
        down_weight_grad,
        down_bias_grad.reshape(-1),
    )


def solution(mesh):
    placed = (
        P("seq", None),
        P(),
        P(),
        P(),
        P(None, None, "head"),
        P(None, "head"),
        P("head", None),
        P(),
        P(None, "head"),
        P("head"),
        P("head", None),
        P(),
        P("seq", None),
    )
    return jax.shard_map(
        local,
        mesh=mesh,
        in_specs=placed,
        out_specs=(
            P("seq", None),
            P("seq", None),
            P(),
            P(),
            P(None, None, "head"),
            P(None, "head"),
            P("head", None),
            P(),
            P(None, "head"),
            P("head"),
            P("head", None),
            P(),
        ),
        check_vma=False,
    )
```

```python
import functools
import math

import jax
import jax.numpy as jnp
import numpy as np
from jax import lax
from jax.experimental import pallas as pl
from jax.experimental.pallas import tpu as pltpu
from jax.sharding import PartitionSpec as P

HD = 48
SEG = 1024
LANES = 128
LEVELS = 5
FOLD = 16

EPS = 1e-05
ROOT = math.sqrt(HD)
EXP_SCALE = math.log2(math.e) / ROOT
ROOT_HALF = 1.0 / math.sqrt(2.0)
DENSITY_NORM = 1.0 / math.sqrt(2.0 * math.pi)
ABSENT = -1e20

ONE = 96
MASK = 99
MULT = 100
TOP = 127

ORDER = (0, 8, 4, 12, 2, 6, 10, 14, 1, 3, 5, 7, 9, 11, 13, 15)
CLASS = (4, 3, 2, 2, 1, 1, 1, 1, 0, 0, 0, 0, 0, 0, 0, 0)

F32 = jnp.float32
BF16 = jnp.bfloat16


LIGHT = pl.CostEstimate(flops=0, bytes_accessed=0, transcendentals=0)


def params(mib=48):
    return pltpu.CompilerParams(vmem_limit_bytes=mib * 2**20)


def dot(left, right):
    return jnp.dot(left, right, preferred_element_type=F32)


def dot_rt(left, right):
    return lax.dot_general(left, right, (((1,), (1,)), ((), ())), preferred_element_type=F32)


def dot_lt(left, right):
    return lax.dot_general(left, right, (((0,), (0,)), ((), ())), preferred_element_type=F32)


def full(shape):
    return pl.BlockSpec(shape, lambda *_: (0,) * len(shape))


def once(shape):
    return pl.BlockSpec(shape, lambda *_: (0,) * len(shape), pipeline_mode=pl.Buffered(1))


def per_head(rows, lanes=LANES):
    return pl.BlockSpec((1, rows, lanes), lambda h: (h, 0, 0))


def shape(dims, kind):
    return jax.ShapeDtypeStruct(dims, kind)


def stored(dims, kind):
    return pltpu.HBM(dims, kind)


def far(x):
    return pltpu.with_memory_space_constraint(x, pltpu.HBM)


def split3(x):
    high = x.astype(BF16).astype(F32)
    rest = x - high
    middle = rest.astype(BF16).astype(F32)
    return high, middle, rest - middle


def with_terms(block, lane, terms):
    high, middle, low = split3(terms)
    block = jnp.where(lane == ONE, high, block)
    block = jnp.where(lane == ONE + 1, middle, block)
    return jnp.where(lane == ONE + 2, low, block)


def unit_rows(x):
    mean = jnp.mean(x, -1, keepdims=True)
    centred = x - mean
    inverse = lax.rsqrt(jnp.mean(centred * centred, -1, keepdims=True) + EPS)
    return centred * inverse, inverse


def norm_back(gradient, unit, inverse, gain):
    z = gradient * gain
    return inverse * (
        z - jnp.mean(z, -1, keepdims=True) - unit * jnp.mean(z * unit, -1, keepdims=True)
    )


def mult_table(level, blocks):
    table = np.zeros((len(blocks), LANES), np.float32)
    for row, key_class in enumerate(blocks):
        for j in range(level + 1, key_class + 1):
            value = np.float32(ROOT * math.log((j - level + 1) / (j - level)))
            high = np.float32(value.astype(jnp.bfloat16))
            table[row, MULT + j - 1] = high
            table[row, MULT + 4 + j - 1] = np.float32((value - high).astype(jnp.bfloat16))
    return table


def flag_table():
    table = np.zeros((FOLD, LANES), np.float32)
    for row, level in enumerate(CLASS):
        table[row, MULT : MULT + level] = 1.0
        table[row, MULT + 4 : MULT + 4 + level] = 1.0
    return table


def permuted(head, tmp):
    n = tmp.shape[0]
    block = n // FOLD
    for p in range(FOLD):
        c = (head + ORDER[p]) % FOLD
        yield p, pl.ds(p * block, block), slice(p, p + 1), tmp[pl.ds(c, block, stride=FOLD), :]


def project_kv_kernel(
    place, rows, gain, shift, w, bias, table, one, two, three, four,
    kv, s1, sx, sz1, sz, normed, wide, w_tmp, b_tmp, extra, *tmps,
):
    i = pl.program_id(0)
    n, d = rows.shape
    heads = w.shape[2] // HD
    block = n // FOLD

    @pl.when(i == 0)
    def _():
        unit, _ = unit_rows(rows[...].astype(F32))
        normed[...] = (unit * gain[...] + shift[...]).astype(BF16)
        lane = lax.broadcasted_iota(jnp.int32, (n, LANES), 1)
        here = lax.broadcasted_iota(jnp.int32, (n, LANES), 0) < place[1]
        extra[...] = jnp.where(here | (lane != MASK), 0.0, ABSENT)

    for k in range(heads // 2):

        @pl.when(i == k)
        def _():
            for j in range(2):
                cut = slice((2 * k + j) * HD, (2 * k + j + 1) * HD)
                at = slice(LANES * j, LANES * (j + 1))
                w_tmp[:, at] = jnp.concatenate(
                    [w[1, :, cut], w[2, :, cut], jnp.zeros((d, LANES - 2 * HD), BF16)], axis=1
                )
                b_tmp[:, at] = jnp.concatenate(
                    [
                        jnp.zeros((1, HD), F32),
                        bias[1:2, cut],
                        jnp.ones((1, 3), F32),
                        jnp.zeros((1, LANES - 2 * HD - 3), F32),
                    ],
                    axis=1,
                )

    product = dot(normed[...], w_tmp[...]) + b_tmp[...]
    for j, tmp in enumerate(tmps):
        lanes = slice(LANES * j, LANES * (j + 1))
        wide[j] = w_tmp[:, lanes]
        tmp[...] = product[:, lanes] + extra[...]
        for p, at, row, kv_rows in permuted(place[0] + 2 * i + j, tmp):
            kv[j, at, :] = (kv_rows + table[row, :]).astype(BF16)
            for out, extras in ((s1, one), (sx, two), (sz1, three), (sz, four)):
                if (p + 1) * block <= out.shape[1]:
                    out[j, at, :] = (kv_rows + extras[row, :]).astype(BF16)


def project_q_kernel(place, normed, w, bias, flags, q, wide, w_tmp, b_tmp, extra, *tmps):
    i = pl.program_id(0)
    n, d = normed.shape
    heads = w.shape[2] // HD

    @pl.when(i == 0)
    def _():
        lane = lax.broadcasted_iota(jnp.int32, (n, LANES), 1)
        here = lax.broadcasted_iota(jnp.int32, (n, LANES), 0) < place[1]
        extra[...] = jnp.where(here & (lane == MASK), 1.0, 0.0)

    for k in range(heads // 2):

        @pl.when(i == k)
        def _():
            for j in range(2):
                cut = slice((2 * k + j) * HD, (2 * k + j + 1) * HD)
                at = slice(LANES * j, LANES * (j + 1))
                w_tmp[:, at] = jnp.concatenate(
                    [w[0, :, cut], jnp.zeros((d, LANES - HD), BF16)], axis=1
                )
                b_tmp[:, at] = jnp.concatenate(
                    [bias[0:1, cut], jnp.zeros((1, LANES - HD), F32)], axis=1
                )

    product = dot(normed[...], w_tmp[...]) + b_tmp[...]
    for j, tmp in enumerate(tmps):
        lanes = slice(LANES * j, LANES * (j + 1))
        wide[j] = w_tmp[:, lanes]
        tmp[...] = product[:, lanes] + extra[...]
        for p, at, row, q_rows in permuted(place[0] + 2 * i + j, tmp):
            q[j, at, :] = (q_rows + flags[row, :]).astype(BF16)


def project_scratch(n, d):
    return [
        pltpu.VMEM((d, 2 * LANES), BF16),
        pltpu.VMEM((1, 2 * LANES), F32),
        pltpu.VMEM((n, LANES), F32),
    ] + [pltpu.VMEM((n, LANES), F32)] * 2


def project_kv(place, rows, gain, shift, w, bias):
    n, d = rows.shape
    heads = w.shape[2] // HD
    tables = [jnp.asarray(mult_table(level, CLASS)) for level in range(LEVELS)]
    sizes = (n, n // 2, n // 4, n // 8, n // 16)
    inputs = (rows, gain, shift, w, bias, *tables)
    return pl.pallas_call(
        project_kv_kernel,
        grid=(heads // 2,),
        in_specs=[pl.BlockSpec(memory_space=pltpu.SMEM)] + [once(x.shape) for x in inputs],
        out_specs=[group_spec(m) for m in sizes] + [full((n, d)), group_spec(d)],
        out_shape=[stored((heads, n, LANES), BF16)]
        + [shape((heads, m, LANES), BF16) for m in sizes[1:]]
        + [shape((n, d), BF16), stored((heads, d, LANES), BF16)],
        scratch_shapes=project_scratch(n, d),
        compiler_params=params(24),
        cost_estimate=pl.CostEstimate(
            flops=2 * n * d * heads * 128, bytes_accessed=9 * 2**20, transcendentals=0
        ),
        name="project_kv",
    )(place, *(far(x) for x in inputs))


def project_q(place, normed, w, bias):
    n, d = normed.shape
    heads = w.shape[2] // HD
    inputs = (normed, far(w), far(bias), jnp.asarray(flag_table()))
    return pl.pallas_call(
        project_q_kernel,
        grid=(heads // 2,),
        in_specs=[pl.BlockSpec(memory_space=pltpu.SMEM)] + [once(x.shape) for x in inputs],
        out_specs=[group_spec(n), group_spec(d)],
        out_shape=[stored((heads, n, LANES), BF16), stored((heads, d, LANES), BF16)],
        scratch_shapes=project_scratch(n, d),
        compiler_params=params(20),
        cost_estimate=pl.CostEstimate(
            flops=2 * n * d * heads * 128, bytes_accessed=6 * 2**20, transcendentals=0
        ),
        name="project_q",
    )(place, *inputs)


def own_kernel(q, kv, out, *, block):
    n = q.shape[1]
    lane = lax.broadcasted_iota(jnp.int32, (block, LANES), 1)
    steps = [(j, k * block) for j in range(q.shape[0]) for k in range(n // block)]

    def scores(j, at):
        return dot_rt(q[j, pl.ds(at, block), :], kv[j])

    now = scores(*steps[0])
    for index, (j, at) in enumerate(steps):
        later = scores(*steps[index + 1]) if index + 1 < len(steps) else None
        top = jnp.max(now, -1, keepdims=True)
        weights = jnp.exp2((now - top) * EXP_SCALE).astype(BF16)
        out[j, pl.ds(at, block), :] = jnp.where(lane == TOP, top, dot(weights, kv[j]))
        now = later


def group_spec(rows, start=0, lanes=LANES, heads=2):
    return pl.BlockSpec((heads, rows, lanes), lambda i: (i + start // heads, 0, 0))


ANYWHERE = pl.BlockSpec(memory_space=pl.ANY)


def own_attention(q, kv, start, count, into=None):
    heads, n, _ = q.shape
    spec = group_spec(n, start)
    kernel = functools.partial(own_kernel, block=256)
    extra = () if into is None else (into,)
    return pl.pallas_call(
        kernel if into is None else lambda q, kv, _, out: kernel(q, kv, out),
        grid=(count // 2,),
        in_specs=[spec] * 2 + [ANYWHERE] * len(extra),
        out_specs=spec,
        out_shape=shape((heads, n, LANES), F32),
        input_output_aliases={2: 0} if extra else {},
        compiler_params=params(12),
        cost_estimate=pl.CostEstimate(
            flops=count * n * n * 1024, bytes_accessed=4 * 2**20, transcendentals=count * n * n
        ),
        name="own_attention",
    )(far(q), far(kv), *extra)


def peers_kernel(
    place, q, own, cs1, rx, crx, zc, rx2, czc, crx2, pick, merged, kv_all, qb, low, nat, wide, *, start
):
    i = pl.program_id(0)
    n = q.shape[1]
    block = n // FOLD
    heads = q.shape[0]
    for j in range(heads):
        at = 0
        near = (zc, rx2, czc, crx2)
        pieces = [(cs1, 0, n // 2), (rx, 0, n // 4), (crx, 0, n // 4)]
        pieces += [(r, 0, n // 8) for r in near] + [(r, n // 8, n // 8) for r in near]
        for ref, begin, count in pieces:
            kv_all[j, pl.ds(at, count), :] = ref[j, pl.ds(begin, count), :]
            at += count

        head = place[0] + heads * i + j + start
        chunks = [
            (0, n // 16, 2 * n),
            (n // 16, n // 16, 3 * n // 2),
            (n // 8, n // 8, n),
            (n // 4, n // 4, n // 2),
            (n // 2, n // 2, 0),
        ]
        scores = []
        for begin, count, keys in chunks:
            if keys:
                scores.append(dot_rt(q[j, pl.ds(begin, count), :], kv_all[j, pl.ds(0, keys), :]))
            else:
                scores.append(None)
        for (begin, count, keys), s in zip(chunks, scores):
            rows = pl.ds(begin, count)
            lane = lax.broadcasted_iota(jnp.int32, (count, LANES), 1)
            o = own[j, rows, :]
            top = o[:, TOP : TOP + 1]
            if keys:
                new = jnp.maximum(top, jnp.max(s, -1, keepdims=True))
                weights = jnp.exp2((s - new) * EXP_SCALE).astype(BF16)
                o = o * jnp.exp2((top - new) * EXP_SCALE) + dot(weights, kv_all[j, pl.ds(0, keys), :])
                top = new
            total = o[:, ONE : ONE + 1]
            o = jnp.where((lane >= HD) & (lane < 2 * HD), o / total, 0.0)
            merged[j, rows, :] = o
            lse = top + jnp.log2(total) * (1.0 / EXP_SCALE)
            qb[j, rows, :] = with_terms(q[j, rows, :].astype(F32), lane, -lse).astype(BF16)
            for p in range(begin // block, (begin + count) // block):
                c = (head + ORDER[p]) % FOLD
                off = p * block - begin
                nat[pl.ds(c, block, stride=FOLD), :] = o[off : off + block]
        wide[:, pl.ds(pl.multiple_of((heads * i + j) * LANES, LANES), LANES)] = nat[...].astype(BF16)

    @pl.when(i == pl.num_programs(0) - 1)
    def _():
        low[...] = dot_rt(pick[...], wide[...]).astype(BF16)


def pick_values(heads):
    m = np.zeros((heads * HD, heads * LANES), np.float32)
    for h in range(heads):
        for j in range(HD):
            m[h * HD + j, h * LANES + HD + j] = 1.0
    return m


def peers_attention(place, q, own, received, start, count, into=None):
    heads, n, _ = q.shape
    pick = jnp.asarray(pick_values(count), BF16)
    extra = () if into is None else tuple(into)
    inputs = 4 + len(received)

    def kernel(*refs):
        peers_kernel(*refs[:inputs], *refs[inputs + len(extra) :], start=start)

    return pl.pallas_call(
        kernel,
        grid=(count,),
        in_specs=[
            pl.BlockSpec(memory_space=pltpu.SMEM),
            group_spec(n, start, heads=1),
            group_spec(n, start, heads=1),
        ]
        + [group_spec(r.shape[1], start, heads=1) for r in received]
        + [once(pick.shape)]
        + [ANYWHERE] * len(extra),
        out_specs=[group_spec(n, start, heads=1), group_spec(2 * n, start, heads=1), group_spec(n, start, heads=1)]
        + [full((count * HD, n))],
        out_shape=[
            stored((heads, n, LANES), F32),
            stored((heads, 2 * n, LANES), BF16),
            stored((heads, n, LANES), BF16),
            shape((count * HD, n), BF16),
        ],
        input_output_aliases={inputs + k: k for k in range(len(extra))},
        scratch_shapes=[pltpu.VMEM((n, LANES), F32), pltpu.VMEM((n, count * LANES), BF16)],
        compiler_params=params(28),
        cost_estimate=pl.CostEstimate(
            flops=count * n * n * 512, bytes_accessed=12 * 2**20, transcendentals=count * n * n // 2
        ),
        name="peers_attention",
    )(place, far(q), own, *received, pick, *extra)


def feed_kernel(
    place, rows, cot, own_c, own_d, peer_c, peer_d, own_w, peer_w, out_b, gain, shift, up_w, up_b, down_w,
    hidden, normed, act, grad_pre, *outs, sizes,
):
    *grad_normed, up_b_grad, w_tmp, c_tmp = outs
    i = pl.program_id(0)
    half = own_w.shape[0]
    group = own_c.shape[0]
    first = place[2] == 0

    @pl.when(i == 0)
    def _():
        w_tmp[:half] = jnp.where(first, own_w[...], peer_w[...])
        w_tmp[half:] = jnp.where(first, peer_w[...], own_w[...])

    c_tmp[:group] = jnp.where(first, own_c[...], peer_c[...])
    c_tmp[group:half] = jnp.where(first, own_d[...], peer_d[...])
    c_tmp[half : half + group] = jnp.where(first, peer_c[...], own_c[...])
    c_tmp[half + group :] = jnp.where(first, peer_d[...], own_d[...])
    attended = dot_lt(c_tmp[...], w_tmp[...])
    hid = rows[...].astype(F32) + (attended + out_b[...])
    hidden[...] = hid
    unit, _ = unit_rows(hid)
    low = (unit * gain[...] + shift[...]).astype(BF16)
    normed[...] = low
    pre = dot(low, up_w[...]) + up_b[...]
    phi = 0.5 * (1.0 + lax.erf(pre * ROOT_HALF))
    act[...] = (pre * phi).astype(BF16)
    slope = phi + pre * jnp.exp(-0.5 * pre * pre) * DENSITY_NORM
    gradient = dot_rt(cot[...], down_w[...]) * slope
    total = jnp.sum(gradient, 0, keepdims=True)

    @pl.when(i == 0)
    def _():
        up_b_grad[...] = total

    @pl.when(i > 0)
    def _():
        up_b_grad[...] += total

    gradient = gradient.astype(BF16)
    grad_pre[...] = gradient
    back = dot_rt(gradient, up_w[...]).astype(BF16)
    begin = 0
    for ref, steps in zip(grad_normed, sizes):

        @pl.when((i >= begin) & (i < begin + steps))
        def _():
            ref[...] = back

        begin += steps


def feed(
    place, rows, cot, merged, own_w, peer_w, out_b, gain, shift, up_w, up_b, down_w, start, sizes, into=None
):
    n, d = rows.shape
    block = 256
    count = sum(sizes)
    steps = [size // block for size in sizes]
    begins = [sum(steps[:k]) for k in range(len(steps))]
    ff = up_w.shape[1]
    half = own_w.shape[0]
    first = start // block
    extra = () if into is None else tuple(into)

    def part(lanes):
        return pl.BlockSpec((block, lanes), lambda i: (i + first, 0))

    def kernel(*refs):
        feed_kernel(*refs[:15], *refs[15 + len(extra) :], sizes=steps)

    return pl.pallas_call(
        kernel,
        grid=(count // block,),
        in_specs=[
            pl.BlockSpec(memory_space=pltpu.SMEM),
            part(d),
            part(d),
        ]
        + [pl.BlockSpec((m.shape[0], block), lambda i: (0, i + first)) for m in merged]
        + [
            once(own_w.shape),
            once(peer_w.shape),
            once((1, d)),
            once((1, d)),
            once((1, d)),
            once(up_w.shape),
            once((1, ff)),
            once(down_w.shape),
        ]
        + [ANYWHERE] * len(extra),
        out_specs=[
            part(d),
            part(d),
            part(ff),
            part(ff),
        ]
        + [
            pl.BlockSpec((block, d), lambda i, b=b, m=m: (jnp.clip(i - b, 0, m - 1), 0))
            for b, m in zip(begins, steps)
        ]
        + [full((1, ff))],
        out_shape=[
            shape((n, d), F32),
            shape((n, d), BF16),
            shape((n, ff), BF16),
            shape((n, ff), BF16),
        ]
        + [shape((size, d), BF16) for size in sizes]
        + [shape((1, ff), F32)],
        input_output_aliases={15 + k: k for k in range(len(extra))},
        scratch_shapes=[pltpu.VMEM((2 * half, d), BF16), pltpu.VMEM((2 * half, block), BF16)],
        compiler_params=params(30),
        cost_estimate=pl.CostEstimate(
            flops=2 * count * d * (ff * 3 + d),
            bytes_accessed=12 * 2**20,
            transcendentals=2 * count * ff,
        ),
        name="feed_forward",
    )(
        place, rows, cot, *merged, own_w, peer_w, out_b, gain, shift, up_w, up_b, down_w, *extra
    )


def weights_kernel(place, act, grad_pre, normed, cot, down_w, mlp, keep, send, acc):
    i = pl.program_id(0)
    part = dot(act[...], down_w[...])

    @pl.when(i == 0)
    def _():
        acc[...] = part

    @pl.when(i > 0)
    def _():
        acc[...] += part

    down = dot_lt(act[...], cot[...])
    up = dot_lt(grad_pre[...], normed[...])
    first = place[3] == 0
    keep[...] = jnp.where(first, down, up).astype(BF16)
    send[...] = jnp.where(first, up, down).astype(BF16)

    @pl.when(i == pl.num_programs(0) - 1)
    def _():
        mlp[...] = acc[...].astype(BF16)


def weights(place, act, grad_pre, normed, cot, down_w):
    n, ff = act.shape
    d = cot.shape[1]
    block = 256
    lanes = pl.BlockSpec((n, block), lambda i: (0, i))
    rows = pl.BlockSpec((block, d), lambda i: (i, 0))
    return pl.pallas_call(
        weights_kernel,
        grid=(ff // block,),
        in_specs=[
            pl.BlockSpec(memory_space=pltpu.SMEM),
            lanes,
            lanes,
            once((n, d)),
            once((n, d)),
            rows,
        ],
        out_specs=[full((n, d)), rows, rows],
        out_shape=[shape((n, d), BF16), shape((ff, d), BF16), shape((ff, d), BF16)],
        scratch_shapes=[pltpu.VMEM((n, d), F32)],
        compiler_params=params(26),
        cost_estimate=pl.CostEstimate(
            flops=6 * n * d * ff, bytes_accessed=20 * 2**20, transcendentals=0
        ),
        name="weights",
    )(place, act, grad_pre, normed, cot, down_w)


def turn_kernel(cot, own_g, peer_g, hidden, gain, out_w, grad_hidden, low_out, gm, sums):
    i = pl.program_id(0)
    unit, inverse = unit_rows(hidden[...])
    gradient = own_g[...].astype(F32) + peer_g[...].astype(F32)
    outer = cot[...].astype(F32)
    total = outer + norm_back(gradient, unit, inverse, gain[...])
    grad_hidden[...] = total
    low = total.astype(BF16)
    low_out[...] = low
    gm[...] = dot_rt(low, out_w[...]).astype(BF16).astype(F32)

    @pl.when(i == 0)
    def _():
        sums[...] = jnp.zeros_like(sums)

    sums[0:1, :] += jnp.sum(gradient * unit, 0, keepdims=True)
    sums[1:2, :] += jnp.sum(gradient, 0, keepdims=True)
    sums[2:3, :] += jnp.sum(total, 0, keepdims=True)
    sums[3:4, :] += jnp.sum(outer, 0, keepdims=True)


def turn(cot, own_g, peer_g, hidden, gain, out_w, start, count, into=None):
    n, d = cot.shape
    block = 256
    first = start // block
    wide = out_w.shape[0]
    extra = () if into is None else tuple(into)

    def part(lanes):
        return pl.BlockSpec((block, lanes), lambda i: (i + first, 0))

    own_part = pl.BlockSpec((block, d), lambda i: (i, 0))

    def kernel(*refs):
        turn_kernel(*refs[:6], *refs[6 + len(extra) :])

    return pl.pallas_call(
        kernel,
        grid=(count // block,),
        in_specs=[part(d), own_part, own_part, part(d), once((1, d)), once((wide, d))]
        + [ANYWHERE] * len(extra),
        out_specs=[part(d), part(d), part(wide), full((8, d))],
        out_shape=[
            stored((n, d), F32),
            stored((n, d), BF16),
            stored((n, wide), F32),
            shape((8, d), F32),
        ],
        input_output_aliases={6 + k: k for k in range(len(extra))},
        compiler_params=params(16),
        cost_estimate=LIGHT,
        name="turn",
    )(cot, own_g, peer_g, hidden, gain, out_w, *extra)


def pair_back(keys, q, do):
    weights = jnp.exp2(dot_rt(keys, q) * EXP_SCALE)
    inner = (weights * dot_rt(keys, do)).astype(BF16)
    grad_keys = dot(weights.astype(BF16), do) + dot(inner, q)
    return grad_keys, dot(keys.T, inner)


def peers_back_kernel(
    place, gm0, gm1, merged, q, kv_all, do, dq, to_core, kept, acc0, acc1, *, start
):
    half = q.shape[1]
    n = 2 * half
    block = n // FOLD
    lane = lax.broadcasted_iota(jnp.int32, (block, LANES), 1)
    for j, (gm_j, acc) in enumerate(((gm0, acc0), (gm1, acc1))):
        head = place[0] + 2 * pl.program_id(0) + j + start
        for p in range(FOLD):
            c = (head + ORDER[p]) % FOLD
            at = pl.ds(p * block, block)
            gradient = gm_j[pl.ds(c, block, stride=FOLD), :]
            delta = jnp.sum(gradient * merged[j, at, :], -1, keepdims=True)
            do[j, at, :] = with_terms(gradient, lane, -delta).astype(BF16)
        for level in (1, 2, 3, 4):
            count = n >> level
            begin = (level - 1) * half
            for k in range(0, half, 256):
                grad, grad_q = pair_back(
                    kv_all[j, pl.ds(begin + k, 256), :], q[j, pl.ds(0, count), :], do[j, pl.ds(0, count), :]
                )
                if level == 1:
                    to_core[j, pl.ds(k, 256), :] = grad.astype(BF16)
                elif level == 2:
                    if k == 0:
                        kept[j, pl.ds(0, 256), :] = grad
                    else:
                        to_core[j, pl.ds(half, 256), :] = grad.astype(BF16)
                else:
                    unit = 256 >> 1
                    off = 0 if level == 3 else unit
                    one, two = grad[:unit], grad[unit:]
                    if k == 0:
                        kept[j, pl.ds(256 + off, unit), :] = one
                        kept[j, pl.ds(512 + off, unit), :] = two
                    else:
                        to_core[j, pl.ds(half + 256 + off, unit), :] = one.astype(BF16)
                        to_core[j, pl.ds(half + 512 + off, unit), :] = two.astype(BF16)
                if count >= LANES:
                    if level == 1 and k == 0:
                        acc[...] = grad_q
                    else:
                        acc[:, :count] += grad_q
                else:
                    acc[:, :LANES] += jnp.concatenate(
                        [grad_q, jnp.zeros((LANES, LANES - count), F32)], axis=1
                    )
        dq[j] = acc[...].T.astype(BF16)


def peers_back(place, gm, merged, q, kv_all, start, count, into=None):
    heads, n, _ = q.shape
    assert n == SEG
    extra = () if into is None else tuple(into)

    def kernel(*refs):
        peers_back_kernel(*refs[:6], *refs[6 + len(extra) :], start=start)

    return pl.pallas_call(
        kernel,
        grid=(count // 2,),
        in_specs=[
            pl.BlockSpec(memory_space=pltpu.SMEM),
            pl.BlockSpec((n, LANES), lambda i: (0, 2 * i + start)),
            pl.BlockSpec((n, LANES), lambda i: (0, 2 * i + 1 + start)),
            group_spec(n, start),
            group_spec(n // 2, start),
            group_spec(2 * n, start),
        ]
        + [ANYWHERE] * len(extra),
        out_specs=[group_spec(n, start), group_spec(n // 2, start), group_spec(n + n // 4, start), group_spec(3 * n // 4, start)],
        out_shape=[
            stored((heads, n, LANES), BF16),
            stored((heads, n // 2, LANES), BF16),
            shape((heads, n + n // 4, LANES), BF16),
            shape((heads, 3 * n // 4, LANES), F32),
        ],
        input_output_aliases={6 + k: k for k in range(len(extra))},
        scratch_shapes=[pltpu.VMEM((LANES, n // 2), F32)] * 2,
        compiler_params=params(24),
        cost_estimate=pl.CostEstimate(
            flops=count * n * n * 1280, bytes_accessed=24 * 2**20, transcendentals=count * n * n // 2
        ),
        name="peers_back",
    )(place, far(gm), far(gm), far(merged), far(q), far(kv_all), *extra)


def own_back_kernel(q, do, kv, dq, dkv, *accs, block):
    n = q.shape[1]
    for j, acc in enumerate(accs):
        for i in range(n // block):
            at = pl.ds(i * block, block)
            grad, grad_q = pair_back(kv[j, at, :], q[j], do[j])
            dkv[j, at, :] = grad.astype(BF16)
            if i == 0:
                acc[...] = grad_q
            else:
                acc[...] += grad_q
        dq[j] = acc[...].T.astype(BF16)


def own_back(q, do, kv, start, count, into=None):
    heads, n, _ = q.shape
    spec = group_spec(n, start)
    kernel = functools.partial(own_back_kernel, block=256)
    extra = () if into is None else tuple(into)
    return pl.pallas_call(
        kernel if into is None else lambda q, do, kv, _, __, *out: kernel(q, do, kv, *out),
        grid=(count // 2,),
        in_specs=[spec] * 3 + [ANYWHERE] * len(extra),
        out_specs=[spec] * 2,
        out_shape=[stored((heads, n, LANES), BF16)] * 2,
        input_output_aliases={3: 0, 4: 1} if extra else {},
        scratch_shapes=[pltpu.VMEM((LANES, n), F32)] * 2,
        compiler_params=params(24),
        cost_estimate=pl.CostEstimate(
            flops=count * n * n * 2560, bytes_accessed=8 * 2**20, transcendentals=count * n * n
        ),
        name="own_back",
    )(far(q), far(do), far(kv), *extra)


def finish_q_kernel(
    place, dq_own, dq_peer, normed, wide, merged_c, merged_d, grad_low, out, grad_w, grad_b, nat0, nat1, acc, both, out_grad
):
    i = pl.program_id(0)
    n = nat0.shape[0]
    lane = lax.broadcasted_iota(jnp.int32, (n, LANES), 1)
    low = []
    for j, nat in enumerate((nat0, nat1)):
        unpermute(place[0] + 2 * i + j, j, (dq_own, dq_peer), nat)
        rows = jnp.where(lane < HD, nat[...] * (1.0 / ROOT), 0.0)
        grad_b[j, 0:1, :] = jnp.sum(rows, 0, keepdims=True)
        low.append(rows.astype(BF16))
    low = jnp.concatenate(low, axis=1)
    gradient = dot_lt(low, normed[...])
    grad_w[0, 0] = gradient[:HD].astype(BF16)
    grad_w[0, 1] = gradient[LANES : LANES + HD].astype(BF16)

    @pl.when(i == 0)
    def _():
        group = merged_c.shape[0]
        both[:group] = merged_c[...]
        both[group:] = merged_d[...]
        out_grad[...] = dot(both[...], grad_low[...]).astype(BF16)

    for j in range(2):
        at = pl.multiple_of((2 * i + j) * HD, HD)
        grad_w[1, j] = out_grad[pl.ds(at, HD), :]

    part = dot_rt(low, jnp.concatenate([wide[0], wide[1]], axis=1))

    @pl.when(i == 0)
    def _():
        acc[...] = part

    @pl.when(i > 0)
    def _():
        acc[...] += part

    @pl.when(i == pl.num_programs(0) - 1)
    def _():
        out[...] = acc[...].astype(BF16)


def unpermute(head, j, sources, nat):
    n = nat.shape[0]
    block = n // FOLD
    for p in range(FOLD):
        c = (head + ORDER[p]) % FOLD
        at = pl.ds(p * block, block)
        total = None
        for ref in sources:
            if p * block < ref.shape[1]:
                piece = ref[j, at, :].astype(F32)
                total = piece if total is None else total + piece
        nat[pl.ds(c, block, stride=FOLD), :] = total


def finish_kv_kernel(
    place, dkv_own, r_core, r_x, r_z1, r_z2, r_z3, normed, rows, wide, start, grad_one,
    grad_normed, keep, send, grad_b, sums, acc, nat0, nat1,
):
    i = pl.program_id(0)
    n, d = rows.shape
    lane = lax.broadcasted_iota(jnp.int32, (n, LANES), 1)
    low = []
    for j, nat in enumerate((nat0, nat1)):
        unpermute(place[0] + 2 * i + j, j, (dkv_own, r_core, r_x, r_z1, r_z2, r_z3), nat)
        both = nat[...]
        both = jnp.where(lane < HD, both * (1.0 / ROOT), jnp.where(lane < 2 * HD, both, 0.0))
        grad_b[j, 0:1, :] = jnp.sum(both, 0, keepdims=True)
        low.append(both.astype(BF16))
    low = jnp.concatenate(low, axis=1)
    gradient = dot_lt(low, normed[...])
    first = place[3] == 0
    for j in range(2):
        for k in range(2):
            one = grad_one[k, j]
            two = gradient[j * LANES + k * HD : j * LANES + (k + 1) * HD].astype(BF16)
            keep[k, j] = jnp.where(first, one, two)
            send[k, j] = jnp.where(first, two, one)
    part = dot_rt(low, jnp.concatenate([wide[0], wide[1]], axis=1))

    @pl.when(i == 0)
    def _():
        acc[...] = start[...].astype(F32) + part

    @pl.when(i > 0)
    def _():
        acc[...] += part

    @pl.when(i == pl.num_programs(0) - 1)
    def _():
        total = acc[...]
        grad_normed[...] = total.astype(BF16)
        unit, _ = unit_rows(rows[...].astype(F32))
        sums[0:1, :] = jnp.sum(total * unit, 0, keepdims=True)
        sums[1:2, :] = jnp.sum(total, 0, keepdims=True)
        sums[2:8, :] = jnp.zeros((6, d), F32)


def pairs(rows):
    return pl.BlockSpec((2, rows, LANES), lambda i: (i, 0, 0))


def finish_q(place, dq_own, dq_peer, normed, wide, merged, grad_low):
    heads, n, _ = dq_own.shape
    d = normed.shape[1]
    return pl.pallas_call(
        finish_q_kernel,
        grid=(heads // 2,),
        in_specs=[
            pl.BlockSpec(memory_space=pltpu.SMEM),
            pairs(n),
            pairs(n // 2),
            once((n, d)),
            pl.BlockSpec((2, d, LANES), lambda i: (i, 0, 0)),
            once(merged[0].shape),
            once(merged[1].shape),
            once((n, d)),
        ],
        out_specs=[
            full((n, d)),
            pl.BlockSpec((2, 2, HD, d), lambda i: (0, i, 0, 0)),
            pl.BlockSpec((2, 1, LANES), lambda i: (i, 0, 0)),
        ],
        out_shape=[
            stored((n, d), BF16),
            stored((2, heads, HD, d), BF16),
            shape((heads, 1, LANES), F32),
        ],
        scratch_shapes=[pltpu.VMEM((n, LANES), F32)] * 2
        + [
            pltpu.VMEM((n, d), F32),
            pltpu.VMEM((heads * HD, n), BF16),
            pltpu.VMEM((heads * HD, d), BF16),
        ],
        compiler_params=params(28),
        cost_estimate=pl.CostEstimate(
            flops=4 * n * d * heads * 128, bytes_accessed=14 * 2**20, transcendentals=0
        ),
        name="finish_q",
    )(place, far(dq_own), far(dq_peer), normed, far(wide), *merged, grad_low)


def finish_kv(place, dkv_own, received, normed, rows, wide, start, grad_one):
    heads, n, _ = dkv_own.shape
    d = normed.shape[1]
    return pl.pallas_call(
        finish_kv_kernel,
        grid=(heads // 2,),
        in_specs=[
            pl.BlockSpec(memory_space=pltpu.SMEM),
            pairs(n),
            pairs(n // 2),
            pairs(n // 4),
            pairs(n // 8),
            pairs(n // 16),
            pairs(n // 16),
            once((n, d)),
            once((n, d)),
            pl.BlockSpec((2, d, LANES), lambda i: (i, 0, 0)),
            once((n, d)),
            pl.BlockSpec((2, 2, HD, d), lambda i: (0, i, 0, 0)),
        ],
        out_specs=[
            full((n, d)),
            pl.BlockSpec((2, 2, HD, d), lambda i: (0, i, 0, 0)),
            pl.BlockSpec((2, 2, HD, d), lambda i: (0, i, 0, 0)),
            pl.BlockSpec((2, 1, LANES), lambda i: (i, 0, 0)),
            full((8, d)),
        ],
        out_shape=[
            shape((n, d), BF16),
            stored((2, heads, HD, d), BF16),
            shape((2, heads, HD, d), BF16),
            shape((heads, 1, LANES), F32),
            shape((8, d), F32),
        ],
        scratch_shapes=[pltpu.VMEM((n, d), F32)] + [pltpu.VMEM((n, LANES), F32)] * 2,
        compiler_params=params(36),
        cost_estimate=pl.CostEstimate(
            flops=4 * n * d * heads * 128, bytes_accessed=20 * 2**20, transcendentals=0
        ),
        name="finish_kv",
    )(place, far(dkv_own), *received, normed, rows, far(wide), far(start), far(grad_one))


def spread_kernel(place, own, peer, down, up):
    first = place[3] == 0
    down[...] = jnp.where(first, own[...], peer[...]).astype(F32)
    up[...] = jnp.where(first, peer[...], own[...]).astype(F32).T


def spread(place, own, peer):
    ff, d = own.shape
    block = 256
    rows = pl.BlockSpec((block, d), lambda i: (i, 0))
    return pl.pallas_call(
        spread_kernel,
        grid=(ff // block,),
        in_specs=[pl.BlockSpec(memory_space=pltpu.SMEM), rows, rows],
        out_specs=[rows, pl.BlockSpec((d, block), lambda i: (0, i))],
        out_shape=[shape((ff, d), F32), shape((d, ff), F32)],
        compiler_params=params(12),
        name="spread",
    )(place, own, peer)


def spread_qkv_kernel(place, own, peer, qkv, out):
    i = pl.program_id(0)
    first = place[3] == 0
    width = qkv.shape[2]

    def piece(on_first, at):
        mine = first == on_first
        return jnp.where(mine, own[at], peer[at]).astype(F32)

    lower, upper = slice(0, width), slice(width, 2 * width)

    @pl.when(i == 0)
    def _():
        qkv[0] = piece(True, lower).T

    @pl.when(i == 1)
    def _():
        qkv[0] = piece(False, lower).T

    @pl.when(i == 2)
    def _():
        qkv[0] = piece(False, upper).T
        out[...] = piece(True, upper)


def spread_qkv(place, own, peer):
    half, d = own.shape
    width = half // 2
    return pl.pallas_call(
        spread_qkv_kernel,
        in_specs=[pl.BlockSpec(memory_space=pltpu.SMEM), once(own.shape), once(own.shape)],
        out_specs=[pl.BlockSpec((1, d, width), lambda i: (i, 0, 0)), full((width, d))],
        grid=(3,),
        out_shape=[shape((3, d, width), F32), shape((width, d), F32)],
        compiler_params=params(16),
        name="spread_qkv",
    )(place, own, peer)


def last_kernel(rows, own_g, peer_g, grad_hidden, gain, out):
    unit, inverse = unit_rows(rows[...].astype(F32))
    gradient = own_g[...].astype(F32) + peer_g[...].astype(F32)
    out[...] = grad_hidden[...] + norm_back(gradient, unit, inverse, gain[...])


def last(rows, own_g, peer_g, grad_hidden, gain):
    n, d = rows.shape
    part = pl.BlockSpec((256, d), lambda i: (i, 0))
    return pl.pallas_call(
        last_kernel,
        grid=(n // 256,),
        in_specs=[part] * 4 + [once((1, d))],
        out_specs=part,
        out_shape=shape((n, d), F32),
        compiler_params=params(12),
        cost_estimate=LIGHT,
        name="last",
    )(rows, own_g, peer_g, grad_hidden, gain)


def gather_small_kernel(sums1, sums_a, sums_b, sums_c, up_a, up_c, grad_bq, grad_bkv, out):
    heads = grad_bq.shape[0]
    d = out.shape[1]
    out[...] = jnp.zeros_like(out)
    out[0:2, :] = sums1[0:2, :]
    out[2:6, :] = sums_a[0:4, :] + sums_b[0:4, :] + sums_c[0:4, :]
    up = up_a[...] + up_c[...]
    for k in range(up.shape[1] // d):
        out[6 + k : 7 + k, :] = up[:, k * d : (k + 1) * d]
    row = [grad_bq[h, :, :HD] for h in range(heads)]
    row += [grad_bkv[h, :, HD : 2 * HD] for h in range(heads)]
    out[15:16, :] = jnp.concatenate(row, axis=1)


def gather_small(sums1, sums2, up_b, grad_bq, grad_bkv):
    d = sums1.shape[1]
    inputs = (sums1, *sums2, *up_b, grad_bq, grad_bkv)
    return pl.pallas_call(
        gather_small_kernel,
        grid=(1,),
        in_specs=[once(x.shape) for x in inputs],
        out_specs=full((FOLD, d)),
        out_shape=shape((FOLD, d), F32),
        compiler_params=params(4),
        cost_estimate=LIGHT,
        name="gather_small",
    )(*inputs)


def add_head(small, peer):
    return jnp.where(jnp.arange(small.shape[0])[:, None] < 2, small + peer, small)


def spread_small_kernel(small, gains, shifts, qv, out_b, up_b, down_b):
    d = small.shape[1]
    width = qv.shape[1]
    gains[0:1, :] = small[0:1, :]
    shifts[0:1, :] = small[1:2, :]
    gains[1:2, :] = small[2:3, :]
    shifts[1:2, :] = small[3:4, :]
    out_b[...] = small[4, :]
    down_b[...] = small[5, :]
    for k in range(up_b.shape[0] // d):
        up_b[k * d : (k + 1) * d] = small[6 + k, :]
    qv[0:1, :] = small[15:16, :width]
    qv[1:2, :] = small[15:16, width:]


def spread_small(small, ff):
    d = small.shape[1]
    dims = [(2, d), (2, d), (2, d // 2), (d,), (ff,), (d,)]
    return pl.pallas_call(
        spread_small_kernel,
        grid=(1,),
        in_specs=[once(small.shape)],
        out_specs=[full(x) for x in dims],
        out_shape=[shape(x, F32) for x in dims],
        compiler_params=params(4),
        cost_estimate=LIGHT,
        name="spread_small",
    )(small)


def swap(x, axis, apart):
    count = lax.axis_size(axis)
    return lax.ppermute(x, axis, [(i, i ^ apart) for i in range(count)])


def whole_call(kernel, place, inputs, outputs, name):
    return pl.pallas_call(
        kernel,
        grid=(1,),
        in_specs=[pl.BlockSpec(memory_space=pltpu.SMEM)] + [once(x.shape) for x in inputs],
        out_specs=[full(dims) for dims, _ in outputs],
        out_shape=[shape(dims, kind) for dims, kind in outputs],
        compiler_params=params(24),
        cost_estimate=LIGHT,
        name=name,
    )(place, *inputs)


def added(refs, at=slice(None)):
    total = refs[0][at, :].astype(F32)
    for ref in refs[1:]:
        total = total + ref[at, :].astype(F32)
    return total


def cut(index, count):
    return pl.ds(pl.multiple_of(index * count, count), count)


class Sum:
    def __init__(self, place, rows, width):
        self.place, self.rows, self.width = place, rows, width
        self.third, self.twelfth = rows // 3, rows // 12

    def call(self, kernel, inputs, outputs, name):
        dims = [((count, self.width), kind) for count, kind in outputs]
        return whole_call(kernel, self.place, inputs, dims, name)

    def start(self, keep, got):
        third, twelfth = self.third, self.twelfth

        def kernel(place, keep, got, m1, s1, m2, *s2):
            side, line = place[4], place[5]
            m1[...] = added((keep, got), cut(side, third))
            s1[...] = added((keep, got), cut(1 - side, third)).astype(BF16)

            def quarter(k):
                at = pl.multiple_of(2 * third + (line ^ k) * twelfth, twelfth)
                return added((keep, got), pl.ds(at, twelfth))

            m2[...] = quarter(0)
            for k in (1, 2, 3):
                s2[k - 1][...] = quarter(k).astype(BF16)

        return self.call(
            kernel,
            (keep, got),
            [(third, F32), (third, BF16), (twelfth, F32)] + [(twelfth, BF16)] * 3,
            "start_sum",
        )

    def send1(self, state):
        m1, s1, m2, *s2 = state
        got = swap(s1, "seq", 2)
        return (m1, m2, got) + tuple(swap(x, "seq", 4 * k) for k, x in zip((1, 2, 3), s2))

    def middle(self, state):
        twelfth = self.twelfth

        def kernel(place, m1, m2, g1, ga, gb, gc, n1, n2, s2, *s1):
            side, line = place[4], place[5]
            n1[...] = added((m1, g1), cut(line, twelfth))
            for k in (1, 2, 3):
                s1[k - 1][...] = added((m1, g1), cut(line ^ k, twelfth)).astype(BF16)
            n2[...] = added((m2, ga, gb, gc), cut(side, twelfth // 2))
            s2[...] = added((m2, ga, gb, gc), cut(1 - side, twelfth // 2)).astype(BF16)

        return self.call(
            kernel,
            state,
            [(twelfth, F32), (twelfth // 2, F32), (twelfth // 2, BF16)] + [(twelfth, BF16)] * 3,
            "middle_sum",
        )

    def send2(self, state):
        n1, n2, s2, *s1 = state
        got = tuple(swap(x, "seq", 4 * k) for k, x in zip((1, 2, 3), s1))
        return (n1, n2) + got + (swap(s2, "seq", 2),)

    def end(self, state):
        twelfth = self.twelfth

        def kernel(place, n1, n2, ga, gb, gc, g2, one, two):
            one[...] = added((n1, ga, gb, gc)).astype(BF16)
            two[...] = added((n2, g2)).astype(BF16)

        pair = self.call(kernel, state, [(twelfth, BF16), (twelfth // 2, BF16)], "end_sum")
        return tuple(self.beyond(x) for x in pair)

    def beyond(self, low):
        apart = FOLD
        while apart < lax.axis_size("seq"):
            low = (low.astype(F32) + swap(low, "seq", apart).astype(F32)).astype(BF16)
            apart *= 2
        return low

    def send3(self, pair):
        one, two = pair
        got = tuple(swap(one, "seq", 4 * k) for k in (1, 2, 3))
        return (one, two) + got + (swap(two, "seq", 2),)

    def join(self, state):
        twelfth, third = self.twelfth, self.third

        def kernel(place, one, two, ga, gb, gc, g2, out1, out2):
            side, line = place[4], place[5]
            for k, ref in enumerate((one, ga, gb, gc)):
                out1[cut(line ^ k, twelfth), :] = ref[...]
            out2[cut(side, twelfth // 2), :] = two[...]
            out2[cut(1 - side, twelfth // 2), :] = g2[...]

        return self.call(kernel, state, [(third, BF16), (twelfth, BF16)], "join_sum")

    def send4(self, pair):
        one, two = pair
        got = swap(one, "seq", 2)
        return (one, two, got) + tuple(swap(two, "seq", 4 * k) for k in (1, 2, 3))

    def whole(self, state):
        twelfth, third = self.twelfth, self.third

        def kernel(place, one, two, g1, ga, gb, gc, out):
            side, line = place[4], place[5]
            out[cut(side, third), :] = one[...]
            out[cut(1 - side, third), :] = g1[...]
            for k, ref in enumerate((two, ga, gb, gc)):
                at = pl.multiple_of(2 * third + (line ^ k) * twelfth, twelfth)
                out[pl.ds(at, twelfth), :] = ref[...]

        return self.call(kernel, state, [(self.rows, BF16)], "whole_sum")[0]


class LineSum(Sum):
    def __init__(self, place, rows, width):
        self.place, self.rows, self.width = place, rows, width
        self.half, self.eighth = rows // 2, rows // 8

    def start(self, keep, got):
        half = self.half

        def kernel(place, keep, got, mine, *sends):
            mine[...] = added((keep, got), cut(place[4], half))
            for k, send in enumerate(sends):
                at = cut(2 * (1 - place[4]) + k, half // 2)
                send[...] = added((keep, got), at).astype(BF16)

        outputs = [(half, F32)] + [(half // 2, BF16)] * 2
        return self.call(kernel, (keep, got), outputs, "start_line")

    def near(self, mine, one, two):
        eighth = self.eighth

        def kernel(place, mine, one, two, keep, send):
            parity = place[5] % 2
            for high, got in enumerate((one, two)):
                out = pl.ds(high * eighth, eighth)

                def piece(low):
                    at = pl.multiple_of((2 * high + low) * eighth, eighth)
                    return mine[pl.ds(at, eighth), :] + got[cut(low, eighth), :].astype(F32)

                keep[out, :] = piece(parity)
                send[out, :] = piece(1 - parity).astype(BF16)

        outputs = [(2 * eighth, F32), (2 * eighth, BF16)]
        return self.call(kernel, (mine, one, two), outputs, "near_line")

    def across(self, keep, got):
        eighth = self.eighth

        def kernel(place, keep, got, mine, send):
            high = place[5] // 2
            mine[...] = added((keep, got), cut(high, eighth))
            send[...] = added((keep, got), cut(1 - high, eighth)).astype(BF16)

        outputs = [(eighth, F32), (eighth, BF16)]
        return self.call(kernel, (keep, got), outputs, "across_line")

    def end(self, mine, got):
        def kernel(place, mine, got, out):
            out[...] = added((mine, got)).astype(BF16)

        outputs = [(self.eighth, BF16)]
        return self.beyond(self.call(kernel, (mine, got), outputs, "end_line")[0])

    def join_across(self, mine, got):
        eighth = self.eighth

        def kernel(place, mine, got, out):
            high = place[5] // 2
            out[cut(high, eighth), :] = mine[...]
            out[cut(1 - high, eighth), :] = got[...]

        return self.call(kernel, (mine, got), [(2 * eighth, BF16)], "join_across")[0]

    def join_near(self, mine, got):
        eighth = self.eighth

        def kernel(place, mine, got, one, two, three):
            parity = place[5] % 2
            low, high = pl.ds(0, eighth), pl.ds(eighth, eighth)
            one[cut(parity, eighth), :] = mine[low, :]
            one[cut(1 - parity, eighth), :] = got[low, :]
            even = parity == 0
            two[...] = jnp.where(even, mine[high, :], got[high, :])
            three[...] = jnp.where(even, got[high, :], mine[high, :])

        outputs = [(2 * eighth, BF16), (eighth, BF16), (eighth, BF16)]
        return self.call(kernel, (mine, got), outputs, "join_near")

    def whole(self, mine, got):
        half, eighth = self.half, self.eighth

        def kernel(place, *refs):
            *parts, out = refs
            for side, group in ((place[4], parts[:3]), (1 - place[4], parts[3:])):
                at = 0
                for ref in group:
                    count = ref.shape[0]
                    out[pl.ds(pl.multiple_of(side * half + at, eighth), count), :] = ref[...]
                    at += count

        return self.call(kernel, (*mine, *got), [(self.rows, BF16)], "whole_line")[0]


def send_home(place, kept, r_core):
    heads, rows, lanes = kept.shape
    quarter = rows // 3
    half = r_core.shape[1] - rows

    def kernel(place, kept, r_core, far, near, stay):
        def both(k):
            return kept[:, cut(k, quarter), :] + r_core[
                :, pl.ds(half + k * quarter, quarter), :
            ].astype(F32)

        near[...] = both(0).astype(BF16)
        stay[...] = both(1)
        far[...] = both(2).astype(BF16)

    dims = (heads, quarter, lanes)
    return whole_call(
        kernel, place, (kept, r_core), [(dims, BF16), (dims, BF16), (dims, F32)], "send_home"
    )


def send_line(place, stay, got):
    heads, rows, lanes = stay.shape

    def kernel(place, stay, got, z1, z2, z3):
        def both(start, count):
            at = pl.ds(start, count)
            return (stay[:, at, :] + got[:, at, :].astype(F32)).astype(BF16)

        z1[...] = both(0, rows // 2)
        z2[...] = both(rows // 2, rows // 4)
        z3[...] = both(3 * rows // 4, rows // 4)

    return whole_call(
        kernel,
        place,
        (stay, got),
        [((heads, count, lanes), BF16) for count in (rows // 2, rows // 4, rows // 4)],
        "send_line",
    )


def tie(*xs):
    return lax.optimization_barrier(xs)


def sum_small(x, apart):
    while apart < lax.axis_size("seq"):
        x = x + swap(x, "seq", apart)
        apart *= 2
    return x


def local(
    rows,
    lengths,
    norm_gains,
    norm_shifts,
    qkv_weight,
    qv_bias,
    out_weight,
    out_bias,
    up_weight,
    up_bias,
    down_weight,
    down_bias,
    out_cot,
):
    n, d = rows.shape
    width = qkv_weight.shape[2]
    heads = width // HD
    seq_place = lax.axis_index("seq")
    head_place = lax.axis_index("head")
    slide_rows = min(FOLD * SEG, n * lax.axis_size("seq"))
    start = seq_place * n
    slide = start // slide_rows
    length = jnp.sum(jnp.where(jnp.arange(lengths.shape[0]) == slide, lengths, 0))
    limit = jnp.clip(length - start % slide_rows, 0, n)
    place = jnp.stack(
        [
            head_place * heads,
            limit,
            head_place,
            seq_place % 2,
            seq_place // 2 % 2,
            seq_place // 4 % 4,
        ]
    ).astype(jnp.int32)
    half, quarter, eighth = n // 2, n // 4, n // 8
    first_heads = heads // 2

    peer_out_weight = swap(out_weight, "head", 1)
    wide_out = jnp.pad(
        out_weight.reshape(heads, HD, d), ((0, 0), (HD, LANES - 2 * HD), (0, 0))
    ).reshape(heads * LANES, d)

    kv, s1, sx, sz1, sz, normed1, wide_kv = project_kv(
        place, rows, norm_gains[:1], norm_shifts[:1], qkv_weight, qv_bias
    )
    rz1 = swap(sz1, "seq", 4)
    rx = swap(sx, "seq", 2)
    rz2 = swap(sz, "seq", 8)
    rz3 = swap(sz, "seq", 12)
    cs1 = swap(s1, "seq", 1)
    q, wide_q = project_q(place, normed1, qkv_weight, qv_bias)
    q, rz1, rz2, rz3 = tie(q, rz1, rz2, rz3)
    zc = jnp.concatenate([rz1, rz2, rz3], 1)
    rx2 = swap(zc, "seq", 2)
    crx = swap(rx, "seq", 1)
    czc = swap(zc, "seq", 1)
    own = own_attention(q, kv, 0, first_heads)
    own = own_attention(q, kv, first_heads, heads - first_heads, own)
    own, rx2, crx, czc, cs1, peer_out_weight = tie(own, rx2, crx, czc, cs1, peer_out_weight)
    crx2 = swap(rx2, "seq", 1)
    received = (cs1, rx, crx, zc, rx2, czc, crx2)
    *state, low_one = peers_attention(place, q, own, received, 0, first_heads)
    peer_low_one = swap(low_one, "head", 1)
    *state, low_two = peers_attention(
        place, q, own, received, first_heads, heads - first_heads, state
    )
    merged, kv_all, qb = state
    merged, low_two, peer_low_one = tie(merged, low_two, peer_low_one)
    merged_low = (low_one, low_two)
    peer_low = (peer_low_one, swap(low_two, "head", 1))

    def feed_rows(start, sizes, into):
        return feed(
            place,
            rows,
            out_cot,
            merged_low + peer_low,
            out_weight,
            peer_out_weight,
            out_bias[None],
            norm_gains[1:],
            norm_shifts[1:],
            up_weight,
            up_bias[None],
            down_weight,
            start,
            sizes,
            into,
        )

    *fed, g2_a, ub_one = feed_rows(0, (quarter,), None)
    peer_a = swap(g2_a, "head", 1)
    *fed, g2_b, g2_c, ub_two = feed_rows(quarter, (quarter, half), fed)
    *fed, peer_a = tie(*fed, peer_a)
    hidden, normed2, act, grad_pre = fed
    peer_b = swap(g2_b, "head", 1)
    mlp, keep, send = weights(place, act, grad_pre, normed2, out_cot, down_weight)
    peer_b, mlp, keep, send = tie(peer_b, mlp, keep, send)

    def turn_rows(own_g, peer_g, start, into):
        count = own_g.shape[0]
        return turn(out_cot, own_g, peer_g, hidden, norm_gains[1:], wide_out, start, count, into)

    ff = up_bias.shape[0]
    sums = LineSum(place, ff, d)
    peer_c = swap(g2_c, "head", 1)
    ff_mine, *ff_send = sums.start(keep, swap(send, "seq", 1))
    ff_got = [swap(ff_send[0], "seq", 2)]
    *turned, sums2_a = turn_rows(g2_a, peer_a, 0, None)
    *turned, sums2_b = turn_rows(g2_b, peer_b, quarter, turned)
    peer_c, ff_mine, ff_send[1], *turned, ff_got[0] = tie(
        peer_c, ff_mine, ff_send[1], *turned, ff_got[0]
    )
    ff_got += [swap(ff_send[1], "seq", 2)]
    grad_hidden, grad_low, gm, sums2_c = turn_rows(g2_c, peer_c, half, turned)
    back = peers_back(place, gm, merged, qb, kv_all, 0, first_heads)
    *back, ff_mine, ff_got[0], ff_got[1] = tie(*back, ff_mine, *ff_got)
    ff_mine, ff_send = sums.near(ff_mine, *ff_got)
    ff_got = swap(ff_send, "seq", 4)
    peer_mlp = swap(mlp, "head", 1)
    back = peers_back(
        place, gm, merged, qb, kv_all, first_heads, heads - first_heads, back
    )
    do, dq_peer, to_core, kept, ff_mine, ff_got = tie(*back, ff_mine, ff_got)
    r_core = swap(to_core, "seq", 1)
    ff_mine, ff_send = sums.across(ff_mine, ff_got)
    ff_got = swap(ff_send, "seq", 8)
    back = own_back(qb, do, kv, 0, first_heads)
    dq_own, dkv_own, r_core, ff_mine, ff_got = tie(*back, r_core, ff_mine, ff_got)
    far_rows, near_rows, stay = send_home(place, kept, r_core)
    r_x2 = swap(far_rows, "seq", 2)
    r_x = swap(near_rows, "seq", 2)
    ff_mine = sums.end(ff_mine, ff_got)
    ff_got = swap(ff_mine, "seq", 8)
    back = own_back(qb, do, kv, first_heads, heads - first_heads, (dq_own, dkv_own))
    dq_own, dkv_own, r_x2, ff_mine, ff_got = tie(*back, r_x2, ff_mine, ff_got)
    z1, z2, z3 = send_line(place, stay, r_x2)
    r_z1 = swap(z1, "seq", 4)
    r_z2 = swap(z2, "seq", 8)
    r_z3 = swap(z3, "seq", 12)
    ff_mine = sums.join_across(ff_mine, ff_got)
    ff_got = swap(ff_mine, "seq", 4)
    start_g, grad_one, grad_bq = finish_q(
        place, dq_own, dq_peer, normed1, wide_q, merged_low, grad_low
    )
    start_g, grad_one, peer_mlp, r_x, r_z1, r_z2, r_z3, ff_mine, ff_got = tie(
        start_g, grad_one, peer_mlp, r_x, r_z1, r_z2, r_z3, ff_mine, ff_got
    )
    out_rows = (
        hidden + ((mlp.astype(F32) + peer_mlp.astype(F32)) + down_bias)
    ).astype(BF16)
    ff_mine = sums.join_near(ff_mine, ff_got)
    ff_got = [swap(ff_mine[0], "seq", 2)]
    grad_normed1, keep, send, grad_bkv, sums1 = finish_kv(
        place, dkv_own, (r_core, r_x, r_z1, r_z2, r_z3), normed1, rows, wide_kv, start_g, grad_one
    )
    keep, send, sums1, out_rows, grad_normed1, ff_got[0], *ff_mine = tie(
        keep, send, sums1, out_rows, grad_normed1, ff_got[0], *ff_mine
    )

    count = 2 * width
    keep, send = keep.reshape(count, d), send.reshape(count, d)
    got = swap(send, "seq", 1)
    peer_normed1 = swap(grad_normed1, "head", 1)
    small = gather_small(sums1, (sums2_a, sums2_b, sums2_c), (ub_one, ub_two), grad_bq, grad_bkv)
    keep, got, small = tie(keep, got, small)
    w_sums = Sum(place, count, d)
    state = w_sums.send1(w_sums.start(keep, got))
    small = small + swap(small, "seq", 1)
    *state, small, ff_mine[1] = tie(*state, small, ff_mine[1])
    state = w_sums.send2(w_sums.middle(state))
    small = small + swap(small, "seq", 4)
    ff_got += [swap(ff_mine[1], "seq", 2)]
    *state, small, ff_got[1], ff_mine[2] = tie(*state, small, ff_got[1], ff_mine[2])
    ff_got += [swap(ff_mine[2], "seq", 2)]
    state = w_sums.send3(w_sums.end(state))
    small = small + swap(small, "seq", 2)
    rows_grad = last(rows, grad_normed1, peer_normed1, grad_hidden, norm_gains[:1])
    ff_own = sums.whole(ff_mine, ff_got)
    *state, small, rows_grad, ff_own = tie(*state, small, rows_grad, ff_own)
    state = w_sums.send4(w_sums.join(state))
    peer_small = swap(small, "head", 1)
    down_weight_grad, up_weight_grad = spread(place, ff_own, swap(ff_own, "seq", 1))
    *state, small, peer_small, down_weight_grad = tie(
        *state, small, peer_small, down_weight_grad
    )
    w_own = w_sums.whole(state)
    w_peer = swap(w_own, "seq", 1)
    gains_grad, shifts_grad, qv_bias_grad, out_bias_grad, up_bias_grad, down_bias_grad = (
        spread_small(sum_small(add_head(small, peer_small), 8), ff)
    )
    qkv_grad, out_weight_grad = spread_qkv(place, w_own, w_peer)
    return (
        out_rows,
        rows_grad,
        gains_grad,
        shifts_grad,
        qkv_grad,
        qv_bias_grad,
        out_weight_grad,
        out_bias_grad,
        up_weight_grad,
        up_bias_grad,
        down_weight_grad,
        down_bias_grad,
    )


def solution(mesh):
    placed = (
        P("seq", None),
        P(),
        P(),
        P(),
        P(None, None, "head"),
        P(None, "head"),
        P("head", None),
        P(),
        P(None, "head"),
        P("head"),
        P("head", None),
        P(),
        P("seq", None),
    )
    return jax.shard_map(
        local,
        mesh=mesh,
        in_specs=placed,
        out_specs=(
            P("seq", None),
            P("seq", None),
            P(),
            P(),
            P(None, None, "head"),
            P(None, "head"),
            P("head", None),
            P(),
            P(None, "head"),
            P("head"),
            P("head", None),
            P(),
        ),
        check_vma=False,
    )
```

```python
import functools
import math

import jax
import jax.numpy as jnp
import numpy as np
from jax import lax
from jax.experimental import pallas as pl
from jax.experimental.pallas import tpu as pltpu
from jax.sharding import PartitionSpec as P

HD = 48
SEG = 1024
LANES = 128
LEVELS = 5
FOLD = 16

EPS = 1e-05
ROOT = math.sqrt(HD)
EXP_SCALE = math.log2(math.e) / ROOT
ROOT_HALF = 1.0 / math.sqrt(2.0)
DENSITY_NORM = 1.0 / math.sqrt(2.0 * math.pi)
ABSENT = -1e20

ONE = 96
MASK = 99
MULT = 100
TOP = 127

ORDER = (0, 8, 4, 12, 2, 6, 10, 14, 1, 3, 5, 7, 9, 11, 13, 15)
CLASS = (4, 3, 2, 2, 1, 1, 1, 1, 0, 0, 0, 0, 0, 0, 0, 0)

F32 = jnp.float32
BF16 = jnp.bfloat16


LIGHT = pl.CostEstimate(flops=0, bytes_accessed=0, transcendentals=0)


def params(mib=48):
    return pltpu.CompilerParams(vmem_limit_bytes=mib * 2**20)


def dot(left, right):
    return jnp.dot(left, right, preferred_element_type=F32)


def dot_rt(left, right):
    return lax.dot_general(left, right, (((1,), (1,)), ((), ())), preferred_element_type=F32)


def dot_lt(left, right):
    return lax.dot_general(left, right, (((0,), (0,)), ((), ())), preferred_element_type=F32)


def full(shape):
    return pl.BlockSpec(shape, lambda *_: (0,) * len(shape))


def once(shape):
    return pl.BlockSpec(shape, lambda *_: (0,) * len(shape), pipeline_mode=pl.Buffered(1))


def per_head(rows, lanes=LANES):
    return pl.BlockSpec((1, rows, lanes), lambda h: (h, 0, 0))


def shape(dims, kind):
    return jax.ShapeDtypeStruct(dims, kind)


def stored(dims, kind):
    return pltpu.HBM(dims, kind)


def far(x):
    return pltpu.with_memory_space_constraint(x, pltpu.HBM)


def split3(x):
    high = x.astype(BF16).astype(F32)
    rest = x - high
    middle = rest.astype(BF16).astype(F32)
    return high, middle, rest - middle


def with_terms(block, lane, terms):
    high, middle, low = split3(terms)
    block = jnp.where(lane == ONE, high, block)
    block = jnp.where(lane == ONE + 1, middle, block)
    return jnp.where(lane == ONE + 2, low, block)


def unit_rows(x):
    mean = jnp.mean(x, -1, keepdims=True)
    centred = x - mean
    inverse = lax.rsqrt(jnp.mean(centred * centred, -1, keepdims=True) + EPS)
    return centred * inverse, inverse


def norm_back(gradient, unit, inverse, gain):
    z = gradient * gain
    return inverse * (
        z - jnp.mean(z, -1, keepdims=True) - unit * jnp.mean(z * unit, -1, keepdims=True)
    )


def mult_table(level, blocks):
    table = np.zeros((len(blocks), LANES), np.float32)
    for row, key_class in enumerate(blocks):
        for j in range(level + 1, key_class + 1):
            value = np.float32(ROOT * math.log((j - level + 1) / (j - level)))
            high = np.float32(value.astype(jnp.bfloat16))
            table[row, MULT + j - 1] = high
            table[row, MULT + 4 + j - 1] = np.float32((value - high).astype(jnp.bfloat16))
    return table


def flag_table():
    table = np.zeros((FOLD, LANES), np.float32)
    for row, level in enumerate(CLASS):
        table[row, MULT : MULT + level] = 1.0
        table[row, MULT + 4 : MULT + 4 + level] = 1.0
    return table


def permuted(head, tmp):
    n = tmp.shape[0]
    block = n // FOLD
    for p in range(FOLD):
        c = (head + ORDER[p]) % FOLD
        yield p, pl.ds(p * block, block), slice(p, p + 1), tmp[pl.ds(c, block, stride=FOLD), :]


def project_kv_kernel(
    place, rows, gain, shift, w, bias, table,
    kv, s1, sx, sz1, sz, normed, wide, w_tmp, b_tmp, extra, *tmps,
):
    i = pl.program_id(0)
    n, d = rows.shape
    heads = w.shape[2] // HD
    block = n // FOLD

    @pl.when(i == 0)
    def _():
        unit, _ = unit_rows(rows[...].astype(F32))
        normed[...] = (unit * gain[...] + shift[...]).astype(BF16)
        lane = lax.broadcasted_iota(jnp.int32, (n, LANES), 1)
        here = lax.broadcasted_iota(jnp.int32, (n, LANES), 0) < place[1]
        extra[...] = jnp.where(here | (lane != MASK), 0.0, ABSENT)

    for k in range(heads // 2):

        @pl.when(i == k)
        def _():
            for j in range(2):
                cut = slice((2 * k + j) * HD, (2 * k + j + 1) * HD)
                at = slice(LANES * j, LANES * (j + 1))
                w_tmp[:, at] = jnp.concatenate(
                    [w[1, :, cut], w[2, :, cut], jnp.zeros((d, LANES - 2 * HD), BF16)], axis=1
                )
                b_tmp[:, at] = jnp.concatenate(
                    [
                        jnp.zeros((1, HD), F32),
                        bias[1:2, cut],
                        jnp.ones((1, 3), F32),
                        jnp.zeros((1, LANES - 2 * HD - 3), F32),
                    ],
                    axis=1,
                )

    product = dot(normed[...], w_tmp[...]) + b_tmp[...]
    for j, tmp in enumerate(tmps):
        lanes = slice(LANES * j, LANES * (j + 1))
        wide[j] = w_tmp[:, lanes]
        tmp[...] = product[:, lanes] + extra[...]
        for p, at, row, kv_rows in permuted(place[0] + 2 * i + j, tmp):
            for level, out in enumerate((kv, s1, sx, sz1, sz)):
                if (p + 1) * block <= out.shape[1]:
                    row = slice(level * FOLD + p, level * FOLD + p + 1)
                    out[j, at, :] = (kv_rows + table[row, :]).astype(BF16)


def project_q_kernel(place, normed, w, bias, flags, q, wide, w_tmp, b_tmp, extra, *tmps):
    i = pl.program_id(0)
    n, d = normed.shape
    heads = w.shape[2] // HD

    @pl.when(i == 0)
    def _():
        lane = lax.broadcasted_iota(jnp.int32, (n, LANES), 1)
        here = lax.broadcasted_iota(jnp.int32, (n, LANES), 0) < place[1]
        extra[...] = jnp.where(here & (lane == MASK), 1.0, 0.0)

    for k in range(heads // 2):

        @pl.when(i == k)
        def _():
            for j in range(2):
                cut = slice((2 * k + j) * HD, (2 * k + j + 1) * HD)
                at = slice(LANES * j, LANES * (j + 1))
                w_tmp[:, at] = jnp.concatenate(
                    [w[0, :, cut], jnp.zeros((d, LANES - HD), BF16)], axis=1
                )
                b_tmp[:, at] = jnp.concatenate(
                    [bias[0:1, cut], jnp.zeros((1, LANES - HD), F32)], axis=1
                )

    product = dot(normed[...], w_tmp[...]) + b_tmp[...]
    for j, tmp in enumerate(tmps):
        lanes = slice(LANES * j, LANES * (j + 1))
        wide[j] = w_tmp[:, lanes]
        tmp[...] = product[:, lanes] + extra[...]
        for p, at, row, q_rows in permuted(place[0] + 2 * i + j, tmp):
            q[j, at, :] = (q_rows + flags[row, :]).astype(BF16)


def project_scratch(n, d):
    return [
        pltpu.VMEM((d, 2 * LANES), BF16),
        pltpu.VMEM((1, 2 * LANES), F32),
        pltpu.VMEM((n, LANES), F32),
    ] + [pltpu.VMEM((n, LANES), F32)] * 2


def project_kv(place, rows, gain, shift, w, bias):
    n, d = rows.shape
    heads = w.shape[2] // HD
    table = np.concatenate([mult_table(level, CLASS) for level in range(LEVELS)])
    sizes = (n, n // 2, n // 4, n // 8, n // 16)
    inputs = (rows, gain, shift, w, bias, jnp.asarray(table))
    return pl.pallas_call(
        project_kv_kernel,
        grid=(heads // 2,),
        in_specs=[pl.BlockSpec(memory_space=pltpu.SMEM)] + [once(x.shape) for x in inputs],
        out_specs=[group_spec(m) for m in sizes] + [full((n, d)), group_spec(d)],
        out_shape=[stored((heads, n, LANES), BF16)]
        + [shape((heads, m, LANES), BF16) for m in sizes[1:]]
        + [shape((n, d), BF16), stored((heads, d, LANES), BF16)],
        scratch_shapes=project_scratch(n, d),
        compiler_params=params(24),
        cost_estimate=pl.CostEstimate(
            flops=2 * n * d * heads * 128, bytes_accessed=9 * 2**20, transcendentals=0
        ),
        name="project_kv",
    )(place, *(far(x) for x in inputs))


def project_q(place, normed, w, bias):
    n, d = normed.shape
    heads = w.shape[2] // HD
    inputs = (normed, far(w), far(bias), jnp.asarray(flag_table()))
    return pl.pallas_call(
        project_q_kernel,
        grid=(heads // 2,),
        in_specs=[pl.BlockSpec(memory_space=pltpu.SMEM)] + [once(x.shape) for x in inputs],
        out_specs=[group_spec(n), group_spec(d)],
        out_shape=[stored((heads, n, LANES), BF16), stored((heads, d, LANES), BF16)],
        scratch_shapes=project_scratch(n, d),
        compiler_params=params(20),
        cost_estimate=pl.CostEstimate(
            flops=2 * n * d * heads * 128, bytes_accessed=6 * 2**20, transcendentals=0
        ),
        name="project_q",
    )(place, *inputs)


def own_kernel(q, kv, out, *, block):
    n = q.shape[1]
    lane = lax.broadcasted_iota(jnp.int32, (block, LANES), 1)
    steps = [(j, k * block) for j in range(q.shape[0]) for k in range(n // block)]

    def scores(j, at):
        return dot_rt(q[j, pl.ds(at, block), :], kv[j])

    now = scores(*steps[0])
    for index, (j, at) in enumerate(steps):
        later = scores(*steps[index + 1]) if index + 1 < len(steps) else None
        top = jnp.max(now, -1, keepdims=True)
        weights = jnp.exp2((now - top) * EXP_SCALE).astype(BF16)
        out[j, pl.ds(at, block), :] = jnp.where(lane == TOP, top, dot(weights, kv[j]))
        now = later


def group_spec(rows, start=0, lanes=LANES, heads=2):
    return pl.BlockSpec((heads, rows, lanes), lambda i: (i + start // heads, 0, 0))


ANYWHERE = pl.BlockSpec(memory_space=pl.ANY)


def own_attention(q, kv, start, count, into=None):
    heads, n, _ = q.shape
    spec = group_spec(n, start)
    kernel = functools.partial(own_kernel, block=256)
    extra = () if into is None else (into,)
    return pl.pallas_call(
        kernel if into is None else lambda q, kv, _, out: kernel(q, kv, out),
        grid=(count // 2,),
        in_specs=[spec] * 2 + [ANYWHERE] * len(extra),
        out_specs=spec,
        out_shape=shape((heads, n, LANES), F32),
        input_output_aliases={2: 0} if extra else {},
        compiler_params=params(12),
        cost_estimate=pl.CostEstimate(
            flops=count * n * n * 1024, bytes_accessed=4 * 2**20, transcendentals=count * n * n
        ),
        name="own_attention",
    )(far(q), far(kv), *extra)


def peers_kernel(
    place, q, own, cs1, rx, crx, zc, rx2, czc, crx2, pick, merged, kv_all, qb, low, nat, wide, *, start
):
    i = pl.program_id(0)
    n = q.shape[1]
    block = n // FOLD
    heads = q.shape[0]
    for j in range(heads):
        at = 0
        near = (zc, rx2, czc, crx2)
        pieces = [(cs1, 0, n // 2), (rx, 0, n // 4), (crx, 0, n // 4)]
        pieces += [(r, 0, n // 8) for r in near] + [(r, n // 8, n // 8) for r in near]
        for ref, begin, count in pieces:
            kv_all[j, pl.ds(at, count), :] = ref[j, pl.ds(begin, count), :]
            at += count

        head = place[0] + heads * i + j + start
        chunks = [
            (0, n // 16, 2 * n),
            (n // 16, n // 16, 3 * n // 2),
            (n // 8, n // 8, n),
            (n // 4, n // 4, n // 2),
            (n // 2, n // 2, 0),
        ]
        scores = []
        for begin, count, keys in chunks:
            if keys:
                scores.append(dot_rt(q[j, pl.ds(begin, count), :], kv_all[j, pl.ds(0, keys), :]))
            else:
                scores.append(None)
        for (begin, count, keys), s in zip(chunks, scores):
            rows = pl.ds(begin, count)
            lane = lax.broadcasted_iota(jnp.int32, (count, LANES), 1)
            o = own[j, rows, :]
            top = o[:, TOP : TOP + 1]
            if keys:
                new = jnp.maximum(top, jnp.max(s, -1, keepdims=True))
                weights = jnp.exp2((s - new) * EXP_SCALE).astype(BF16)
                o = o * jnp.exp2((top - new) * EXP_SCALE) + dot(weights, kv_all[j, pl.ds(0, keys), :])
                top = new
            total = o[:, ONE : ONE + 1]
            o = jnp.where((lane >= HD) & (lane < 2 * HD), o / total, 0.0)
            merged[j, rows, :] = o
            lse = top + jnp.log2(total) * (1.0 / EXP_SCALE)
            qb[j, rows, :] = with_terms(q[j, rows, :].astype(F32), lane, -lse).astype(BF16)
            for p in range(begin // block, (begin + count) // block):
                c = (head + ORDER[p]) % FOLD
                off = p * block - begin
                nat[pl.ds(c, block, stride=FOLD), :] = o[off : off + block]
        wide[:, pl.ds(pl.multiple_of((heads * i + j) * LANES, LANES), LANES)] = nat[...].astype(BF16)

    @pl.when(i == pl.num_programs(0) - 1)
    def _():
        low[...] = dot_rt(pick[...], wide[...]).astype(BF16)


def pick_values(heads):
    m = np.zeros((heads * HD, heads * LANES), np.float32)
    for h in range(heads):
        for j in range(HD):
            m[h * HD + j, h * LANES + HD + j] = 1.0
    return m


def peers_attention(place, q, own, received, start, count, into=None):
    heads, n, _ = q.shape
    pick = jnp.asarray(pick_values(count), BF16)
    extra = () if into is None else tuple(into)
    inputs = 4 + len(received)

    def kernel(*refs):
        peers_kernel(*refs[:inputs], *refs[inputs + len(extra) :], start=start)

    return pl.pallas_call(
        kernel,
        grid=(count,),
        in_specs=[
            pl.BlockSpec(memory_space=pltpu.SMEM),
            group_spec(n, start, heads=1),
            group_spec(n, start, heads=1),
        ]
        + [group_spec(r.shape[1], start, heads=1) for r in received]
        + [once(pick.shape)]
        + [ANYWHERE] * len(extra),
        out_specs=[group_spec(n, start, heads=1), group_spec(2 * n, start, heads=1), group_spec(n, start, heads=1)]
        + [full((count * HD, n))],
        out_shape=[
            stored((heads, n, LANES), F32),
            stored((heads, 2 * n, LANES), BF16),
            stored((heads, n, LANES), BF16),
            shape((count * HD, n), BF16),
        ],
        input_output_aliases={inputs + k: k for k in range(len(extra))},
        scratch_shapes=[pltpu.VMEM((n, LANES), F32), pltpu.VMEM((n, count * LANES), BF16)],
        compiler_params=params(28),
        cost_estimate=pl.CostEstimate(
            flops=count * n * n * 512, bytes_accessed=12 * 2**20, transcendentals=count * n * n // 2
        ),
        name="peers_attention",
    )(place, far(q), own, *received, pick, *extra)


def feed_kernel(
    place, rows, cot, own_c, own_d, peer_c, peer_d, own_w, peer_w, out_b, gain, shift, up_w, up_b, down_w,
    hidden, normed, act, grad_pre, *outs, sizes,
):
    *grad_normed, up_b_grad, w_tmp, c_tmp = outs
    i = pl.program_id(0)
    half = own_w.shape[0]
    group = own_c.shape[0]
    first = place[2] == 0

    @pl.when(i == 0)
    def _():
        w_tmp[:half] = jnp.where(first, own_w[...], peer_w[...])
        w_tmp[half:] = jnp.where(first, peer_w[...], own_w[...])

    c_tmp[:group] = jnp.where(first, own_c[...], peer_c[...])
    c_tmp[group:half] = jnp.where(first, own_d[...], peer_d[...])
    c_tmp[half : half + group] = jnp.where(first, peer_c[...], own_c[...])
    c_tmp[half + group :] = jnp.where(first, peer_d[...], own_d[...])
    attended = dot_lt(c_tmp[...], w_tmp[...])
    hid = rows[...].astype(F32) + (attended + out_b[...])
    hidden[...] = hid
    unit, _ = unit_rows(hid)
    low = (unit * gain[...] + shift[...]).astype(BF16)
    normed[...] = low
    pre = dot(low, up_w[...]) + up_b[...]
    phi = 0.5 * (1.0 + lax.erf(pre * ROOT_HALF))
    act[...] = (pre * phi).astype(BF16)
    slope = phi + pre * jnp.exp(-0.5 * pre * pre) * DENSITY_NORM
    gradient = dot_rt(cot[...], down_w[...]) * slope
    total = jnp.sum(gradient, 0, keepdims=True)

    @pl.when(i == 0)
    def _():
        up_b_grad[...] = total

    @pl.when(i > 0)
    def _():
        up_b_grad[...] += total

    gradient = gradient.astype(BF16)
    grad_pre[...] = gradient
    back = dot_rt(gradient, up_w[...]).astype(BF16)
    begin = 0
    for ref, steps in zip(grad_normed, sizes):

        @pl.when((i >= begin) & (i < begin + steps))
        def _():
            ref[...] = back

        begin += steps


def feed(
    place, rows, cot, merged, own_w, peer_w, out_b, gain, shift, up_w, up_b, down_w, start, sizes, into=None
):
    n, d = rows.shape
    block = 256
    count = sum(sizes)
    steps = [size // block for size in sizes]
    begins = [sum(steps[:k]) for k in range(len(steps))]
    ff = up_w.shape[1]
    half = own_w.shape[0]
    first = start // block
    extra = () if into is None else tuple(into)

    def part(lanes):
        return pl.BlockSpec((block, lanes), lambda i: (i + first, 0))

    def kernel(*refs):
        feed_kernel(*refs[:15], *refs[15 + len(extra) :], sizes=steps)

    return pl.pallas_call(
        kernel,
        grid=(count // block,),
        in_specs=[
            pl.BlockSpec(memory_space=pltpu.SMEM),
            part(d),
            part(d),
        ]
        + [pl.BlockSpec((m.shape[0], block), lambda i: (0, i + first)) for m in merged]
        + [
            once(own_w.shape),
            once(peer_w.shape),
            once((1, d)),
            once((1, d)),
            once((1, d)),
            once(up_w.shape),
            once((1, ff)),
            once(down_w.shape),
        ]
        + [ANYWHERE] * len(extra),
        out_specs=[
            part(d),
            part(d),
            part(ff),
            part(ff),
        ]
        + [
            pl.BlockSpec((block, d), lambda i, b=b, m=m: (jnp.clip(i - b, 0, m - 1), 0))
            for b, m in zip(begins, steps)
        ]
        + [full((1, ff))],
        out_shape=[
            shape((n, d), F32),
            shape((n, d), BF16),
            shape((n, ff), BF16),
            shape((n, ff), BF16),
        ]
        + [shape((size, d), BF16) for size in sizes]
        + [shape((1, ff), F32)],
        input_output_aliases={15 + k: k for k in range(len(extra))},
        scratch_shapes=[pltpu.VMEM((2 * half, d), BF16), pltpu.VMEM((2 * half, block), BF16)],
        compiler_params=params(30),
        cost_estimate=pl.CostEstimate(
            flops=2 * count * d * (ff * 3 + d),
            bytes_accessed=12 * 2**20,
            transcendentals=2 * count * ff,
        ),
        name="feed_forward",
    )(
        place, rows, cot, *merged, own_w, peer_w, out_b, gain, shift, up_w, up_b, down_w, *extra
    )


def weights_kernel(place, act, grad_pre, normed, cot, down_w, mlp, keep, send, acc):
    i = pl.program_id(0)
    part = dot(act[...], down_w[...])

    @pl.when(i == 0)
    def _():
        acc[...] = part

    @pl.when(i > 0)
    def _():
        acc[...] += part

    down = dot_lt(act[...], cot[...])
    up = dot_lt(grad_pre[...], normed[...])
    first = place[3] == 0
    keep[...] = jnp.where(first, down, up).astype(BF16)
    send[...] = jnp.where(first, up, down).astype(BF16)

    @pl.when(i == pl.num_programs(0) - 1)
    def _():
        mlp[...] = acc[...].astype(BF16)


def weights(place, act, grad_pre, normed, cot, down_w):
    n, ff = act.shape
    d = cot.shape[1]
    block = 256
    lanes = pl.BlockSpec((n, block), lambda i: (0, i))
    rows = pl.BlockSpec((block, d), lambda i: (i, 0))
    return pl.pallas_call(
        weights_kernel,
        grid=(ff // block,),
        in_specs=[
            pl.BlockSpec(memory_space=pltpu.SMEM),
            lanes,
            lanes,
            once((n, d)),
            once((n, d)),
            rows,
        ],
        out_specs=[full((n, d)), rows, rows],
        out_shape=[shape((n, d), BF16), shape((ff, d), BF16), shape((ff, d), BF16)],
        scratch_shapes=[pltpu.VMEM((n, d), F32)],
        compiler_params=params(26),
        cost_estimate=pl.CostEstimate(
            flops=6 * n * d * ff, bytes_accessed=20 * 2**20, transcendentals=0
        ),
        name="weights",
    )(place, act, grad_pre, normed, cot, down_w)


def turn_kernel(cot, own_g, peer_g, hidden, gain, out_w, grad_hidden, low_out, gm, sums):
    i = pl.program_id(0)
    unit, inverse = unit_rows(hidden[...])
    gradient = own_g[...].astype(F32) + peer_g[...].astype(F32)
    outer = cot[...].astype(F32)
    total = outer + norm_back(gradient, unit, inverse, gain[...])
    grad_hidden[...] = total
    low = total.astype(BF16)
    low_out[...] = low
    gm[...] = dot_rt(low, out_w[...]).astype(BF16).astype(F32)

    @pl.when(i == 0)
    def _():
        sums[...] = jnp.zeros_like(sums)

    sums[0:1, :] += jnp.sum(gradient * unit, 0, keepdims=True)
    sums[1:2, :] += jnp.sum(gradient, 0, keepdims=True)
    sums[2:3, :] += jnp.sum(total, 0, keepdims=True)
    sums[3:4, :] += jnp.sum(outer, 0, keepdims=True)


def turn(cot, own_g, peer_g, hidden, gain, out_w, start, count, into=None):
    n, d = cot.shape
    block = 256
    first = start // block
    wide = out_w.shape[0]
    extra = () if into is None else tuple(into)

    def part(lanes):
        return pl.BlockSpec((block, lanes), lambda i: (i + first, 0))

    own_part = pl.BlockSpec((block, d), lambda i: (i, 0))

    def kernel(*refs):
        turn_kernel(*refs[:6], *refs[6 + len(extra) :])

    return pl.pallas_call(
        kernel,
        grid=(count // block,),
        in_specs=[part(d), own_part, own_part, part(d), once((1, d)), once((wide, d))]
        + [ANYWHERE] * len(extra),
        out_specs=[part(d), part(d), part(wide), full((8, d))],
        out_shape=[
            stored((n, d), F32),
            stored((n, d), BF16),
            stored((n, wide), F32),
            shape((8, d), F32),
        ],
        input_output_aliases={6 + k: k for k in range(len(extra))},
        compiler_params=params(16),
        cost_estimate=LIGHT,
        name="turn",
    )(cot, own_g, peer_g, hidden, gain, out_w, *extra)


def pair_back(keys, q, do):
    weights = jnp.exp2(dot_rt(keys, q) * EXP_SCALE)
    inner = (weights * dot_rt(keys, do)).astype(BF16)
    grad_keys = dot(weights.astype(BF16), do) + dot(inner, q)
    return grad_keys, dot(keys.T, inner)


def peers_back_kernel(
    place, gm, merged, q, kv_all, do, dq, to_core, kept, acc, *, start
):
    half = q.shape[1]
    n = 2 * half
    block = n // FOLD
    lane = lax.broadcasted_iota(jnp.int32, (block, LANES), 1)
    for j in range(q.shape[0]):
        head = place[0] + pl.program_id(0) + start
        for p in range(FOLD):
            c = (head + ORDER[p]) % FOLD
            at = pl.ds(p * block, block)
            gradient = gm[pl.ds(c, block, stride=FOLD), :]
            delta = jnp.sum(gradient * merged[j, at, :], -1, keepdims=True)
            do[j, at, :] = with_terms(gradient, lane, -delta).astype(BF16)
        for level in (1, 2, 3, 4):
            count = n >> level
            begin = (level - 1) * half
            for k in range(0, half, 256):
                grad, grad_q = pair_back(
                    kv_all[j, pl.ds(begin + k, 256), :], q[j, pl.ds(0, count), :], do[j, pl.ds(0, count), :]
                )
                if level == 1:
                    to_core[j, pl.ds(k, 256), :] = grad.astype(BF16)
                elif level == 2:
                    if k == 0:
                        kept[j, pl.ds(0, 256), :] = grad
                    else:
                        to_core[j, pl.ds(half, 256), :] = grad.astype(BF16)
                else:
                    unit = 256 >> 1
                    off = 0 if level == 3 else unit
                    one, two = grad[:unit], grad[unit:]
                    if k == 0:
                        kept[j, pl.ds(256 + off, unit), :] = one
                        kept[j, pl.ds(512 + off, unit), :] = two
                    else:
                        to_core[j, pl.ds(half + 256 + off, unit), :] = one.astype(BF16)
                        to_core[j, pl.ds(half + 512 + off, unit), :] = two.astype(BF16)
                if count >= LANES:
                    if level == 1 and k == 0:
                        acc[...] = grad_q
                    else:
                        acc[:, :count] += grad_q
                else:
                    acc[:, :LANES] += jnp.concatenate(
                        [grad_q, jnp.zeros((LANES, LANES - count), F32)], axis=1
                    )
        dq[j] = acc[...].T.astype(BF16)


def peers_back(place, gm, merged, q, kv_all, start, count, into=None):
    heads, n, _ = q.shape
    assert n == SEG
    extra = () if into is None else tuple(into)

    def kernel(*refs):
        peers_back_kernel(*refs[:5], *refs[5 + len(extra) :], start=start)

    return pl.pallas_call(
        kernel,
        grid=(count,),
        in_specs=[
            pl.BlockSpec(memory_space=pltpu.SMEM),
            pl.BlockSpec((n, LANES), lambda i: (0, i + start)),
            group_spec(n, start, heads=1),
            group_spec(n // 2, start, heads=1),
            group_spec(2 * n, start, heads=1),
        ]
        + [ANYWHERE] * len(extra),
        out_specs=[group_spec(n, start, heads=1), group_spec(n // 2, start, heads=1), group_spec(n + n // 4, start, heads=1), group_spec(3 * n // 4, start, heads=1)],
        out_shape=[
            stored((heads, n, LANES), BF16),
            stored((heads, n // 2, LANES), BF16),
            shape((heads, n + n // 4, LANES), BF16),
            shape((heads, 3 * n // 4, LANES), F32),
        ],
        input_output_aliases={5 + k: k for k in range(len(extra))},
        scratch_shapes=[pltpu.VMEM((LANES, n // 2), F32)],
        compiler_params=params(16),
        cost_estimate=pl.CostEstimate(
            flops=count * n * n * 1280, bytes_accessed=24 * 2**20, transcendentals=count * n * n // 2
        ),
        name="peers_back",
    )(place, far(gm), far(merged), far(q), far(kv_all), *extra)


def own_back_kernel(q, do, kv, dq, dkv, *accs, block):
    n = q.shape[1]
    for j, acc in enumerate(accs):
        for i in range(n // block):
            at = pl.ds(i * block, block)
            grad, grad_q = pair_back(kv[j, at, :], q[j], do[j])
            dkv[j, at, :] = grad.astype(BF16)
            if i == 0:
                acc[...] = grad_q
            else:
                acc[...] += grad_q
        dq[j] = acc[...].T.astype(BF16)


def own_back(q, do, kv, start, count, into=None):
    heads, n, _ = q.shape
    spec = group_spec(n, start)
    kernel = functools.partial(own_back_kernel, block=256)
    extra = () if into is None else tuple(into)
    return pl.pallas_call(
        kernel if into is None else lambda q, do, kv, _, __, *out: kernel(q, do, kv, *out),
        grid=(count // 2,),
        in_specs=[spec] * 3 + [ANYWHERE] * len(extra),
        out_specs=[spec] * 2,
        out_shape=[stored((heads, n, LANES), BF16)] * 2,
        input_output_aliases={3: 0, 4: 1} if extra else {},
        scratch_shapes=[pltpu.VMEM((LANES, n), F32)] * 2,
        compiler_params=params(24),
        cost_estimate=pl.CostEstimate(
            flops=count * n * n * 2560, bytes_accessed=8 * 2**20, transcendentals=count * n * n
        ),
        name="own_back",
    )(far(q), far(do), far(kv), *extra)


def finish_q_kernel(
    place, dq_own, dq_peer, normed, wide, merged_c, merged_d, grad_low, out, grad_w, grad_b, nat0, nat1, nat2, nat3, acc, both, out_grad
):
    i = pl.program_id(0)
    n = nat0.shape[0]
    lane = lax.broadcasted_iota(jnp.int32, (n, LANES), 1)
    low = []
    for j, nat in enumerate((nat0, nat1, nat2, nat3)):
        unpermute(place[0] + 4 * i + j, j, (dq_own, dq_peer), nat)
        rows = jnp.where(lane < HD, nat[...] * (1.0 / ROOT), 0.0)
        grad_b[j, 0:1, :] = jnp.sum(rows, 0, keepdims=True)
        low.append(rows.astype(BF16))
    low = jnp.concatenate(low, axis=1)
    gradient = dot_lt(low, normed[...])
    for j in range(4):
        grad_w[0, j] = gradient[j * LANES : j * LANES + HD].astype(BF16)

    @pl.when(i == 0)
    def _():
        group = merged_c.shape[0]
        both[:group] = merged_c[...]
        both[group:] = merged_d[...]
        out_grad[...] = dot(both[...], grad_low[...]).astype(BF16)

    for j in range(4):
        at = pl.multiple_of((4 * i + j) * HD, HD)
        grad_w[1, j] = out_grad[pl.ds(at, HD), :]

    part = dot_rt(low, jnp.concatenate([wide[j] for j in range(4)], axis=1))

    @pl.when(i == 0)
    def _():
        acc[...] = part

    @pl.when(i > 0)
    def _():
        acc[...] += part

    @pl.when(i == pl.num_programs(0) - 1)
    def _():
        out[...] = acc[...].astype(BF16)


def unpermute(head, j, sources, nat):
    n = nat.shape[0]
    block = n // FOLD
    for p in range(FOLD):
        c = (head + ORDER[p]) % FOLD
        at = pl.ds(p * block, block)
        total = None
        for ref in sources:
            if p * block < ref.shape[1]:
                piece = ref[j, at, :].astype(F32)
                total = piece if total is None else total + piece
        nat[pl.ds(c, block, stride=FOLD), :] = total


def finish_kv_kernel(
    place, dkv_own, r_core, r_x, r_z1, r_z2, r_z3, normed, rows, wide, start, grad_one,
    grad_normed, keep, send, grad_b, sums, acc, nat0, nat1, nat2, nat3,
):
    i = pl.program_id(0)
    n, d = rows.shape
    lane = lax.broadcasted_iota(jnp.int32, (n, LANES), 1)
    low = []
    for j, nat in enumerate((nat0, nat1, nat2, nat3)):
        unpermute(place[0] + 4 * i + j, j, (dkv_own, r_core, r_x, r_z1, r_z2, r_z3), nat)
        both = nat[...]
        both = jnp.where(lane < HD, both * (1.0 / ROOT), jnp.where(lane < 2 * HD, both, 0.0))
        grad_b[j, 0:1, :] = jnp.sum(both, 0, keepdims=True)
        low.append(both.astype(BF16))
    low = jnp.concatenate(low, axis=1)
    gradient = dot_lt(low, normed[...])
    first = place[3] == 0
    for j in range(4):
        for k in range(2):
            one = grad_one[k, j]
            two = gradient[j * LANES + k * HD : j * LANES + (k + 1) * HD].astype(BF16)
            keep[k, j] = jnp.where(first, one, two)
            send[k, j] = jnp.where(first, two, one)
    part = dot_rt(low, jnp.concatenate([wide[j] for j in range(4)], axis=1))

    @pl.when(i == 0)
    def _():
        acc[...] = start[...].astype(F32) + part

    @pl.when(i > 0)
    def _():
        acc[...] += part

    @pl.when(i == pl.num_programs(0) - 1)
    def _():
        total = acc[...]
        grad_normed[...] = total.astype(BF16)
        unit, _ = unit_rows(rows[...].astype(F32))
        sums[0:1, :] = jnp.sum(total * unit, 0, keepdims=True)
        sums[1:2, :] = jnp.sum(total, 0, keepdims=True)
        sums[2:8, :] = jnp.zeros((6, d), F32)


def pairs(rows):
    return pl.BlockSpec((4, rows, LANES), lambda i: (i, 0, 0))


def finish_q(place, dq_own, dq_peer, normed, wide, merged, grad_low):
    heads, n, _ = dq_own.shape
    d = normed.shape[1]
    return pl.pallas_call(
        finish_q_kernel,
        grid=(heads // 4,),
        in_specs=[
            pl.BlockSpec(memory_space=pltpu.SMEM),
            pairs(n),
            pairs(n // 2),
            once((n, d)),
            pl.BlockSpec((4, d, LANES), lambda i: (i, 0, 0)),
            once(merged[0].shape),
            once(merged[1].shape),
            once((n, d)),
        ],
        out_specs=[
            full((n, d)),
            pl.BlockSpec((2, 4, HD, d), lambda i: (0, i, 0, 0)),
            pl.BlockSpec((4, 1, LANES), lambda i: (i, 0, 0)),
        ],
        out_shape=[
            stored((n, d), BF16),
            stored((2, heads, HD, d), BF16),
            shape((heads, 1, LANES), F32),
        ],
        scratch_shapes=[pltpu.VMEM((n, LANES), F32)] * 4
        + [
            pltpu.VMEM((n, d), F32),
            pltpu.VMEM((heads * HD, n), BF16),
            pltpu.VMEM((heads * HD, d), BF16),
        ],
        compiler_params=params(29),
        cost_estimate=pl.CostEstimate(
            flops=4 * n * d * heads * 128, bytes_accessed=14 * 2**20, transcendentals=0
        ),
        name="finish_q",
    )(place, far(dq_own), far(dq_peer), normed, far(wide), *merged, grad_low)


def finish_kv(place, dkv_own, received, normed, rows, wide, start, grad_one):
    heads, n, _ = dkv_own.shape
    d = normed.shape[1]
    return pl.pallas_call(
        finish_kv_kernel,
        grid=(heads // 4,),
        in_specs=[
            pl.BlockSpec(memory_space=pltpu.SMEM),
            pairs(n),
            pairs(n // 2),
            pairs(n // 4),
            pairs(n // 8),
            pairs(n // 16),
            pairs(n // 16),
            once((n, d)),
            once((n, d)),
            pl.BlockSpec((4, d, LANES), lambda i: (i, 0, 0)),
            once((n, d)),
            pl.BlockSpec((2, 4, HD, d), lambda i: (0, i, 0, 0)),
        ],
        out_specs=[
            full((n, d)),
            pl.BlockSpec((2, 4, HD, d), lambda i: (0, i, 0, 0)),
            pl.BlockSpec((2, 4, HD, d), lambda i: (0, i, 0, 0)),
            pl.BlockSpec((4, 1, LANES), lambda i: (i, 0, 0)),
            full((8, d)),
        ],
        out_shape=[
            shape((n, d), BF16),
            stored((2, heads, HD, d), BF16),
            shape((2, heads, HD, d), BF16),
            shape((heads, 1, LANES), F32),
            shape((8, d), F32),
        ],
        scratch_shapes=[pltpu.VMEM((n, d), F32)] + [pltpu.VMEM((n, LANES), F32)] * 4,
        compiler_params=params(36),
        cost_estimate=pl.CostEstimate(
            flops=4 * n * d * heads * 128, bytes_accessed=20 * 2**20, transcendentals=0
        ),
        name="finish_kv",
    )(place, far(dkv_own), *received, normed, rows, far(wide), far(start), far(grad_one))


def spread_kernel(place, own, peer, down, up):
    first = place[3] == 0
    down[...] = jnp.where(first, own[...], peer[...]).astype(F32)
    up[...] = jnp.where(first, peer[...], own[...]).astype(F32).T


def spread(place, own, peer):
    ff, d = own.shape
    block = 256
    rows = pl.BlockSpec((block, d), lambda i: (i, 0))
    return pl.pallas_call(
        spread_kernel,
        grid=(ff // block,),
        in_specs=[pl.BlockSpec(memory_space=pltpu.SMEM), rows, rows],
        out_specs=[rows, pl.BlockSpec((d, block), lambda i: (0, i))],
        out_shape=[shape((ff, d), F32), shape((d, ff), F32)],
        compiler_params=params(12),
        name="spread",
    )(place, own, peer)


def spread_qkv_kernel(place, own, peer, qkv, out):
    i = pl.program_id(0)
    first = place[3] == 0
    width = qkv.shape[2]

    def piece(on_first, at):
        mine = first == on_first
        return jnp.where(mine, own[at], peer[at]).astype(F32)

    lower, upper = slice(0, width), slice(width, 2 * width)

    @pl.when(i == 0)
    def _():
        qkv[0] = piece(True, lower).T

    @pl.when(i == 1)
    def _():
        qkv[0] = piece(False, lower).T

    @pl.when(i == 2)
    def _():
        qkv[0] = piece(False, upper).T
        out[...] = piece(True, upper)


def spread_qkv(place, own, peer):
    half, d = own.shape
    width = half // 2
    return pl.pallas_call(
        spread_qkv_kernel,
        in_specs=[pl.BlockSpec(memory_space=pltpu.SMEM), once(own.shape), once(own.shape)],
        out_specs=[pl.BlockSpec((1, d, width), lambda i: (i, 0, 0)), full((width, d))],
        grid=(3,),
        out_shape=[shape((3, d, width), F32), shape((width, d), F32)],
        compiler_params=params(16),
        name="spread_qkv",
    )(place, own, peer)


def last_kernel(rows, own_g, peer_g, grad_hidden, gain, out):
    unit, inverse = unit_rows(rows[...].astype(F32))
    gradient = own_g[...].astype(F32) + peer_g[...].astype(F32)
    out[...] = grad_hidden[...] + norm_back(gradient, unit, inverse, gain[...])


def last(rows, own_g, peer_g, grad_hidden, gain):
    n, d = rows.shape
    part = pl.BlockSpec((256, d), lambda i: (i, 0))
    return pl.pallas_call(
        last_kernel,
        grid=(n // 256,),
        in_specs=[part] * 4 + [once((1, d))],
        out_specs=part,
        out_shape=shape((n, d), F32),
        compiler_params=params(12),
        cost_estimate=LIGHT,
        name="last",
    )(rows, own_g, peer_g, grad_hidden, gain)


def gather_small_kernel(sums1, sums_a, sums_b, sums_c, up_a, up_c, grad_bq, grad_bkv, out):
    heads = grad_bq.shape[0]
    d = out.shape[1]
    out[...] = jnp.zeros_like(out)
    out[0:2, :] = sums1[0:2, :]
    out[2:6, :] = sums_a[0:4, :] + sums_b[0:4, :] + sums_c[0:4, :]
    up = up_a[...] + up_c[...]
    for k in range(up.shape[1] // d):
        out[6 + k : 7 + k, :] = up[:, k * d : (k + 1) * d]
    row = [grad_bq[h, :, :HD] for h in range(heads)]
    row += [grad_bkv[h, :, HD : 2 * HD] for h in range(heads)]
    out[15:16, :] = jnp.concatenate(row, axis=1)


def gather_small(sums1, sums2, up_b, grad_bq, grad_bkv):
    d = sums1.shape[1]
    inputs = (sums1, *sums2, *up_b, grad_bq, grad_bkv)
    return pl.pallas_call(
        gather_small_kernel,
        grid=(1,),
        in_specs=[once(x.shape) for x in inputs],
        out_specs=full((FOLD, d)),
        out_shape=shape((FOLD, d), F32),
        compiler_params=params(4),
        cost_estimate=LIGHT,
        name="gather_small",
    )(*inputs)


def add_head(small, peer):
    return jnp.where(jnp.arange(small.shape[0])[:, None] < 2, small + peer, small)


def spread_small_kernel(small, gains, shifts, qv, out_b, up_b, down_b):
    d = small.shape[1]
    width = qv.shape[1]
    gains[0:1, :] = small[0:1, :]
    shifts[0:1, :] = small[1:2, :]
    gains[1:2, :] = small[2:3, :]
    shifts[1:2, :] = small[3:4, :]
    out_b[...] = small[4, :]
    down_b[...] = small[5, :]
    for k in range(up_b.shape[0] // d):
        up_b[k * d : (k + 1) * d] = small[6 + k, :]
    qv[0:1, :] = small[15:16, :width]
    qv[1:2, :] = small[15:16, width:]


def spread_small(small, ff):
    d = small.shape[1]
    dims = [(2, d), (2, d), (2, d // 2), (d,), (ff,), (d,)]
    return pl.pallas_call(
        spread_small_kernel,
        grid=(1,),
        in_specs=[once(small.shape)],
        out_specs=[full(x) for x in dims],
        out_shape=[shape(x, F32) for x in dims],
        compiler_params=params(4),
        cost_estimate=LIGHT,
        name="spread_small",
    )(small)


def swap(x, axis, apart):
    count = lax.axis_size(axis)
    return lax.ppermute(x, axis, [(i, i ^ apart) for i in range(count)])


def whole_call(kernel, place, inputs, outputs, name):
    return pl.pallas_call(
        kernel,
        grid=(1,),
        in_specs=[pl.BlockSpec(memory_space=pltpu.SMEM)] + [once(x.shape) for x in inputs],
        out_specs=[full(dims) for dims, _ in outputs],
        out_shape=[shape(dims, kind) for dims, kind in outputs],
        compiler_params=params(24),
        cost_estimate=LIGHT,
        name=name,
    )(place, *inputs)


def added(refs, at=slice(None)):
    total = refs[0][at, :].astype(F32)
    for ref in refs[1:]:
        total = total + ref[at, :].astype(F32)
    return total


def cut(index, count):
    return pl.ds(pl.multiple_of(index * count, count), count)


class Sum:
    def __init__(self, place, rows, width):
        self.place, self.rows, self.width = place, rows, width
        self.third, self.twelfth = rows // 3, rows // 12

    def call(self, kernel, inputs, outputs, name):
        dims = [((count, self.width), kind) for count, kind in outputs]
        return whole_call(kernel, self.place, inputs, dims, name)

    def start(self, keep, got):
        third, twelfth = self.third, self.twelfth

        def kernel(place, keep, got, m1, s1, m2, *s2):
            side, line = place[4], place[5]
            m1[...] = added((keep, got), cut(side, third))
            s1[...] = added((keep, got), cut(1 - side, third)).astype(BF16)

            def quarter(k):
                at = pl.multiple_of(2 * third + (line ^ k) * twelfth, twelfth)
                return added((keep, got), pl.ds(at, twelfth))

            m2[...] = quarter(0)
            for k in (1, 2, 3):
                s2[k - 1][...] = quarter(k).astype(BF16)

        return self.call(
            kernel,
            (keep, got),
            [(third, F32), (third, BF16), (twelfth, F32)] + [(twelfth, BF16)] * 3,
            "start_sum",
        )

    def send1(self, state):
        m1, s1, m2, *s2 = state
        got = swap(s1, "seq", 2)
        return (m1, m2, got) + tuple(swap(x, "seq", 4 * k) for k, x in zip((1, 2, 3), s2))

    def middle(self, state):
        twelfth = self.twelfth

        def kernel(place, m1, m2, g1, ga, gb, gc, n1, n2, s2, *s1):
            side, line = place[4], place[5]
            n1[...] = added((m1, g1), cut(line, twelfth))
            for k in (1, 2, 3):
                s1[k - 1][...] = added((m1, g1), cut(line ^ k, twelfth)).astype(BF16)
            n2[...] = added((m2, ga, gb, gc), cut(side, twelfth // 2))
            s2[...] = added((m2, ga, gb, gc), cut(1 - side, twelfth // 2)).astype(BF16)

        return self.call(
            kernel,
            state,
            [(twelfth, F32), (twelfth // 2, F32), (twelfth // 2, BF16)] + [(twelfth, BF16)] * 3,
            "middle_sum",
        )

    def send2(self, state):
        n1, n2, s2, *s1 = state
        got = tuple(swap(x, "seq", 4 * k) for k, x in zip((1, 2, 3), s1))
        return (n1, n2) + got + (swap(s2, "seq", 2),)

    def end(self, state):
        twelfth = self.twelfth

        def kernel(place, n1, n2, ga, gb, gc, g2, one, two):
            one[...] = added((n1, ga, gb, gc)).astype(BF16)
            two[...] = added((n2, g2)).astype(BF16)

        pair = self.call(kernel, state, [(twelfth, BF16), (twelfth // 2, BF16)], "end_sum")
        return tuple(self.beyond(x) for x in pair)

    def beyond(self, low):
        apart = FOLD
        while apart < lax.axis_size("seq"):
            low = (low.astype(F32) + swap(low, "seq", apart).astype(F32)).astype(BF16)
            apart *= 2
        return low

    def send3(self, pair):
        one, two = pair
        got = tuple(swap(one, "seq", 4 * k) for k in (1, 2, 3))
        return (one, two) + got + (swap(two, "seq", 2),)

    def join(self, state):
        twelfth, third = self.twelfth, self.third

        def kernel(place, one, two, ga, gb, gc, g2, out1, out2):
            side, line = place[4], place[5]
            for k, ref in enumerate((one, ga, gb, gc)):
                out1[cut(line ^ k, twelfth), :] = ref[...]
            out2[cut(side, twelfth // 2), :] = two[...]
            out2[cut(1 - side, twelfth // 2), :] = g2[...]

        return self.call(kernel, state, [(third, BF16), (twelfth, BF16)], "join_sum")

    def send4(self, pair):
        one, two = pair
        got = swap(one, "seq", 2)
        return (one, two, got) + tuple(swap(two, "seq", 4 * k) for k in (1, 2, 3))

    def whole(self, state):
        twelfth, third = self.twelfth, self.third

        def kernel(place, one, two, g1, ga, gb, gc, out):
            side, line = place[4], place[5]
            out[cut(side, third), :] = one[...]
            out[cut(1 - side, third), :] = g1[...]
            for k, ref in enumerate((two, ga, gb, gc)):
                at = pl.multiple_of(2 * third + (line ^ k) * twelfth, twelfth)
                out[pl.ds(at, twelfth), :] = ref[...]

        return self.call(kernel, state, [(self.rows, BF16)], "whole_sum")[0]


class LineSum(Sum):
    def __init__(self, place, rows, width):
        self.place, self.rows, self.width = place, rows, width
        self.half, self.eighth = rows // 2, rows // 8

    def start(self, keep, got):
        half = self.half

        def kernel(place, keep, got, mine, *sends):
            mine[...] = added((keep, got), cut(place[4], half))
            for k, send in enumerate(sends):
                at = cut(2 * (1 - place[4]) + k, half // 2)
                send[...] = added((keep, got), at).astype(BF16)

        outputs = [(half, F32)] + [(half // 2, BF16)] * 2
        return self.call(kernel, (keep, got), outputs, "start_line")

    def near(self, mine, one, two):
        eighth = self.eighth

        def kernel(place, mine, one, two, keep, send):
            parity = place[5] % 2
            for high, got in enumerate((one, two)):
                out = pl.ds(high * eighth, eighth)

                def piece(low):
                    at = pl.multiple_of((2 * high + low) * eighth, eighth)
                    return mine[pl.ds(at, eighth), :] + got[cut(low, eighth), :].astype(F32)

                keep[out, :] = piece(parity)
                send[out, :] = piece(1 - parity).astype(BF16)

        outputs = [(2 * eighth, F32), (2 * eighth, BF16)]
        return self.call(kernel, (mine, one, two), outputs, "near_line")

    def across(self, keep, got):
        eighth = self.eighth

        def kernel(place, keep, got, mine, send):
            high = place[5] // 2
            mine[...] = added((keep, got), cut(high, eighth))
            send[...] = added((keep, got), cut(1 - high, eighth)).astype(BF16)

        outputs = [(eighth, F32), (eighth, BF16)]
        return self.call(kernel, (keep, got), outputs, "across_line")

    def end(self, mine, got):
        def kernel(place, mine, got, out):
            out[...] = added((mine, got)).astype(BF16)

        outputs = [(self.eighth, BF16)]
        return self.beyond(self.call(kernel, (mine, got), outputs, "end_line")[0])

    def join_across(self, mine, got):
        def kernel(place, mine, got, low, high):
            lower = place[5] // 2 == 0
            low[...] = jnp.where(lower, mine[...], got[...])
            high[...] = jnp.where(lower, got[...], mine[...])

        outputs = [(self.eighth, BF16)] * 2
        return self.call(kernel, (mine, got), outputs, "join_across")

    def join_low(self, mine, got):
        eighth = self.eighth

        def kernel(place, mine, got, out):
            parity = place[5] % 2
            out[cut(parity, eighth), :] = mine[...]
            out[cut(1 - parity, eighth), :] = got[...]

        return self.call(kernel, (mine, got), [(2 * eighth, BF16)], "join_low")[0]

    def join_high(self, mine, got):
        def kernel(place, mine, got, one, two):
            even = place[5] % 2 == 0
            one[...] = jnp.where(even, mine[...], got[...])
            two[...] = jnp.where(even, got[...], mine[...])

        outputs = [(self.eighth, BF16)] * 2
        return self.call(kernel, (mine, got), outputs, "join_high")

    def whole(self, mine, got):
        half, eighth = self.half, self.eighth

        def kernel(place, *refs):
            *parts, out = refs
            for side, group in ((place[4], parts[:3]), (1 - place[4], parts[3:])):
                at = 0
                for ref in group:
                    count = ref.shape[0]
                    out[pl.ds(pl.multiple_of(side * half + at, eighth), count), :] = ref[...]
                    at += count

        return self.call(kernel, (*mine, *got), [(self.rows, BF16)], "whole_line")[0]


def send_home(place, kept, r_core):
    heads, rows, lanes = kept.shape
    quarter = rows // 3
    half = r_core.shape[1] - rows

    def kernel(place, kept, r_core, far, near, stay):
        def both(k):
            return kept[:, cut(k, quarter), :] + r_core[
                :, pl.ds(half + k * quarter, quarter), :
            ].astype(F32)

        near[...] = both(0).astype(BF16)
        stay[...] = both(1)
        far[...] = both(2).astype(BF16)

    dims = (heads, quarter, lanes)
    return whole_call(
        kernel, place, (kept, r_core), [(dims, BF16), (dims, BF16), (dims, F32)], "send_home"
    )


def send_line(place, stay, got):
    heads, rows, lanes = stay.shape

    def kernel(place, stay, got, z1, z2, z3):
        def both(start, count):
            at = pl.ds(start, count)
            return (stay[:, at, :] + got[:, at, :].astype(F32)).astype(BF16)

        z1[...] = both(0, rows // 2)
        z2[...] = both(rows // 2, rows // 4)
        z3[...] = both(3 * rows // 4, rows // 4)

    return whole_call(
        kernel,
        place,
        (stay, got),
        [((heads, count, lanes), BF16) for count in (rows // 2, rows // 4, rows // 4)],
        "send_line",
    )


def tie(*xs):
    return lax.optimization_barrier(xs)


def sum_small(x, apart):
    while apart < lax.axis_size("seq"):
        x = x + swap(x, "seq", apart)
        apart *= 2
    return x


def local(
    rows,
    lengths,
    norm_gains,
    norm_shifts,
    qkv_weight,
    qv_bias,
    out_weight,
    out_bias,
    up_weight,
    up_bias,
    down_weight,
    down_bias,
    out_cot,
):
    n, d = rows.shape
    width = qkv_weight.shape[2]
    heads = width // HD
    seq_place = lax.axis_index("seq")
    head_place = lax.axis_index("head")
    slide_rows = min(FOLD * SEG, n * lax.axis_size("seq"))
    start = seq_place * n
    slide = start // slide_rows
    length = jnp.sum(jnp.where(jnp.arange(lengths.shape[0]) == slide, lengths, 0))
    limit = jnp.clip(length - start % slide_rows, 0, n)
    place = jnp.stack(
        [
            head_place * heads,
            limit,
            head_place,
            seq_place % 2,
            seq_place // 2 % 2,
            seq_place // 4 % 4,
        ]
    ).astype(jnp.int32)
    half, quarter, eighth = n // 2, n // 4, n // 8
    first_heads = heads // 2

    peer_out_weight = swap(out_weight, "head", 1)
    wide_out = jnp.pad(
        out_weight.reshape(heads, HD, d), ((0, 0), (HD, LANES - 2 * HD), (0, 0))
    ).reshape(heads * LANES, d)

    kv, s1, sx, sz1, sz, normed1, wide_kv = project_kv(
        place, rows, norm_gains[:1], norm_shifts[:1], qkv_weight, qv_bias
    )
    rz1 = swap(sz1, "seq", 4)
    rx = swap(sx, "seq", 2)
    rz2 = swap(sz, "seq", 8)
    rz3 = swap(sz, "seq", 12)
    cs1 = swap(s1, "seq", 1)
    q, wide_q = project_q(place, normed1, qkv_weight, qv_bias)
    q, rz1, rz2, rz3 = tie(q, rz1, rz2, rz3)
    zc = jnp.concatenate([rz1, rz2, rz3], 1)
    rx2 = swap(zc, "seq", 2)
    crx = swap(rx, "seq", 1)
    czc = swap(zc, "seq", 1)
    own = own_attention(q, kv, 0, first_heads)
    own = own_attention(q, kv, first_heads, heads - first_heads, own)
    own, rx2, crx, czc, cs1, peer_out_weight = tie(own, rx2, crx, czc, cs1, peer_out_weight)
    crx2 = swap(rx2, "seq", 1)
    received = (cs1, rx, crx, zc, rx2, czc, crx2)
    *state, low_one = peers_attention(place, q, own, received, 0, first_heads)
    peer_low_one = swap(low_one, "head", 1)
    *state, low_two = peers_attention(
        place, q, own, received, first_heads, heads - first_heads, state
    )
    merged, kv_all, qb = state
    merged, low_two, peer_low_one = tie(merged, low_two, peer_low_one)
    merged_low = (low_one, low_two)
    peer_low = (peer_low_one, swap(low_two, "head", 1))

    def feed_rows(start, sizes, into):
        return feed(
            place,
            rows,
            out_cot,
            merged_low + peer_low,
            out_weight,
            peer_out_weight,
            out_bias[None],
            norm_gains[1:],
            norm_shifts[1:],
            up_weight,
            up_bias[None],
            down_weight,
            start,
            sizes,
            into,
        )

    *fed, g2_a, ub_one = feed_rows(0, (quarter,), None)
    peer_a = swap(g2_a, "head", 1)
    *fed, g2_b, g2_c, ub_two = feed_rows(quarter, (quarter, half), fed)
    *fed, peer_a = tie(*fed, peer_a)
    hidden, normed2, act, grad_pre = fed
    peer_b = swap(g2_b, "head", 1)
    mlp, keep, send = weights(place, act, grad_pre, normed2, out_cot, down_weight)
    peer_b, mlp, keep, send = tie(peer_b, mlp, keep, send)

    def turn_rows(own_g, peer_g, start, into):
        count = own_g.shape[0]
        return turn(out_cot, own_g, peer_g, hidden, norm_gains[1:], wide_out, start, count, into)

    ff = up_bias.shape[0]
    sums = LineSum(place, ff, d)
    peer_c = swap(g2_c, "head", 1)
    ff_mine, *ff_send = sums.start(keep, swap(send, "seq", 1))
    ff_got = [swap(ff_send[0], "seq", 2)]
    *turned, sums2_a = turn_rows(g2_a, peer_a, 0, None)
    *turned, sums2_b = turn_rows(g2_b, peer_b, quarter, turned)
    peer_c, ff_mine, ff_send[1], *turned, ff_got[0] = tie(
        peer_c, ff_mine, ff_send[1], *turned, ff_got[0]
    )
    ff_got += [swap(ff_send[1], "seq", 2)]
    grad_hidden, grad_low, gm, sums2_c = turn_rows(g2_c, peer_c, half, turned)
    back = peers_back(place, gm, merged, qb, kv_all, 0, first_heads)
    *back, ff_mine, ff_got[0], ff_got[1] = tie(*back, ff_mine, *ff_got)
    ff_mine, ff_send = sums.near(ff_mine, *ff_got)
    ff_got = swap(ff_send, "seq", 4)
    peer_mlp = swap(mlp, "head", 1)
    back = peers_back(
        place, gm, merged, qb, kv_all, first_heads, heads - first_heads, back
    )
    do, dq_peer, to_core, kept, ff_mine, ff_got = tie(*back, ff_mine, ff_got)
    r_core = swap(to_core, "seq", 1)
    ff_mine, ff_send = sums.across(ff_mine, ff_got)
    ff_got = swap(ff_send, "seq", 8)
    back = own_back(qb, do, kv, 0, first_heads)
    dq_own, dkv_own, r_core, ff_mine, ff_got = tie(*back, r_core, ff_mine, ff_got)
    far_rows, near_rows, stay = send_home(place, kept, r_core)
    r_x2 = swap(far_rows, "seq", 2)
    r_x = swap(near_rows, "seq", 2)
    ff_mine = sums.end(ff_mine, ff_got)
    ff_got = swap(ff_mine, "seq", 8)
    back = own_back(qb, do, kv, first_heads, heads - first_heads, (dq_own, dkv_own))
    dq_own, dkv_own, r_x2, ff_mine, ff_got = tie(*back, r_x2, ff_mine, ff_got)
    z1, z2, z3 = send_line(place, stay, r_x2)
    r_z1 = swap(z1, "seq", 4)
    r_z2 = swap(z2, "seq", 8)
    r_z3 = swap(z3, "seq", 12)
    ff_low, ff_high = sums.join_across(ff_mine, ff_got)
    ff_got = swap(ff_low, "seq", 4)
    start_g, grad_one, grad_bq = finish_q(
        place, dq_own, dq_peer, normed1, wide_q, merged_low, grad_low
    )
    start_g, grad_one, peer_mlp, r_x, r_z1, r_z2, r_z3, ff_low, ff_high, ff_got = tie(
        start_g, grad_one, peer_mlp, r_x, r_z1, r_z2, r_z3, ff_low, ff_high, ff_got
    )
    out_rows = (
        hidden + ((mlp.astype(F32) + peer_mlp.astype(F32)) + down_bias)
    ).astype(BF16)
    ff_mine = [sums.join_low(ff_low, ff_got)]
    ff_got = [swap(ff_mine[0], "seq", 2)]
    high_got = swap(ff_high, "seq", 4)
    grad_normed1, keep, send, grad_bkv, sums1 = finish_kv(
        place, dkv_own, (r_core, r_x, r_z1, r_z2, r_z3), normed1, rows, wide_kv, start_g, grad_one
    )
    keep, send, sums1, out_rows, grad_normed1, ff_got[0], ff_high, high_got = tie(
        keep, send, sums1, out_rows, grad_normed1, ff_got[0], ff_high, high_got
    )

    count = 2 * width
    keep, send = keep.reshape(count, d), send.reshape(count, d)
    got = swap(send, "seq", 1)
    peer_normed1 = swap(grad_normed1, "head", 1)
    small = gather_small(sums1, (sums2_a, sums2_b, sums2_c), (ub_one, ub_two), grad_bq, grad_bkv)
    small = small + swap(small, "seq", 1)
    keep, got, small = tie(keep, got, small)
    w_sums = Sum(place, count, d)
    state = w_sums.send1(w_sums.start(far(keep), got))
    small = small + swap(small, "seq", 4)
    ff_mine += sums.join_high(ff_high, high_got)
    *state, small = tie(*state, small)
    state = w_sums.send2(w_sums.middle(state))
    small = small + swap(small, "seq", 2)
    *state, small, ff_mine[1], ff_mine[2] = tie(*state, small, ff_mine[1], ff_mine[2])
    ff_got += [swap(ff_mine[1], "seq", 2), swap(ff_mine[2], "seq", 2)]
    state = w_sums.send3(w_sums.end(state))
    small = small + swap(small, "seq", 8)
    rows_grad = last(rows, grad_normed1, peer_normed1, grad_hidden, norm_gains[:1])
    ff_own = sums.whole(ff_mine, ff_got)
    *state, small, rows_grad, ff_own = tie(*state, small, rows_grad, ff_own)
    state = w_sums.send4(w_sums.join(state))
    peer_small = swap(small, "head", 1)
    down_weight_grad, up_weight_grad = spread(place, ff_own, swap(ff_own, "seq", 1))
    *state, small, peer_small, down_weight_grad = tie(
        *state, small, peer_small, down_weight_grad
    )
    w_own = w_sums.whole(state)
    w_peer = swap(w_own, "seq", 1)
    small = sum_small(add_head(small, peer_small), FOLD)
    qkv_grad, out_weight_grad = spread_qkv(place, w_own, w_peer)
    small, qkv_grad = tie(small, qkv_grad)
    gains_grad, shifts_grad, qv_bias_grad, out_bias_grad, up_bias_grad, down_bias_grad = (
        spread_small(small, ff)
    )
    return (
        out_rows,
        rows_grad,
        gains_grad,
        shifts_grad,
        qkv_grad,
        qv_bias_grad,
        out_weight_grad,
        out_bias_grad,
        up_weight_grad,
        up_bias_grad,
        down_weight_grad,
        down_bias_grad,
    )


def solution(mesh):
    placed = (
        P("seq", None),
        P(),
        P(),
        P(),
        P(None, None, "head"),
        P(None, "head"),
        P("head", None),
        P(),
        P(None, "head"),
        P("head"),
        P("head", None),
        P(),
        P("seq", None),
    )
    return jax.shard_map(
        local,
        mesh=mesh,
        in_specs=placed,
        out_specs=(
            P("seq", None),
            P("seq", None),
            P(),
            P(),
            P(None, None, "head"),
            P(None, "head"),
            P("head", None),
            P(),
            P(None, "head"),
            P("head"),
            P("head", None),
            P(),
        ),
        check_vma=False,
    )
```

```python
import functools
import math

import jax
import jax.numpy as jnp
import numpy as np
from jax import lax
from jax.experimental import pallas as pl
from jax.experimental.pallas import tpu as pltpu
from jax.sharding import PartitionSpec as P

HD = 48
SEG = 1024
LANES = 128
LEVELS = 5
FOLD = 16

EPS = 1e-05
ROOT = math.sqrt(HD)
EXP_SCALE = math.log2(math.e) / ROOT
ROOT_HALF = 1.0 / math.sqrt(2.0)
DENSITY_NORM = 1.0 / math.sqrt(2.0 * math.pi)
ABSENT = -1e20

ONE = 96
MASK = 99
MULT = 100
TOP = 127

ORDER = (0, 8, 4, 12, 2, 6, 10, 14, 1, 3, 5, 7, 9, 11, 13, 15)
CLASS = (4, 3, 2, 2, 1, 1, 1, 1, 0, 0, 0, 0, 0, 0, 0, 0)

F32 = jnp.float32
BF16 = jnp.bfloat16


LIGHT = pl.CostEstimate(flops=0, bytes_accessed=0, transcendentals=0)


def params(mib=48):
    return pltpu.CompilerParams(vmem_limit_bytes=mib * 2**20)


def dot(left, right):
    return jnp.dot(left, right, preferred_element_type=F32)


def dot_rt(left, right):
    return lax.dot_general(left, right, (((1,), (1,)), ((), ())), preferred_element_type=F32)


def dot_lt(left, right):
    return lax.dot_general(left, right, (((0,), (0,)), ((), ())), preferred_element_type=F32)


def full(shape):
    return pl.BlockSpec(shape, lambda *_: (0,) * len(shape))


def once(shape):
    return pl.BlockSpec(shape, lambda *_: (0,) * len(shape), pipeline_mode=pl.Buffered(1))


def per_head(rows, lanes=LANES):
    return pl.BlockSpec((1, rows, lanes), lambda h: (h, 0, 0))


def shape(dims, kind):
    return jax.ShapeDtypeStruct(dims, kind)


def stored(dims, kind):
    return pltpu.HBM(dims, kind)


def far(x):
    return pltpu.with_memory_space_constraint(x, pltpu.HBM)


def split3(x):
    high = x.astype(BF16).astype(F32)
    rest = x - high
    middle = rest.astype(BF16).astype(F32)
    return high, middle, rest - middle


def with_terms(block, lane, terms):
    high, middle, low = split3(terms)
    block = jnp.where(lane == ONE, high, block)
    block = jnp.where(lane == ONE + 1, middle, block)
    return jnp.where(lane == ONE + 2, low, block)


def unit_rows(x):
    mean = jnp.mean(x, -1, keepdims=True)
    centred = x - mean
    inverse = lax.rsqrt(jnp.mean(centred * centred, -1, keepdims=True) + EPS)
    return centred * inverse, inverse


def norm_back(gradient, unit, inverse, gain):
    z = gradient * gain
    return inverse * (
        z - jnp.mean(z, -1, keepdims=True) - unit * jnp.mean(z * unit, -1, keepdims=True)
    )


def mult_table(level, blocks):
    table = np.zeros((len(blocks), LANES), np.float32)
    for row, key_class in enumerate(blocks):
        for j in range(level + 1, key_class + 1):
            value = np.float32(ROOT * math.log((j - level + 1) / (j - level)))
            high = np.float32(value.astype(jnp.bfloat16))
            table[row, MULT + j - 1] = high
            table[row, MULT + 4 + j - 1] = np.float32((value - high).astype(jnp.bfloat16))
    return table


def flag_table():
    table = np.zeros((FOLD, LANES), np.float32)
    for row, level in enumerate(CLASS):
        table[row, MULT : MULT + level] = 1.0
        table[row, MULT + 4 : MULT + 4 + level] = 1.0
    return table


def permuted(head, tmp):
    n = tmp.shape[0]
    block = n // FOLD
    for p in range(FOLD):
        c = (head + ORDER[p]) % FOLD
        yield p, pl.ds(p * block, block), slice(p, p + 1), tmp[pl.ds(c, block, stride=FOLD), :]


def project_kv_kernel(
    place, rows, gain, shift, w, bias, table,
    kv, s1, sx, sz1, sz, normed, wide, w_tmp, b_tmp, extra, *tmps,
):
    i = pl.program_id(0)
    n, d = rows.shape
    heads = w.shape[2] // HD
    block = n // FOLD

    @pl.when(i == 0)
    def _():
        unit, _ = unit_rows(rows[...].astype(F32))
        normed[...] = (unit * gain[...] + shift[...]).astype(BF16)
        lane = lax.broadcasted_iota(jnp.int32, (n, LANES), 1)
        here = lax.broadcasted_iota(jnp.int32, (n, LANES), 0) < place[1]
        extra[...] = jnp.where(here | (lane != MASK), 0.0, ABSENT)

    for k in range(heads // 2):

        @pl.when(i == k)
        def _():
            for j in range(2):
                cut = slice((2 * k + j) * HD, (2 * k + j + 1) * HD)
                at = slice(LANES * j, LANES * (j + 1))
                w_tmp[:, at] = jnp.concatenate(
                    [w[1, :, cut], w[2, :, cut], jnp.zeros((d, LANES - 2 * HD), BF16)], axis=1
                )
                b_tmp[:, at] = jnp.concatenate(
                    [
                        jnp.zeros((1, HD), F32),
                        bias[1:2, cut],
                        jnp.ones((1, 3), F32),
                        jnp.zeros((1, LANES - 2 * HD - 3), F32),
                    ],
                    axis=1,
                )

    product = dot(normed[...], w_tmp[...]) + b_tmp[...]
    for j, tmp in enumerate(tmps):
        lanes = slice(LANES * j, LANES * (j + 1))
        wide[j] = w_tmp[:, lanes]
        tmp[...] = product[:, lanes] + extra[...]
        for p, at, row, kv_rows in permuted(place[0] + 2 * i + j, tmp):
            for level, out in enumerate((kv, s1, sx, sz1, sz)):
                if (p + 1) * block <= out.shape[1]:
                    row = slice(level * FOLD + p, level * FOLD + p + 1)
                    out[j, at, :] = (kv_rows + table[row, :]).astype(BF16)


def project_q_kernel(place, normed, w, bias, flags, q, wide, w_tmp, b_tmp, extra, *tmps):
    i = pl.program_id(0)
    n, d = normed.shape
    heads = w.shape[2] // HD

    @pl.when(i == 0)
    def _():
        lane = lax.broadcasted_iota(jnp.int32, (n, LANES), 1)
        here = lax.broadcasted_iota(jnp.int32, (n, LANES), 0) < place[1]
        extra[...] = jnp.where(here & (lane == MASK), 1.0, 0.0)

    for k in range(heads // 2):

        @pl.when(i == k)
        def _():
            for j in range(2):
                cut = slice((2 * k + j) * HD, (2 * k + j + 1) * HD)
                at = slice(LANES * j, LANES * (j + 1))
                w_tmp[:, at] = jnp.concatenate(
                    [w[0, :, cut], jnp.zeros((d, LANES - HD), BF16)], axis=1
                )
                b_tmp[:, at] = jnp.concatenate(
                    [bias[0:1, cut], jnp.zeros((1, LANES - HD), F32)], axis=1
                )

    product = dot(normed[...], w_tmp[...]) + b_tmp[...]
    for j, tmp in enumerate(tmps):
        lanes = slice(LANES * j, LANES * (j + 1))
        wide[j] = w_tmp[:, lanes]
        tmp[...] = product[:, lanes] + extra[...]
        for p, at, row, q_rows in permuted(place[0] + 2 * i + j, tmp):
            q[j, at, :] = (q_rows + flags[row, :]).astype(BF16)


def project_scratch(n, d):
    return [
        pltpu.VMEM((d, 2 * LANES), BF16),
        pltpu.VMEM((1, 2 * LANES), F32),
        pltpu.VMEM((n, LANES), F32),
    ] + [pltpu.VMEM((n, LANES), F32)] * 2


def project_kv(place, rows, gain, shift, w, bias):
    n, d = rows.shape
    heads = w.shape[2] // HD
    table = np.concatenate([mult_table(level, CLASS) for level in range(LEVELS)])
    sizes = (n, n // 2, n // 4, n // 8, n // 16)
    inputs = (rows, gain, shift, w, bias, jnp.asarray(table))
    return pl.pallas_call(
        project_kv_kernel,
        grid=(heads // 2,),
        in_specs=[pl.BlockSpec(memory_space=pltpu.SMEM)] + [once(x.shape) for x in inputs],
        out_specs=[group_spec(m) for m in sizes] + [full((n, d)), group_spec(d)],
        out_shape=[stored((heads, n, LANES), BF16)]
        + [shape((heads, m, LANES), BF16) for m in sizes[1:]]
        + [shape((n, d), BF16), stored((heads, d, LANES), BF16)],
        scratch_shapes=project_scratch(n, d),
        compiler_params=params(24),
        cost_estimate=pl.CostEstimate(
            flops=2 * n * d * heads * 128, bytes_accessed=9 * 2**20, transcendentals=0
        ),
        name="project_kv",
    )(place, *(far(x) for x in inputs))


def project_q(place, normed, w, bias):
    n, d = normed.shape
    heads = w.shape[2] // HD
    inputs = (normed, far(w), far(bias), jnp.asarray(flag_table()))
    return pl.pallas_call(
        project_q_kernel,
        grid=(heads // 2,),
        in_specs=[pl.BlockSpec(memory_space=pltpu.SMEM)] + [once(x.shape) for x in inputs],
        out_specs=[group_spec(n), group_spec(d)],
        out_shape=[stored((heads, n, LANES), BF16), stored((heads, d, LANES), BF16)],
        scratch_shapes=project_scratch(n, d),
        compiler_params=params(20),
        cost_estimate=pl.CostEstimate(
            flops=2 * n * d * heads * 128, bytes_accessed=6 * 2**20, transcendentals=0
        ),
        name="project_q",
    )(place, *inputs)


def own_kernel(q, kv, out, *, block):
    n = q.shape[1]
    lane = lax.broadcasted_iota(jnp.int32, (block, LANES), 1)
    steps = [(j, k * block) for j in range(q.shape[0]) for k in range(n // block)]

    def scores(j, at):
        return dot_rt(q[j, pl.ds(at, block), :], kv[j])

    now = scores(*steps[0])
    for index, (j, at) in enumerate(steps):
        later = scores(*steps[index + 1]) if index + 1 < len(steps) else None
        top = jnp.max(now, -1, keepdims=True)
        weights = jnp.exp2((now - top) * EXP_SCALE).astype(BF16)
        out[j, pl.ds(at, block), :] = jnp.where(lane == TOP, top, dot(weights, kv[j]))
        now = later


def group_spec(rows, start=0, lanes=LANES, heads=2):
    return pl.BlockSpec((heads, rows, lanes), lambda i: (i + start // heads, 0, 0))


ANYWHERE = pl.BlockSpec(memory_space=pl.ANY)


def own_attention(q, kv, start, count, into=None):
    heads, n, _ = q.shape
    spec = group_spec(n, start)
    kernel = functools.partial(own_kernel, block=256)
    extra = () if into is None else (into,)
    return pl.pallas_call(
        kernel if into is None else lambda q, kv, _, out: kernel(q, kv, out),
        grid=(count // 2,),
        in_specs=[spec] * 2 + [ANYWHERE] * len(extra),
        out_specs=spec,
        out_shape=shape((heads, n, LANES), F32),
        input_output_aliases={2: 0} if extra else {},
        compiler_params=params(12),
        cost_estimate=pl.CostEstimate(
            flops=count * n * n * 1024, bytes_accessed=4 * 2**20, transcendentals=count * n * n
        ),
        name="own_attention",
    )(far(q), far(kv), *extra)


def peers_kernel(
    place, q, own, cs1, rx, crx, zc, rx2, czc, crx2, pick, merged, kv_all, qb, low, nat, wide, *, start
):
    i = pl.program_id(0)
    n = q.shape[1]
    block = n // FOLD
    heads = q.shape[0]
    for j in range(heads):
        at = 0
        near = (zc, rx2, czc, crx2)
        pieces = [(cs1, 0, n // 2), (rx, 0, n // 4), (crx, 0, n // 4)]
        pieces += [(r, 0, n // 8) for r in near] + [(r, n // 8, n // 8) for r in near]
        for ref, begin, count in pieces:
            kv_all[j, pl.ds(at, count), :] = ref[j, pl.ds(begin, count), :]
            at += count

        head = place[0] + heads * i + j + start
        chunks = [
            (0, n // 16, 2 * n),
            (n // 16, n // 16, 3 * n // 2),
            (n // 8, n // 8, n),
            (n // 4, n // 4, n // 2),
            (n // 2, n // 2, 0),
        ]
        scores = []
        for begin, count, keys in chunks:
            if keys:
                scores.append(dot_rt(q[j, pl.ds(begin, count), :], kv_all[j, pl.ds(0, keys), :]))
            else:
                scores.append(None)
        for (begin, count, keys), s in zip(chunks, scores):
            rows = pl.ds(begin, count)
            lane = lax.broadcasted_iota(jnp.int32, (count, LANES), 1)
            o = own[j, rows, :]
            top = o[:, TOP : TOP + 1]
            if keys:
                new = jnp.maximum(top, jnp.max(s, -1, keepdims=True))
                weights = jnp.exp2((s - new) * EXP_SCALE).astype(BF16)
                o = o * jnp.exp2((top - new) * EXP_SCALE) + dot(weights, kv_all[j, pl.ds(0, keys), :])
                top = new
            total = o[:, ONE : ONE + 1]
            o = jnp.where((lane >= HD) & (lane < 2 * HD), o / total, 0.0)
            merged[j, rows, :] = o
            lse = top + jnp.log2(total) * (1.0 / EXP_SCALE)
            qb[j, rows, :] = with_terms(q[j, rows, :].astype(F32), lane, -lse).astype(BF16)
            for p in range(begin // block, (begin + count) // block):
                c = (head + ORDER[p]) % FOLD
                off = p * block - begin
                nat[pl.ds(c, block, stride=FOLD), :] = o[off : off + block]
        wide[:, pl.ds(pl.multiple_of((heads * i + j) * LANES, LANES), LANES)] = nat[...].astype(BF16)

    @pl.when(i == pl.num_programs(0) - 1)
    def _():
        low[...] = dot_rt(pick[...], wide[...]).astype(BF16)


def pick_values(heads):
    m = np.zeros((heads * HD, heads * LANES), np.float32)
    for h in range(heads):
        for j in range(HD):
            m[h * HD + j, h * LANES + HD + j] = 1.0
    return m


def peers_attention(place, q, own, received, start, count, into=None):
    heads, n, _ = q.shape
    pick = jnp.asarray(pick_values(count), BF16)
    extra = () if into is None else tuple(into)
    inputs = 4 + len(received)

    def kernel(*refs):
        peers_kernel(*refs[:inputs], *refs[inputs + len(extra) :], start=start)

    return pl.pallas_call(
        kernel,
        grid=(count,),
        in_specs=[
            pl.BlockSpec(memory_space=pltpu.SMEM),
            group_spec(n, start, heads=1),
            group_spec(n, start, heads=1),
        ]
        + [group_spec(r.shape[1], start, heads=1) for r in received]
        + [once(pick.shape)]
        + [ANYWHERE] * len(extra),
        out_specs=[group_spec(n, start, heads=1), group_spec(2 * n, start, heads=1), group_spec(n, start, heads=1)]
        + [full((count * HD, n))],
        out_shape=[
            stored((heads, n, LANES), F32),
            stored((heads, 2 * n, LANES), BF16),
            stored((heads, n, LANES), BF16),
            shape((count * HD, n), BF16),
        ],
        input_output_aliases={inputs + k: k for k in range(len(extra))},
        scratch_shapes=[pltpu.VMEM((n, LANES), F32), pltpu.VMEM((n, count * LANES), BF16)],
        compiler_params=params(28),
        cost_estimate=pl.CostEstimate(
            flops=count * n * n * 512, bytes_accessed=12 * 2**20, transcendentals=count * n * n // 2
        ),
        name="peers_attention",
    )(place, far(q), own, *received, pick, *extra)


def feed_kernel(
    place, rows, cot, own_c, own_d, peer_c, peer_d, own_w, peer_w, out_b, gain, shift, up_w, up_b, down_w,
    hidden, normed, act, grad_pre, *outs, sizes,
):
    *grad_normed, up_b_grad, w_tmp, c_tmp = outs
    i = pl.program_id(0)
    half = own_w.shape[0]
    group = own_c.shape[0]
    first = place[2] == 0

    @pl.when(i == 0)
    def _():
        w_tmp[:half] = jnp.where(first, own_w[...], peer_w[...])
        w_tmp[half:] = jnp.where(first, peer_w[...], own_w[...])

    c_tmp[:group] = jnp.where(first, own_c[...], peer_c[...])
    c_tmp[group:half] = jnp.where(first, own_d[...], peer_d[...])
    c_tmp[half : half + group] = jnp.where(first, peer_c[...], own_c[...])
    c_tmp[half + group :] = jnp.where(first, peer_d[...], own_d[...])
    attended = dot_lt(c_tmp[...], w_tmp[...])
    hid = rows[...].astype(F32) + (attended + out_b[...])
    hidden[...] = hid
    unit, _ = unit_rows(hid)
    low = (unit * gain[...] + shift[...]).astype(BF16)
    normed[...] = low
    pre = dot(low, up_w[...]) + up_b[...]
    phi = 0.5 * (1.0 + lax.erf(pre * ROOT_HALF))
    act[...] = (pre * phi).astype(BF16)
    slope = phi + pre * jnp.exp(-0.5 * pre * pre) * DENSITY_NORM
    gradient = dot_rt(cot[...], down_w[...]) * slope
    total = jnp.sum(gradient, 0, keepdims=True)

    @pl.when(i == 0)
    def _():
        up_b_grad[...] = total

    @pl.when(i > 0)
    def _():
        up_b_grad[...] += total

    gradient = gradient.astype(BF16)
    grad_pre[...] = gradient
    back = dot_rt(gradient, up_w[...]).astype(BF16)
    begin = 0
    for ref, steps in zip(grad_normed, sizes):

        @pl.when((i >= begin) & (i < begin + steps))
        def _():
            ref[...] = back

        begin += steps


def feed(
    place, rows, cot, merged, own_w, peer_w, out_b, gain, shift, up_w, up_b, down_w, start, sizes, into=None
):
    n, d = rows.shape
    block = 256
    count = sum(sizes)
    steps = [size // block for size in sizes]
    begins = [sum(steps[:k]) for k in range(len(steps))]
    ff = up_w.shape[1]
    half = own_w.shape[0]
    first = start // block
    extra = () if into is None else tuple(into)

    def part(lanes):
        return pl.BlockSpec((block, lanes), lambda i: (i + first, 0))

    def kernel(*refs):
        feed_kernel(*refs[:15], *refs[15 + len(extra) :], sizes=steps)

    return pl.pallas_call(
        kernel,
        grid=(count // block,),
        in_specs=[
            pl.BlockSpec(memory_space=pltpu.SMEM),
            part(d),
            part(d),
        ]
        + [pl.BlockSpec((m.shape[0], block), lambda i: (0, i + first)) for m in merged]
        + [
            once(own_w.shape),
            once(peer_w.shape),
            once((1, d)),
            once((1, d)),
            once((1, d)),
            once(up_w.shape),
            once((1, ff)),
            once(down_w.shape),
        ]
        + [ANYWHERE] * len(extra),
        out_specs=[
            part(d),
            part(d),
            part(ff),
            part(ff),
        ]
        + [
            pl.BlockSpec((block, d), lambda i, b=b, m=m: (jnp.clip(i - b, 0, m - 1), 0))
            for b, m in zip(begins, steps)
        ]
        + [full((1, ff))],
        out_shape=[
            shape((n, d), F32),
            shape((n, d), BF16),
            shape((n, ff), BF16),
            shape((n, ff), BF16),
        ]
        + [shape((size, d), BF16) for size in sizes]
        + [shape((1, ff), F32)],
        input_output_aliases={15 + k: k for k in range(len(extra))},
        scratch_shapes=[pltpu.VMEM((2 * half, d), BF16), pltpu.VMEM((2 * half, block), BF16)],
        compiler_params=params(30),
        cost_estimate=pl.CostEstimate(
            flops=2 * count * d * (ff * 3 + d),
            bytes_accessed=12 * 2**20,
            transcendentals=2 * count * ff,
        ),
        name="feed_forward",
    )(
        place, rows, cot, *merged, own_w, peer_w, out_b, gain, shift, up_w, up_b, down_w, *extra
    )


def weights_kernel(place, act, grad_pre, normed, cot, down_w, mlp, keep, send, acc):
    i = pl.program_id(0)
    part = dot(act[...], down_w[...])

    @pl.when(i == 0)
    def _():
        acc[...] = part

    @pl.when(i > 0)
    def _():
        acc[...] += part

    down = dot_lt(act[...], cot[...])
    up = dot_lt(grad_pre[...], normed[...])
    first = place[3] == 0
    keep[...] = jnp.where(first, down, up).astype(BF16)
    send[...] = jnp.where(first, up, down).astype(BF16)

    @pl.when(i == pl.num_programs(0) - 1)
    def _():
        mlp[...] = acc[...].astype(BF16)


def weights(place, act, grad_pre, normed, cot, down_w):
    n, ff = act.shape
    d = cot.shape[1]
    block = 256
    lanes = pl.BlockSpec((n, block), lambda i: (0, i))
    rows = pl.BlockSpec((block, d), lambda i: (i, 0))
    return pl.pallas_call(
        weights_kernel,
        grid=(ff // block,),
        in_specs=[
            pl.BlockSpec(memory_space=pltpu.SMEM),
            lanes,
            lanes,
            once((n, d)),
            once((n, d)),
            rows,
        ],
        out_specs=[full((n, d)), rows, rows],
        out_shape=[shape((n, d), BF16), shape((ff, d), BF16), shape((ff, d), BF16)],
        scratch_shapes=[pltpu.VMEM((n, d), F32)],
        compiler_params=params(26),
        cost_estimate=pl.CostEstimate(
            flops=6 * n * d * ff, bytes_accessed=20 * 2**20, transcendentals=0
        ),
        name="weights",
    )(place, act, grad_pre, normed, cot, down_w)


def turn_kernel(cot, own_g, peer_g, hidden, gain, out_w, grad_hidden, low_out, gm, sums):
    i = pl.program_id(0)
    unit, inverse = unit_rows(hidden[...])
    gradient = own_g[...].astype(F32) + peer_g[...].astype(F32)
    outer = cot[...].astype(F32)
    total = outer + norm_back(gradient, unit, inverse, gain[...])
    grad_hidden[...] = total
    low = total.astype(BF16)
    low_out[...] = low
    gm[...] = dot_rt(low, out_w[...]).astype(BF16).astype(F32)

    @pl.when(i == 0)
    def _():
        sums[...] = jnp.zeros_like(sums)

    sums[0:1, :] += jnp.sum(gradient * unit, 0, keepdims=True)
    sums[1:2, :] += jnp.sum(gradient, 0, keepdims=True)
    sums[2:3, :] += jnp.sum(total, 0, keepdims=True)
    sums[3:4, :] += jnp.sum(outer, 0, keepdims=True)


def turn(cot, own_g, peer_g, hidden, gain, out_w, start, count, into=None):
    n, d = cot.shape
    block = 256
    first = start // block
    wide = out_w.shape[0]
    extra = () if into is None else tuple(into)

    def part(lanes):
        return pl.BlockSpec((block, lanes), lambda i: (i + first, 0))

    own_part = pl.BlockSpec((block, d), lambda i: (i, 0))

    def kernel(*refs):
        turn_kernel(*refs[:6], *refs[6 + len(extra) :])

    return pl.pallas_call(
        kernel,
        grid=(count // block,),
        in_specs=[part(d), own_part, own_part, part(d), once((1, d)), once((wide, d))]
        + [ANYWHERE] * len(extra),
        out_specs=[part(d), part(d), part(wide), full((8, d))],
        out_shape=[
            stored((n, d), F32),
            stored((n, d), BF16),
            stored((n, wide), F32),
            shape((8, d), F32),
        ],
        input_output_aliases={6 + k: k for k in range(len(extra))},
        compiler_params=params(16),
        cost_estimate=LIGHT,
        name="turn",
    )(cot, own_g, peer_g, hidden, gain, out_w, *extra)


def pair_back(keys, q, do):
    weights = jnp.exp2(dot_rt(keys, q) * EXP_SCALE)
    inner = (weights * dot_rt(keys, do)).astype(BF16)
    grad_keys = dot(weights.astype(BF16), do) + dot(inner, q)
    return grad_keys, dot(keys.T, inner)


def peers_back_kernel(
    place, gm, merged, q, kv_all, do, dq, to_core, kept, acc, *, start
):
    half = q.shape[1]
    n = 2 * half
    block = n // FOLD
    lane = lax.broadcasted_iota(jnp.int32, (block, LANES), 1)
    for j in range(q.shape[0]):
        head = place[0] + pl.program_id(0) + start
        for p in range(FOLD):
            c = (head + ORDER[p]) % FOLD
            at = pl.ds(p * block, block)
            gradient = gm[pl.ds(c, block, stride=FOLD), :]
            delta = jnp.sum(gradient * merged[j, at, :], -1, keepdims=True)
            do[j, at, :] = with_terms(gradient, lane, -delta).astype(BF16)
        for level in (1, 2, 3, 4):
            count = n >> level
            begin = (level - 1) * half
            for k in range(0, half, 256):
                grad, grad_q = pair_back(
                    kv_all[j, pl.ds(begin + k, 256), :], q[j, pl.ds(0, count), :], do[j, pl.ds(0, count), :]
                )
                if level == 1:
                    to_core[j, pl.ds(k, 256), :] = grad.astype(BF16)
                elif level == 2:
                    if k == 0:
                        kept[j, pl.ds(0, 256), :] = grad
                    else:
                        to_core[j, pl.ds(half, 256), :] = grad.astype(BF16)
                else:
                    unit = 256 >> 1
                    off = 0 if level == 3 else unit
                    one, two = grad[:unit], grad[unit:]
                    if k == 0:
                        kept[j, pl.ds(256 + off, unit), :] = one
                        kept[j, pl.ds(512 + off, unit), :] = two
                    else:
                        to_core[j, pl.ds(half + 256 + off, unit), :] = one.astype(BF16)
                        to_core[j, pl.ds(half + 512 + off, unit), :] = two.astype(BF16)
                if count >= LANES:
                    if level == 1 and k == 0:
                        acc[...] = grad_q
                    else:
                        acc[:, :count] += grad_q
                else:
                    acc[:, :LANES] += jnp.concatenate(
                        [grad_q, jnp.zeros((LANES, LANES - count), F32)], axis=1
                    )
        dq[j] = acc[...].T.astype(BF16)


def peers_back(place, gm, merged, q, kv_all, start, count, into=None):
    heads, n, _ = q.shape
    assert n == SEG
    extra = () if into is None else tuple(into)

    def kernel(*refs):
        peers_back_kernel(*refs[:5], *refs[5 + len(extra) :], start=start)

    return pl.pallas_call(
        kernel,
        grid=(count,),
        in_specs=[
            pl.BlockSpec(memory_space=pltpu.SMEM),
            pl.BlockSpec((n, LANES), lambda i: (0, i + start)),
            group_spec(n, start, heads=1),
            group_spec(n // 2, start, heads=1),
            group_spec(2 * n, start, heads=1),
        ]
        + [ANYWHERE] * len(extra),
        out_specs=[group_spec(n, start, heads=1), group_spec(n // 2, start, heads=1), group_spec(n + n // 4, start, heads=1), group_spec(3 * n // 4, start, heads=1)],
        out_shape=[
            stored((heads, n, LANES), BF16),
            stored((heads, n // 2, LANES), BF16),
            shape((heads, n + n // 4, LANES), BF16),
            shape((heads, 3 * n // 4, LANES), F32),
        ],
        input_output_aliases={5 + k: k for k in range(len(extra))},
        scratch_shapes=[pltpu.VMEM((LANES, n // 2), F32)],
        compiler_params=params(16),
        cost_estimate=pl.CostEstimate(
            flops=count * n * n * 1280, bytes_accessed=24 * 2**20, transcendentals=count * n * n // 2
        ),
        name="peers_back",
    )(place, far(gm), far(merged), far(q), far(kv_all), *extra)


def own_back_kernel(q, do, kv, dq, dkv, *accs, block):
    n = q.shape[1]
    for j, acc in enumerate(accs):
        for i in range(n // block):
            at = pl.ds(i * block, block)
            grad, grad_q = pair_back(kv[j, at, :], q[j], do[j])
            dkv[j, at, :] = grad.astype(BF16)
            if i == 0:
                acc[...] = grad_q
            else:
                acc[...] += grad_q
        dq[j] = acc[...].T.astype(BF16)


def own_back(q, do, kv, start, count, into=None):
    heads, n, _ = q.shape
    spec = group_spec(n, start)
    kernel = functools.partial(own_back_kernel, block=256)
    extra = () if into is None else tuple(into)
    return pl.pallas_call(
        kernel if into is None else lambda q, do, kv, _, __, *out: kernel(q, do, kv, *out),
        grid=(count // 2,),
        in_specs=[spec] * 3 + [ANYWHERE] * len(extra),
        out_specs=[spec] * 2,
        out_shape=[stored((heads, n, LANES), BF16)] * 2,
        input_output_aliases={3: 0, 4: 1} if extra else {},
        scratch_shapes=[pltpu.VMEM((LANES, n), F32)] * 2,
        compiler_params=params(24),
        cost_estimate=pl.CostEstimate(
            flops=count * n * n * 2560, bytes_accessed=8 * 2**20, transcendentals=count * n * n
        ),
        name="own_back",
    )(far(q), far(do), far(kv), *extra)


def finish_q_kernel(
    place, dq_own, dq_peer, normed, wide, merged_c, merged_d, grad_low, out, grad_w, grad_b, nat0, nat1, nat2, nat3, acc, both, out_grad
):
    i = pl.program_id(0)
    n = nat0.shape[0]
    lane = lax.broadcasted_iota(jnp.int32, (n, LANES), 1)
    low = []
    for j, nat in enumerate((nat0, nat1, nat2, nat3)):
        unpermute(place[0] + 4 * i + j, j, (dq_own, dq_peer), nat)
        rows = jnp.where(lane < HD, nat[...] * (1.0 / ROOT), 0.0)
        grad_b[j, 0:1, :] = jnp.sum(rows, 0, keepdims=True)
        low.append(rows.astype(BF16))
    low = jnp.concatenate(low, axis=1)
    gradient = dot_lt(low, normed[...])
    for j in range(4):
        grad_w[0, j] = gradient[j * LANES : j * LANES + HD].astype(BF16)

    @pl.when(i == 0)
    def _():
        group = merged_c.shape[0]
        both[:group] = merged_c[...]
        both[group:] = merged_d[...]
        out_grad[...] = dot(both[...], grad_low[...]).astype(BF16)

    for j in range(4):
        at = pl.multiple_of((4 * i + j) * HD, HD)
        grad_w[1, j] = out_grad[pl.ds(at, HD), :]

    part = dot_rt(low, jnp.concatenate([wide[j] for j in range(4)], axis=1))

    @pl.when(i == 0)
    def _():
        acc[...] = part

    @pl.when(i > 0)
    def _():
        acc[...] += part

    @pl.when(i == pl.num_programs(0) - 1)
    def _():
        out[...] = acc[...].astype(BF16)


def unpermute(head, j, sources, nat):
    n = nat.shape[0]
    block = n // FOLD
    for p in range(FOLD):
        c = (head + ORDER[p]) % FOLD
        at = pl.ds(p * block, block)
        total = None
        for ref in sources:
            if p * block < ref.shape[1]:
                piece = ref[j, at, :].astype(F32)
                total = piece if total is None else total + piece
        nat[pl.ds(c, block, stride=FOLD), :] = total


def finish_kv_kernel(
    place, dkv_own, r_core, r_x, r_z1, r_z2, r_z3, normed, rows, wide, start, grad_one,
    grad_normed, keep, send, grad_b, sums, acc, nat0, nat1, nat2, nat3,
):
    i = pl.program_id(0)
    n, d = rows.shape
    lane = lax.broadcasted_iota(jnp.int32, (n, LANES), 1)
    low = []
    for j, nat in enumerate((nat0, nat1, nat2, nat3)):
        unpermute(place[0] + 4 * i + j, j, (dkv_own, r_core, r_x, r_z1, r_z2, r_z3), nat)
        both = nat[...]
        both = jnp.where(lane < HD, both * (1.0 / ROOT), jnp.where(lane < 2 * HD, both, 0.0))
        grad_b[j, 0:1, :] = jnp.sum(both, 0, keepdims=True)
        low.append(both.astype(BF16))
    low = jnp.concatenate(low, axis=1)
    gradient = dot_lt(low, normed[...])
    first = place[3] == 0
    for j in range(4):
        for k in range(2):
            one = grad_one[k, j]
            two = gradient[j * LANES + k * HD : j * LANES + (k + 1) * HD].astype(BF16)
            keep[k, j] = jnp.where(first, one, two)
            send[k, j] = jnp.where(first, two, one)
    part = dot_rt(low, jnp.concatenate([wide[j] for j in range(4)], axis=1))

    @pl.when(i == 0)
    def _():
        acc[...] = start[...].astype(F32) + part

    @pl.when(i > 0)
    def _():
        acc[...] += part

    @pl.when(i == pl.num_programs(0) - 1)
    def _():
        total = acc[...]
        grad_normed[...] = total.astype(BF16)
        unit, _ = unit_rows(rows[...].astype(F32))
        sums[0:1, :] = jnp.sum(total * unit, 0, keepdims=True)
        sums[1:2, :] = jnp.sum(total, 0, keepdims=True)
        sums[2:8, :] = jnp.zeros((6, d), F32)


def pairs(rows):
    return pl.BlockSpec((4, rows, LANES), lambda i: (i, 0, 0))


def finish_q(place, dq_own, dq_peer, normed, wide, merged, grad_low):
    heads, n, _ = dq_own.shape
    d = normed.shape[1]
    return pl.pallas_call(
        finish_q_kernel,
        grid=(heads // 4,),
        in_specs=[
            pl.BlockSpec(memory_space=pltpu.SMEM),
            pairs(n),
            pairs(n // 2),
            once((n, d)),
            pl.BlockSpec((4, d, LANES), lambda i: (i, 0, 0)),
            once(merged[0].shape),
            once(merged[1].shape),
            once((n, d)),
        ],
        out_specs=[
            full((n, d)),
            pl.BlockSpec((2, 4, HD, d), lambda i: (0, i, 0, 0)),
            pl.BlockSpec((4, 1, LANES), lambda i: (i, 0, 0)),
        ],
        out_shape=[
            stored((n, d), BF16),
            stored((2, heads, HD, d), BF16),
            shape((heads, 1, LANES), F32),
        ],
        scratch_shapes=[pltpu.VMEM((n, LANES), F32)] * 4
        + [
            pltpu.VMEM((n, d), F32),
            pltpu.VMEM((heads * HD, n), BF16),
            pltpu.VMEM((heads * HD, d), BF16),
        ],
        compiler_params=params(29),
        cost_estimate=pl.CostEstimate(
            flops=4 * n * d * heads * 128, bytes_accessed=14 * 2**20, transcendentals=0
        ),
        name="finish_q",
    )(place, far(dq_own), far(dq_peer), normed, far(wide), *merged, grad_low)


def finish_kv(place, dkv_own, received, normed, rows, wide, start, grad_one):
    heads, n, _ = dkv_own.shape
    d = normed.shape[1]
    return pl.pallas_call(
        finish_kv_kernel,
        grid=(heads // 4,),
        in_specs=[
            pl.BlockSpec(memory_space=pltpu.SMEM),
            pairs(n),
            pairs(n // 2),
            pairs(n // 4),
            pairs(n // 8),
            pairs(n // 16),
            pairs(n // 16),
            once((n, d)),
            once((n, d)),
            pl.BlockSpec((4, d, LANES), lambda i: (i, 0, 0)),
            once((n, d)),
            pl.BlockSpec((2, 4, HD, d), lambda i: (0, i, 0, 0)),
        ],
        out_specs=[
            full((n, d)),
            pl.BlockSpec((2, 4, HD, d), lambda i: (0, i, 0, 0)),
            pl.BlockSpec((2, 4, HD, d), lambda i: (0, i, 0, 0)),
            pl.BlockSpec((4, 1, LANES), lambda i: (i, 0, 0)),
            full((8, d)),
        ],
        out_shape=[
            shape((n, d), BF16),
            stored((2, heads, HD, d), BF16),
            shape((2, heads, HD, d), BF16),
            shape((heads, 1, LANES), F32),
            shape((8, d), F32),
        ],
        scratch_shapes=[pltpu.VMEM((n, d), F32)] + [pltpu.VMEM((n, LANES), F32)] * 4,
        compiler_params=params(36),
        cost_estimate=pl.CostEstimate(
            flops=4 * n * d * heads * 128, bytes_accessed=20 * 2**20, transcendentals=0
        ),
        name="finish_kv",
    )(place, far(dkv_own), *received, normed, rows, far(wide), far(start), far(grad_one))


def spread_kernel(place, own, peer, down, up):
    first = place[3] == 0
    down[...] = jnp.where(first, own[...], peer[...]).astype(F32)
    up[...] = jnp.where(first, peer[...], own[...]).astype(F32).T


def spread(place, own, peer):
    ff, d = own.shape
    block = 256
    rows = pl.BlockSpec((block, d), lambda i: (i, 0))
    return pl.pallas_call(
        spread_kernel,
        grid=(ff // block,),
        in_specs=[pl.BlockSpec(memory_space=pltpu.SMEM), rows, rows],
        out_specs=[rows, pl.BlockSpec((d, block), lambda i: (0, i))],
        out_shape=[shape((ff, d), F32), shape((d, ff), F32)],
        compiler_params=params(12),
        name="spread",
    )(place, own, peer)


def spread_qkv_kernel(place, own, peer, qkv, out):
    i = pl.program_id(0)
    first = place[3] == 0
    width = qkv.shape[2]

    def piece(on_first, at):
        mine = first == on_first
        return jnp.where(mine, own[at], peer[at]).astype(F32)

    lower, upper = slice(0, width), slice(width, 2 * width)

    @pl.when(i == 0)
    def _():
        qkv[0] = piece(True, lower).T

    @pl.when(i == 1)
    def _():
        qkv[0] = piece(False, lower).T

    @pl.when(i == 2)
    def _():
        qkv[0] = piece(False, upper).T
        out[...] = piece(True, upper)


def spread_qkv(place, own, peer):
    half, d = own.shape
    width = half // 2
    return pl.pallas_call(
        spread_qkv_kernel,
        in_specs=[pl.BlockSpec(memory_space=pltpu.SMEM), once(own.shape), once(own.shape)],
        out_specs=[pl.BlockSpec((1, d, width), lambda i: (i, 0, 0)), full((width, d))],
        grid=(3,),
        out_shape=[shape((3, d, width), F32), shape((width, d), F32)],
        compiler_params=params(16),
        name="spread_qkv",
    )(place, own, peer)


def last_kernel(rows, own_g, peer_g, grad_hidden, gain, out):
    unit, inverse = unit_rows(rows[...].astype(F32))
    gradient = own_g[...].astype(F32) + peer_g[...].astype(F32)
    out[...] = grad_hidden[...] + norm_back(gradient, unit, inverse, gain[...])


def last(rows, own_g, peer_g, grad_hidden, gain):
    n, d = rows.shape
    part = pl.BlockSpec((256, d), lambda i: (i, 0))
    return pl.pallas_call(
        last_kernel,
        grid=(n // 256,),
        in_specs=[part] * 4 + [once((1, d))],
        out_specs=part,
        out_shape=shape((n, d), F32),
        compiler_params=params(12),
        cost_estimate=LIGHT,
        name="last",
    )(rows, own_g, peer_g, grad_hidden, gain)


def gather_small_kernel(sums1, sums_a, sums_b, sums_c, up_a, up_c, grad_bq, grad_bkv, out):
    heads = grad_bq.shape[0]
    d = out.shape[1]
    out[...] = jnp.zeros_like(out)
    out[0:2, :] = sums1[0:2, :]
    out[2:6, :] = sums_a[0:4, :] + sums_b[0:4, :] + sums_c[0:4, :]
    up = up_a[...] + up_c[...]
    for k in range(up.shape[1] // d):
        out[6 + k : 7 + k, :] = up[:, k * d : (k + 1) * d]
    row = [grad_bq[h, :, :HD] for h in range(heads)]
    row += [grad_bkv[h, :, HD : 2 * HD] for h in range(heads)]
    out[15:16, :] = jnp.concatenate(row, axis=1)


def gather_small(sums1, sums2, up_b, grad_bq, grad_bkv):
    d = sums1.shape[1]
    inputs = (sums1, *sums2, *up_b, grad_bq, grad_bkv)
    return pl.pallas_call(
        gather_small_kernel,
        grid=(1,),
        in_specs=[once(x.shape) for x in inputs],
        out_specs=full((FOLD, d)),
        out_shape=shape((FOLD, d), F32),
        compiler_params=params(4),
        cost_estimate=LIGHT,
        name="gather_small",
    )(*inputs)


def add_head(small, peer):
    return jnp.where(jnp.arange(small.shape[0])[:, None] < 2, small + peer, small)


def spread_small_kernel(small, gains, shifts, qv, out_b, up_b, down_b):
    d = small.shape[1]
    width = qv.shape[1]
    gains[0:1, :] = small[0:1, :]
    shifts[0:1, :] = small[1:2, :]
    gains[1:2, :] = small[2:3, :]
    shifts[1:2, :] = small[3:4, :]
    out_b[...] = small[4, :]
    down_b[...] = small[5, :]
    for k in range(up_b.shape[0] // d):
        up_b[k * d : (k + 1) * d] = small[6 + k, :]
    qv[0:1, :] = small[15:16, :width]
    qv[1:2, :] = small[15:16, width:]


def spread_small(small, ff):
    d = small.shape[1]
    dims = [(2, d), (2, d), (2, d // 2), (d,), (ff,), (d,)]
    return pl.pallas_call(
        spread_small_kernel,
        grid=(1,),
        in_specs=[once(small.shape)],
        out_specs=[full(x) for x in dims],
        out_shape=[shape(x, F32) for x in dims],
        compiler_params=params(4),
        cost_estimate=LIGHT,
        name="spread_small",
    )(small)


def swap(x, axis, apart):
    count = lax.axis_size(axis)
    return lax.ppermute(x, axis, [(i, i ^ apart) for i in range(count)])


def whole_call(kernel, place, inputs, outputs, name):
    return pl.pallas_call(
        kernel,
        grid=(1,),
        in_specs=[pl.BlockSpec(memory_space=pltpu.SMEM)] + [once(x.shape) for x in inputs],
        out_specs=[full(dims) for dims, _ in outputs],
        out_shape=[shape(dims, kind) for dims, kind in outputs],
        compiler_params=params(24),
        cost_estimate=LIGHT,
        name=name,
    )(place, *inputs)


def added(refs, at=slice(None)):
    total = refs[0][at, :].astype(F32)
    for ref in refs[1:]:
        total = total + ref[at, :].astype(F32)
    return total


def cut(index, count):
    return pl.ds(pl.multiple_of(index * count, count), count)


class Sum:
    def __init__(self, place, rows, width):
        self.place, self.rows, self.width = place, rows, width
        self.third, self.twelfth = rows // 3, rows // 12

    def call(self, kernel, inputs, outputs, name):
        dims = [((count, self.width), kind) for count, kind in outputs]
        return whole_call(kernel, self.place, inputs, dims, name)

    def start(self, keep, got):
        third, twelfth = self.third, self.twelfth

        def kernel(place, keep, got, m1, s1, m2, *s2):
            side, line = place[4], place[5]
            m1[...] = added((keep, got), cut(side, third))
            s1[...] = added((keep, got), cut(1 - side, third)).astype(BF16)

            def quarter(k):
                at = pl.multiple_of(2 * third + (line ^ k) * twelfth, twelfth)
                return added((keep, got), pl.ds(at, twelfth))

            m2[...] = quarter(0)
            for k in (1, 2, 3):
                s2[k - 1][...] = quarter(k).astype(BF16)

        return self.call(
            kernel,
            (keep, got),
            [(third, F32), (third, BF16), (twelfth, F32)] + [(twelfth, BF16)] * 3,
            "start_sum",
        )

    def send1(self, state):
        m1, s1, m2, *s2 = state
        got = swap(s1, "seq", 2)
        return (m1, m2, got) + tuple(swap(x, "seq", 4 * k) for k, x in zip((1, 2, 3), s2))

    def middle(self, state):
        twelfth = self.twelfth

        def kernel(place, m1, m2, g1, ga, gb, gc, n1, n2, s2, *s1):
            side, line = place[4], place[5]
            n1[...] = added((m1, g1), cut(line, twelfth))
            for k in (1, 2, 3):
                s1[k - 1][...] = added((m1, g1), cut(line ^ k, twelfth)).astype(BF16)
            n2[...] = added((m2, ga, gb, gc), cut(side, twelfth // 2))
            s2[...] = added((m2, ga, gb, gc), cut(1 - side, twelfth // 2)).astype(BF16)

        return self.call(
            kernel,
            state,
            [(twelfth, F32), (twelfth // 2, F32), (twelfth // 2, BF16)] + [(twelfth, BF16)] * 3,
            "middle_sum",
        )

    def send2(self, state):
        n1, n2, s2, *s1 = state
        got = tuple(swap(x, "seq", 4 * k) for k, x in zip((1, 2, 3), s1))
        return (n1, n2) + got + (swap(s2, "seq", 2),)

    def end(self, state):
        twelfth = self.twelfth

        def kernel(place, n1, n2, ga, gb, gc, g2, one, two):
            one[...] = added((n1, ga, gb, gc)).astype(BF16)
            two[...] = added((n2, g2)).astype(BF16)

        pair = self.call(kernel, state, [(twelfth, BF16), (twelfth // 2, BF16)], "end_sum")
        return tuple(self.beyond(x) for x in pair)

    def beyond(self, low):
        apart = FOLD
        while apart < lax.axis_size("seq"):
            low = (low.astype(F32) + swap(low, "seq", apart).astype(F32)).astype(BF16)
            apart *= 2
        return low

    def send3(self, pair):
        one, two = pair
        got = tuple(swap(one, "seq", 4 * k) for k in (1, 2, 3))
        return (one, two) + got + (swap(two, "seq", 2),)

    def join(self, state):
        twelfth, third = self.twelfth, self.third

        def kernel(place, one, two, ga, gb, gc, g2, out1, out2):
            side, line = place[4], place[5]
            for k, ref in enumerate((one, ga, gb, gc)):
                out1[cut(line ^ k, twelfth), :] = ref[...]
            out2[cut(side, twelfth // 2), :] = two[...]
            out2[cut(1 - side, twelfth // 2), :] = g2[...]

        return self.call(kernel, state, [(third, BF16), (twelfth, BF16)], "join_sum")

    def send4(self, pair):
        one, two = pair
        got = swap(one, "seq", 2)
        return (one, two, got) + tuple(swap(two, "seq", 4 * k) for k in (1, 2, 3))

    def whole(self, state):
        twelfth, third = self.twelfth, self.third

        def kernel(place, one, two, g1, ga, gb, gc, out):
            side, line = place[4], place[5]
            out[cut(side, third), :] = one[...]
            out[cut(1 - side, third), :] = g1[...]
            for k, ref in enumerate((two, ga, gb, gc)):
                at = pl.multiple_of(2 * third + (line ^ k) * twelfth, twelfth)
                out[pl.ds(at, twelfth), :] = ref[...]

        return self.call(kernel, state, [(self.rows, BF16)], "whole_sum")[0]


class LineSum(Sum):
    def __init__(self, place, rows, width):
        self.place, self.rows, self.width = place, rows, width
        self.half, self.eighth = rows // 2, rows // 8

    def start(self, keep, got):
        half = self.half

        def kernel(place, keep, got, mine, *sends):
            mine[...] = added((keep, got), cut(place[4], half))
            for k, send in enumerate(sends):
                at = cut(2 * (1 - place[4]) + k, half // 2)
                send[...] = added((keep, got), at).astype(BF16)

        outputs = [(half, F32)] + [(half // 2, BF16)] * 2
        return self.call(kernel, (keep, got), outputs, "start_line")

    def near(self, mine, one, two):
        eighth = self.eighth

        def kernel(place, mine, one, two, keep, send):
            parity = place[5] % 2
            for high, got in enumerate((one, two)):
                out = pl.ds(high * eighth, eighth)

                def piece(low):
                    at = pl.multiple_of((2 * high + low) * eighth, eighth)
                    return mine[pl.ds(at, eighth), :] + got[cut(low, eighth), :].astype(F32)

                keep[out, :] = piece(parity)
                send[out, :] = piece(1 - parity).astype(BF16)

        outputs = [(2 * eighth, F32), (2 * eighth, BF16)]
        return self.call(kernel, (mine, one, two), outputs, "near_line")

    def across(self, keep, got):
        eighth = self.eighth

        def kernel(place, keep, got, mine, send):
            high = place[5] // 2
            mine[...] = added((keep, got), cut(high, eighth))
            send[...] = added((keep, got), cut(1 - high, eighth)).astype(BF16)

        outputs = [(eighth, F32), (eighth, BF16)]
        return self.call(kernel, (keep, got), outputs, "across_line")

    def end(self, mine, got):
        def kernel(place, mine, got, out):
            out[...] = added((mine, got)).astype(BF16)

        outputs = [(self.eighth, BF16)]
        return self.beyond(self.call(kernel, (mine, got), outputs, "end_line")[0])

    def join_across(self, mine, got):
        def kernel(place, mine, got, low, high):
            lower = place[5] // 2 == 0
            low[...] = jnp.where(lower, mine[...], got[...])
            high[...] = jnp.where(lower, got[...], mine[...])

        outputs = [(self.eighth, BF16)] * 2
        return self.call(kernel, (mine, got), outputs, "join_across")

    def join_low(self, mine, got):
        eighth = self.eighth

        def kernel(place, mine, got, out):
            parity = place[5] % 2
            out[cut(parity, eighth), :] = mine[...]
            out[cut(1 - parity, eighth), :] = got[...]

        return self.call(kernel, (mine, got), [(2 * eighth, BF16)], "join_low")[0]

    def join_high(self, mine, got):
        def kernel(place, mine, got, one, two):
            even = place[5] % 2 == 0
            one[...] = jnp.where(even, mine[...], got[...])
            two[...] = jnp.where(even, got[...], mine[...])

        outputs = [(self.eighth, BF16)] * 2
        return self.call(kernel, (mine, got), outputs, "join_high")

    def whole(self, mine, got):
        half, eighth = self.half, self.eighth

        def kernel(place, *refs):
            *parts, out = refs
            for side, group in ((place[4], parts[:3]), (1 - place[4], parts[3:])):
                at = 0
                for ref in group:
                    count = ref.shape[0]
                    out[pl.ds(pl.multiple_of(side * half + at, eighth), count), :] = ref[...]
                    at += count

        return self.call(kernel, (*mine, *got), [(self.rows, BF16)], "whole_line")[0]


def send_home(place, kept, r_core):
    heads, rows, lanes = kept.shape
    quarter = rows // 3
    half = r_core.shape[1] - rows

    def kernel(place, kept, r_core, far, near, stay):
        def both(k):
            return kept[:, cut(k, quarter), :] + r_core[
                :, pl.ds(half + k * quarter, quarter), :
            ].astype(F32)

        near[...] = both(0).astype(BF16)
        stay[...] = both(1)
        far[...] = both(2).astype(BF16)

    dims = (heads, quarter, lanes)
    return whole_call(
        kernel, place, (kept, r_core), [(dims, BF16), (dims, BF16), (dims, F32)], "send_home"
    )


def send_line(place, stay, got):
    heads, rows, lanes = stay.shape

    def kernel(place, stay, got, z1, z2, z3):
        def both(start, count):
            at = pl.ds(start, count)
            return (stay[:, at, :] + got[:, at, :].astype(F32)).astype(BF16)

        z1[...] = both(0, rows // 2)
        z2[...] = both(rows // 2, rows // 4)
        z3[...] = both(3 * rows // 4, rows // 4)

    return whole_call(
        kernel,
        place,
        (stay, got),
        [((heads, count, lanes), BF16) for count in (rows // 2, rows // 4, rows // 4)],
        "send_line",
    )


def tie(*xs):
    return lax.optimization_barrier(xs)


def sum_small(x, apart):
    while apart < lax.axis_size("seq"):
        x = x + swap(x, "seq", apart)
        apart *= 2
    return x


def local(
    rows,
    lengths,
    norm_gains,
    norm_shifts,
    qkv_weight,
    qv_bias,
    out_weight,
    out_bias,
    up_weight,
    up_bias,
    down_weight,
    down_bias,
    out_cot,
):
    n, d = rows.shape
    width = qkv_weight.shape[2]
    heads = width // HD
    seq_place = lax.axis_index("seq")
    head_place = lax.axis_index("head")
    slide_rows = min(FOLD * SEG, n * lax.axis_size("seq"))
    start = seq_place * n
    slide = start // slide_rows
    length = jnp.sum(jnp.where(jnp.arange(lengths.shape[0]) == slide, lengths, 0))
    limit = jnp.clip(length - start % slide_rows, 0, n)
    place = jnp.stack(
        [
            head_place * heads,
            limit,
            head_place,
            seq_place % 2,
            seq_place // 2 % 2,
            seq_place // 4 % 4,
        ]
    ).astype(jnp.int32)
    half, quarter, eighth = n // 2, n // 4, n // 8
    first_heads = heads // 2

    peer_out_weight = swap(out_weight, "head", 1)
    wide_out = jnp.pad(
        out_weight.reshape(heads, HD, d), ((0, 0), (HD, LANES - 2 * HD), (0, 0))
    ).reshape(heads * LANES, d)

    kv, s1, sx, sz1, sz, normed1, wide_kv = project_kv(
        place, rows, norm_gains[:1], norm_shifts[:1], qkv_weight, qv_bias
    )
    rz1 = swap(sz1, "seq", 4)
    rx = swap(sx, "seq", 2)
    rz2 = swap(sz, "seq", 8)
    rz3 = swap(sz, "seq", 12)
    cs1 = swap(s1, "seq", 1)
    q, wide_q = project_q(place, normed1, qkv_weight, qv_bias)
    q, rz1, rz2, rz3 = tie(q, rz1, rz2, rz3)
    zc = jnp.concatenate([rz1, rz2, rz3], 1)
    rx2 = swap(zc, "seq", 2)
    crx = swap(rx, "seq", 1)
    czc = swap(zc, "seq", 1)
    own = own_attention(q, kv, 0, first_heads)
    own = own_attention(q, kv, first_heads, heads - first_heads, own)
    own, rx2, crx, czc, cs1, peer_out_weight = tie(own, rx2, crx, czc, cs1, peer_out_weight)
    crx2 = swap(rx2, "seq", 1)
    received = (cs1, rx, crx, zc, rx2, czc, crx2)
    *state, low_one = peers_attention(place, q, own, received, 0, first_heads)
    peer_low_one = swap(low_one, "head", 1)
    *state, low_two = peers_attention(
        place, q, own, received, first_heads, heads - first_heads, state
    )
    merged, kv_all, qb = state
    merged, low_two, peer_low_one = tie(merged, low_two, peer_low_one)
    merged_low = (low_one, low_two)
    peer_low = (peer_low_one, swap(low_two, "head", 1))

    def feed_rows(start, sizes, into):
        return feed(
            place,
            rows,
            out_cot,
            merged_low + peer_low,
            out_weight,
            peer_out_weight,
            out_bias[None],
            norm_gains[1:],
            norm_shifts[1:],
            up_weight,
            up_bias[None],
            down_weight,
            start,
            sizes,
            into,
        )

    *fed, g2_a, ub_one = feed_rows(0, (quarter,), None)
    peer_a = swap(g2_a, "head", 1)
    *fed, g2_b, g2_c, ub_two = feed_rows(quarter, (quarter, half), fed)
    *fed, peer_a = tie(*fed, peer_a)
    hidden, normed2, act, grad_pre = fed
    peer_b = swap(g2_b, "head", 1)
    mlp, keep, send = weights(place, act, grad_pre, normed2, out_cot, down_weight)
    peer_b, mlp, keep, send = tie(peer_b, mlp, keep, send)

    def turn_rows(own_g, peer_g, start, into):
        count = own_g.shape[0]
        return turn(out_cot, own_g, peer_g, hidden, norm_gains[1:], wide_out, start, count, into)

    ff = up_bias.shape[0]
    sums = LineSum(place, ff, d)
    peer_c = swap(g2_c, "head", 1)
    ff_mine, *ff_send = sums.start(keep, swap(send, "seq", 1))
    ff_got = [swap(ff_send[0], "seq", 2)]
    *turned, sums2_a = turn_rows(g2_a, peer_a, 0, None)
    *turned, sums2_b = turn_rows(g2_b, peer_b, quarter, turned)
    peer_c, ff_mine, ff_send[1], *turned, ff_got[0] = tie(
        peer_c, ff_mine, ff_send[1], *turned, ff_got[0]
    )
    ff_got += [swap(ff_send[1], "seq", 2)]
    grad_hidden, grad_low, gm, sums2_c = turn_rows(g2_c, peer_c, half, turned)
    back = peers_back(place, gm, merged, qb, kv_all, 0, first_heads)
    *back, ff_mine, ff_got[0], ff_got[1] = tie(*back, ff_mine, *ff_got)
    ff_mine, ff_send = sums.near(ff_mine, *ff_got)
    ff_got = swap(ff_send, "seq", 4)
    peer_mlp = swap(mlp, "head", 1)
    back = peers_back(
        place, gm, merged, qb, kv_all, first_heads, heads - first_heads, back
    )
    do, dq_peer, to_core, kept, ff_mine, ff_got = tie(*back, ff_mine, ff_got)
    r_core = swap(to_core, "seq", 1)
    ff_mine, ff_send = sums.across(ff_mine, ff_got)
    ff_got = swap(ff_send, "seq", 8)
    back = own_back(qb, do, kv, 0, first_heads)
    dq_own, dkv_own, r_core, ff_mine, ff_got = tie(*back, r_core, ff_mine, ff_got)
    far_rows, near_rows, stay = send_home(place, kept, r_core)
    r_x2 = swap(far_rows, "seq", 2)
    r_x = swap(near_rows, "seq", 2)
    ff_mine = sums.end(ff_mine, ff_got)
    ff_got = swap(ff_mine, "seq", 8)
    back = own_back(qb, do, kv, first_heads, heads - first_heads, (dq_own, dkv_own))
    dq_own, dkv_own, r_x2, ff_mine, ff_got = tie(*back, r_x2, ff_mine, ff_got)
    z1, z2, z3 = send_line(place, stay, r_x2)
    r_z1 = swap(z1, "seq", 4)
    r_z2 = swap(z2, "seq", 8)
    r_z3 = swap(z3, "seq", 12)
    ff_low, ff_high = sums.join_across(ff_mine, ff_got)
    ff_got = swap(ff_low, "seq", 4)
    start_g, grad_one, grad_bq = finish_q(
        place, dq_own, dq_peer, normed1, wide_q, merged_low, grad_low
    )
    start_g, grad_one, peer_mlp, r_x, r_z1, r_z2, r_z3, ff_low, ff_high, ff_got = tie(
        start_g, grad_one, peer_mlp, r_x, r_z1, r_z2, r_z3, ff_low, ff_high, ff_got
    )
    ff_mine = [sums.join_low(ff_low, ff_got)]
    ff_got = [swap(ff_mine[0], "seq", 2)]
    high_got = swap(ff_high, "seq", 4)
    grad_normed1, keep, send, grad_bkv, sums1 = finish_kv(
        place, dkv_own, (r_core, r_x, r_z1, r_z2, r_z3), normed1, rows, wide_kv, start_g, grad_one
    )
    keep, send, sums1, grad_normed1, ff_got[0], ff_high, high_got = tie(
        keep, send, sums1, grad_normed1, ff_got[0], ff_high, high_got
    )

    count = 2 * width
    keep, send = keep.reshape(count, d), send.reshape(count, d)
    got = swap(send, "seq", 1)
    peer_normed1 = swap(grad_normed1, "head", 1)
    small = gather_small(sums1, (sums2_a, sums2_b, sums2_c), (ub_one, ub_two), grad_bq, grad_bkv)
    small = small + swap(small, "seq", 1)
    keep, got, small = tie(keep, got, small)
    w_sums = Sum(place, count, d)
    state = w_sums.send1(w_sums.start(far(keep), got))
    small = small + swap(small, "seq", 4)
    ff_mine += sums.join_high(ff_high, high_got)
    *state, small, peer_mlp = tie(*state, small, peer_mlp)
    state = w_sums.send2(w_sums.middle(state))
    small = small + swap(small, "seq", 2)
    out_rows = (
        hidden + ((mlp.astype(F32) + peer_mlp.astype(F32)) + down_bias)
    ).astype(BF16)
    *state, small, out_rows, ff_mine[1], ff_mine[2] = tie(
        *state, small, out_rows, ff_mine[1], ff_mine[2]
    )
    ff_got += [swap(ff_mine[1], "seq", 2), swap(ff_mine[2], "seq", 2)]
    state = w_sums.send3(w_sums.end(state))
    small = small + swap(small, "seq", 8)
    rows_grad = last(rows, grad_normed1, peer_normed1, grad_hidden, norm_gains[:1])
    ff_own = sums.whole(ff_mine, ff_got)
    *state, small, rows_grad, ff_own = tie(*state, small, rows_grad, ff_own)
    state = w_sums.send4(w_sums.join(state))
    peer_small = swap(small, "head", 1)
    down_weight_grad, up_weight_grad = spread(place, ff_own, swap(ff_own, "seq", 1))
    *state, small, peer_small, down_weight_grad = tie(
        *state, small, peer_small, down_weight_grad
    )
    w_own = w_sums.whole(state)
    w_peer = swap(w_own, "seq", 1)
    small = sum_small(add_head(small, peer_small), FOLD)
    qkv_grad, out_weight_grad = spread_qkv(place, w_own, w_peer)
    gains_grad, shifts_grad, qv_bias_grad, out_bias_grad, up_bias_grad, down_bias_grad = (
        spread_small(small, ff)
    )
    return (
        out_rows,
        rows_grad,
        gains_grad,
        shifts_grad,
        qkv_grad,
        qv_bias_grad,
        out_weight_grad,
        out_bias_grad,
        up_weight_grad,
        up_bias_grad,
        down_weight_grad,
        down_bias_grad,
    )


def solution(mesh):
    placed = (
        P("seq", None),
        P(),
        P(),
        P(),
        P(None, None, "head"),
        P(None, "head"),
        P("head", None),
        P(),
        P(None, "head"),
        P("head"),
        P("head", None),
        P(),
        P("seq", None),
    )
    return jax.shard_map(
        local,
        mesh=mesh,
        in_specs=placed,
        out_specs=(
            P("seq", None),
            P("seq", None),
            P(),
            P(),
            P(None, None, "head"),
            P(None, "head"),
            P("head", None),
            P(),
            P(None, "head"),
            P("head"),
            P("head", None),
            P(),
        ),
        check_vma=False,
    )
```
